32 devices in a mesh: dp: 4 (over y, x), sp: 8 (over z, core).
Axes of the slice: x: 2, y: 2, z: 4, core: 2. Of those that a mesh axis runs over, the one named last changes fastest.
Arguments:
- query_matrix: bfloat16 [4, 4096, 8192], P('dp', 'sp'), may hold values from -8 to 8
- key_matrix: bfloat16 [4, 4096, 1024], P('dp', 'sp'), may hold values from -8 to 8
- value_matrix: bfloat16 [4, 4096, 1024], P('dp', 'sp'), may hold values from -6 to 6
- block_source: int32 [8, 16], replicated, may hold values from 0 to 15, as said below
- documents: int32 [4, 32], P('dp'), may hold values from 0 to 7, never falling along the last dimension, each value on 1 to 8 neighbouring positions
Outputs:
- attended: bfloat16 [4, 4096, 8192], P('dp', 'sp')
The draws below stay inside these ranges and needn't reach their ends.
Inputs may be any that keep to these rules, and one draw needn't show every extreme that they name: `block_source`: each row is a permutation of 0 to 15, and for every pair of dp indices g and h exactly 1 entries of row s at positions g * 4 to g * 4 + 3 lie in h * 4 to h * 4 + 3. `documents`: each row never falls, and a document spans at most 8 blocks.
All inputs are finite; a program needn't handle non-finite values.
Results may differ from the reference program's by a relative error of at most 0.0036.
Values may be sent and summed in bfloat16 or wider, within the bound.
No kernel may reach another device: no remote copies, remote signals or barrier semaphores. Data moves between devices by JAX's collectives and lax.ppermute only.
A program may use at most 128 MiB of HBM per device.

```python
import math
import jax
import jax.numpy as jnp
import numpy as np
from jax import lax

QUERY_HEADS = 64
KEY_VALUE_HEADS = 8
HEAD_WIDTH = 128
BALANCE_TOKENS = 128
MOST_BLK = 8
CAP = 1
BLK_DEV = 4
GROUP_TOKENS = 4096
GB = 32
N_DP = 4
N_SP = 8


def base_values(key, width):
    return jnp.clip(jax.random.normal(key, (N_DP, GROUP_TOKENS, width), jnp.float32), -6.0, 6.0)


def draw_key_matrix(key, part):
    field_values = base_values(jax.random.fold_in(key, 1), KEY_VALUE_HEADS * HEAD_WIDTH)
    return field_values.astype(jnp.bfloat16)


def draw_query_matrix(key, part):
    field_values = base_values(jax.random.fold_in(key, 2), QUERY_HEADS * HEAD_WIDTH)
    return field_values.astype(jnp.bfloat16)


def draw_block_source(key, part):

    def one_column(column_key):
        slot_key, dest_key, place_key = jax.random.split(column_key, 3)
        slot_order = jax.vmap(lambda sub: jax.random.permutation(sub, BLK_DEV))(jax.random.split(slot_key, N_DP))
        dest_order = jax.vmap(lambda sub: jax.random.permutation(sub, N_DP))(jax.random.split(dest_key, N_DP))
        sources = jnp.arange(N_DP, dtype=jnp.int32)[:, None] * BLK_DEV + slot_order.astype(jnp.int32)
        pieces = sources.reshape(N_DP, N_DP, CAP)
        piece_of = jnp.argsort(dest_order, axis=1, stable=True)
        picker = jnp.broadcast_to(piece_of[:, :, None], (N_DP, N_DP, CAP))
        incoming = jnp.take_along_axis(pieces, picker, axis=1)
        incoming = jnp.transpose(incoming, (1, 0, 2)).reshape(N_DP, BLK_DEV)
        placing = jax.vmap(lambda sub: jax.random.permutation(sub, BLK_DEV))(jax.random.split(place_key, N_DP))
        return jnp.take_along_axis(incoming, placing, axis=1).reshape(-1)
    return jax.vmap(one_column)(jax.random.split(key, N_SP)).astype(jnp.int32)


def level_of(stream_key, dims, shards, smallest, top_value):
    def one(dim, blocks):
        draws = jax.random.uniform(jax.random.fold_in(jax.random.fold_in(stream_key, 6), dim), (blocks,), jnp.float32, smallest / len(shards), top_value / len(shards))
        return jnp.repeat(jnp.exp(draws), dims[dim] // blocks).reshape((-1,) + (1,) * (len(dims) - dim - 1))

    loudness = one(*shards[0])
    for cut in shards[1:]:
        loudness = loudness * one(*cut)
    return loudness


def length_profile(amount, total, bound, slope):
    loads = [(1 << 20) // math.isqrt(standing ** slope) + 1 for standing in range(2, amount + 1)]
    rest, holding = total - bound - (amount - 1), [1] * (amount - 1)
    while rest > 0:
        candidates = [i for i in range(amount - 1) if holding[i] < bound]
        mass, remaining = sum([loads[i] for i in candidates]), rest
        for i in candidates:
            addition = min(bound - holding[i], max(1, remaining * loads[i] // mass), rest)
            holding[i] = holding[i] + addition
            rest = rest - addition
    return np.array([bound] + holding)


def uneven(own_key, number_of, total, limit, slope):
    if number_of == 2:
        one = jax.random.randint(own_key, (), max(1, total - limit), min(limit, total - 1) + 1)
        return jnp.stack([one, total - one])
    lengths = jnp.asarray(length_profile(number_of, total, limit, slope), jnp.int32)
    twos = (number_of - 1) // 2
    giver, sink = lengths[1:1 + 2 * twos:2], lengths[2:2 + 2 * twos:2]
    slack = jnp.minimum(giver - 1, limit - sink)
    shifted = jax.random.randint(jax.random.fold_in(own_key, 1), (twos,), 0, 1 << 20) % (slack + 1)
    lengths = lengths.at[1:1 + 2 * twos:2].set(giver - shifted).at[2:2 + 2 * twos:2].set(sink + shifted)
    return lengths[jax.random.permutation(jax.random.fold_in(own_key, 2), number_of)]


def noise(key, shape, spread, reach, cuts=(), kind=jnp.bfloat16):
    drawn = jax.random.normal(key, shape, jnp.float32) * spread
    if len(cuts) > 0:
        drawn = level_of(key, shape, cuts, -0.22, 0.18) * drawn
    return jnp.clip(drawn, min=-reach, max=reach).astype(kind)


def setup_inputs(seed: int = 0) -> dict:
    streams_of = jax.random.split(jax.random.key(seed), 6)
    return {
        "query_matrix": draw_query_matrix(jax.random.fold_in(streams_of[5], 71), 0),
        "key_matrix": draw_key_matrix(jax.random.fold_in(streams_of[5], 71), 0),
        "value_matrix": noise(streams_of[2], (N_DP, GROUP_TOKENS, KEY_VALUE_HEADS * HEAD_WIDTH), 1.0, 6.0, ((0, 4), (1, 8))),
        "block_source": draw_block_source(jax.random.fold_in(streams_of[5], 71), 0),
        "documents": jax.vmap(lambda own: jnp.searchsorted(jnp.cumsum(uneven(own, GB // 4, GB, MOST_BLK, 2)), jnp.arange(GB), side="right"))(jax.random.split(streams_of[4], N_DP)).reshape((N_DP, GB)).astype(jnp.int32),
    }


def even_out_blocks(field_values, sender_group, sender_position, column_number):
    width = field_values.shape[-1]
    reshaped_rows = field_values.reshape(N_DP, N_SP, BLK_DEV, BALANCE_TOKENS, width)
    return reshaped_rows[sender_group, column_number, sender_position].reshape(N_DP, GROUP_TOKENS, width)


def attend_group(query_group, key_group, value_group, block_docs):
    span = MOST_BLK * BALANCE_TOKENS
    key_padded = jnp.pad(key_group, ((0, span), (0, 0)))
    value_padded = jnp.pad(value_group, ((0, span), (0, 0)))
    token_docs = jnp.pad(jnp.repeat(block_docs, BALANCE_TOKENS), (0, span), constant_values=-1)
    doc_first = jnp.sum(block_docs[None, :] < block_docs[:, None], axis=1, dtype=jnp.int32) * BALANCE_TOKENS
    scale = HEAD_WIDTH ** -0.5

    def one_block(block_number):
        start = block_number * BALANCE_TOKENS
        query_tile = lax.dynamic_slice_in_dim(query_group, start, BALANCE_TOKENS, 0).astype(jnp.float32)
        first = doc_first[block_number]
        key_tile = lax.dynamic_slice_in_dim(key_padded, first, span, 0).astype(jnp.float32)
        value_tile = lax.dynamic_slice_in_dim(value_padded, first, span, 0).astype(jnp.float32)
        key_docs = lax.dynamic_slice_in_dim(token_docs, first, span, 0)
        key_pos = first + jnp.arange(span, dtype=jnp.int32)
        query_pos = start + jnp.arange(BALANCE_TOKENS, dtype=jnp.int32)
        allowed = (key_docs[None, :] == block_docs[block_number]) & (key_pos[None, :] <= query_pos[:, None])
        scores = jnp.einsum("qhd,kd->qhk", query_tile, key_tile) * scale
        scores = jnp.where(allowed[:, None, :], scores, -1e30)
        top = jnp.max(scores, axis=-1, keepdims=True)
        weights = jnp.where(allowed[:, None, :], jnp.exp(scores - top), 0.0)
        total = jnp.sum(weights, axis=-1, keepdims=True)
        rounded = lax.optimization_barrier(weights.astype(jnp.bfloat16)).astype(jnp.float32)
        mixed = jnp.einsum("qhk,kd->qhd", rounded, value_tile) / total
        return mixed.astype(jnp.bfloat16)

    blocks_out = lax.map(one_block, jnp.arange(GB, dtype=jnp.int32))
    return blocks_out.reshape(GROUP_TOKENS, query_group.shape[1], HEAD_WIDTH)


def reference(query_matrix, key_matrix, value_matrix, block_source, documents):
    routing = block_source.reshape(N_SP, N_DP, BLK_DEV)
    sender_group = jnp.transpose(routing // BLK_DEV, (1, 0, 2))
    sender_position = jnp.transpose(routing % BLK_DEV, (1, 0, 2))
    column_number = jnp.broadcast_to(jnp.arange(N_SP, dtype=jnp.int32)[None, :, None], sender_group.shape)
    group_length = QUERY_HEADS // KEY_VALUE_HEADS
    query_list = even_out_blocks(query_matrix, sender_group, sender_position, column_number).reshape(N_DP, GROUP_TOKENS, KEY_VALUE_HEADS, group_length, HEAD_WIDTH)
    every_key = even_out_blocks(key_matrix, sender_group, sender_position, column_number).reshape(N_DP, GROUP_TOKENS, KEY_VALUE_HEADS, HEAD_WIDTH)
    every_value = even_out_blocks(value_matrix, sender_group, sender_position, column_number).reshape(N_DP, GROUP_TOKENS, KEY_VALUE_HEADS, HEAD_WIDTH)
    query_entries = jnp.transpose(query_list, (0, 2, 1, 3, 4)).reshape(N_DP * KEY_VALUE_HEADS, GROUP_TOKENS, group_length, HEAD_WIDTH)
    key_entries = jnp.transpose(every_key, (0, 2, 1, 3)).reshape(N_DP * KEY_VALUE_HEADS, GROUP_TOKENS, HEAD_WIDTH)
    value_entries = jnp.transpose(every_value, (0, 2, 1, 3)).reshape(N_DP * KEY_VALUE_HEADS, GROUP_TOKENS, HEAD_WIDTH)
    document_items = jnp.repeat(documents, KEY_VALUE_HEADS, axis=0)
    output_rows = lax.map(lambda item: attend_group(item[0], item[1], item[2], item[3]),
                      (query_entries, key_entries, value_entries, document_items))
    output_rows = output_rows.reshape(N_DP, KEY_VALUE_HEADS, GROUP_TOKENS, group_length, HEAD_WIDTH)
    return jnp.transpose(output_rows, (0, 2, 1, 3, 4)).reshape(N_DP, GROUP_TOKENS, QUERY_HEADS * HEAD_WIDTH)
```

```python
import functools
import math

import jax
import jax.numpy as jnp
from jax import lax
from jax.experimental import pallas as pl
from jax.experimental.pallas import tpu as pltpu
from jax.sharding import PartitionSpec as P

QUERY_HEADS = 64
KEY_VALUE_HEADS = 8
HEAD_WIDTH = 128
BALANCE_TOKENS = 128
MOST_BLK = 8
GROUP_HEADS = QUERY_HEADS // KEY_VALUE_HEADS
GROUP_WIDTH = GROUP_HEADS * HEAD_WIDTH
PAIR = 256
EXP2_SCALE = math.log2(math.e) / math.sqrt(HEAD_WIDTH)
VMEM_LIMIT = 40 * 1024 * 1024


def position():
    return lax.axis_index("dp"), lax.axis_index("sp")


def leaving_slot(source_ref, blocks, dp, sp, other):
    slot = jnp.int32(0)
    for place in range(blocks):
        entry = source_ref[sp, other * blocks + place]
        slot = jnp.where(entry // blocks == dp, entry % blocks, slot)
    return slot


def landing_slot(source_ref, blocks, dp, sp, other):
    slot = jnp.int32(0)
    for place in range(blocks):
        entry = source_ref[sp, dp * blocks + place]
        slot = jnp.where(entry // blocks == other, place, slot)
    return slot


def block_rows(slot):
    return pl.ds(pl.multiple_of(slot * BALANCE_TOKENS, BALANCE_TOKENS), BALANCE_TOKENS)


def pack_kv_kernel(blocks, source_ref, k_ref, v_ref, *rest):
    outs, sem = rest[:-1], rest[-1]
    dp, sp = position()
    copies = []
    for step, out in enumerate(outs):
        rows = block_rows(leaving_slot(source_ref, blocks, dp, sp, dp ^ step))
        copies.append(pltpu.make_async_copy(k_ref.at[rows], out.at[0], sem.at[2 * step]))
        copies.append(pltpu.make_async_copy(v_ref.at[rows], out.at[1], sem.at[2 * step + 1]))
    for copy in copies:
        copy.start()
    for copy in copies:
        copy.wait()


def pack_kv(source, k, v, blocks):
    width = k.shape[1]
    any_spec = pl.BlockSpec(memory_space=pl.ANY)
    return pl.pallas_call(
        functools.partial(pack_kv_kernel, blocks),
        out_shape=[jax.ShapeDtypeStruct((2, BALANCE_TOKENS, width), k.dtype)] * blocks,
        in_specs=[pl.BlockSpec(memory_space=pltpu.SMEM), any_spec, any_spec],
        out_specs=[any_spec] * blocks,
        scratch_shapes=[pltpu.SemaphoreType.DMA((2 * blocks,))],
        compiler_params=pltpu.CompilerParams(vmem_limit_bytes=VMEM_LIMIT),
        cost_estimate=pl.CostEstimate(flops=0, bytes_accessed=4 * 2**20, transcendentals=0),
        name="pack_kv",
    )(source, k, v)


def pack_q_kernel(blocks, parts, source_ref, q_ref, *rest):
    outs, sem = rest[:-1], rest[-1]
    dp, sp = position()
    width = q_ref.shape[1] // parts
    copies = []
    for step in range(1, blocks):
        rows = block_rows(leaving_slot(source_ref, blocks, dp, sp, dp ^ step))
        for part in range(parts):
            number = (step - 1) * parts + part
            copies.append(
                pltpu.make_async_copy(
                    q_ref.at[rows, pl.ds(part * width, width)], outs[number], sem.at[number]
                )
            )
    for copy in copies:
        copy.start()
    for copy in copies:
        copy.wait()


def pack_q(source, q, blocks, parts):
    width = q.shape[1] // parts
    count = (blocks - 1) * parts
    any_spec = pl.BlockSpec(memory_space=pl.ANY)
    outs = pl.pallas_call(
        functools.partial(pack_q_kernel, blocks, parts),
        out_shape=[jax.ShapeDtypeStruct((BALANCE_TOKENS, width), q.dtype)] * count,
        in_specs=[pl.BlockSpec(memory_space=pltpu.SMEM), any_spec],
        out_specs=[any_spec] * count,
        scratch_shapes=[pltpu.SemaphoreType.DMA((count,))],
        compiler_params=pltpu.CompilerParams(vmem_limit_bytes=VMEM_LIMIT),
        cost_estimate=pl.CostEstimate(flops=0, bytes_accessed=12 * 2**20, transcendentals=0),
        name="pack_q",
    )(source, q)
    return [outs[step * parts : (step + 1) * parts] for step in range(blocks - 1)]


def attend_kernel(blocks, step, first_head, heads, *refs):
    source_ref, doc_ref, q_ref = refs[:3]
    windows = refs[3 : 3 + 3 * blocks]
    has_base = step != 0 or first_head != 0
    out_ref = refs[3 + 3 * blocks + has_base]
    q_buf, k_buf, v_buf, o_buf, s_buf, acc, q_sem, kv_sem, o_sem = refs[4 + 3 * blocks + has_base :]
    dp, sp = position()
    slot = landing_slot(source_ref, blocks, dp, sp, dp ^ step)
    block = sp * blocks + slot
    count = jnp.int32(1)
    for back in range(1, MOST_BLK):
        same = (block >= back) & (doc_ref[0, jnp.maximum(block - back, 0)] == doc_ref[0, block])
        count = count + same.astype(jnp.int32)
    first = block - count + 1

    if step == 0:
        rows = block_rows(leaving_slot(source_ref, blocks, dp, sp, dp))
        q_from = q_ref.at[rows, pl.ds(first_head * GROUP_WIDTH, heads * GROUP_WIDTH)]
    else:
        q_from = q_ref
    q_copy = pltpu.make_async_copy(q_from, q_buf, q_sem)
    q_copy.start()
    kv_lanes = pl.ds(first_head * HEAD_WIDTH, heads * HEAD_WIDTH)

    def fetch(number, carry):
        wanted = first + number
        column = wanted // blocks
        entry = source_ref[column, dp * blocks + wanted % blocks]
        code = (column - sp + 2) * blocks + ((entry // blocks) ^ dp)
        for index, window in enumerate(windows):

            @pl.when(code == index)
            def _():
                pltpu.make_async_copy(
                    window.at[0, :, kv_lanes], k_buf.at[number], kv_sem.at[number, 0]
                ).start()
                pltpu.make_async_copy(
                    window.at[1, :, kv_lanes], v_buf.at[number], kv_sem.at[number, 1]
                ).start()

        return carry

    lax.fori_loop(0, count, fetch, 0)

    def arrive(number, carry):
        pltpu.make_async_copy(
            windows[0].at[0, :, kv_lanes], k_buf.at[number], kv_sem.at[number, 0]
        ).wait()
        pltpu.make_async_copy(
            windows[0].at[1, :, kv_lanes], v_buf.at[number], kv_sem.at[number, 1]
        ).wait()
        return carry

    lax.fori_loop(0, count, arrive, 0)
    q_copy.wait()

    pairs = GROUP_WIDTH // PAIR
    tops = BALANCE_TOKENS // 8

    def one_head(head, carry):
        lanes = pl.ds(pl.multiple_of(head * HEAD_WIDTH, HEAD_WIDTH), HEAD_WIDTH)

        def q_of(pair):
            parts = []
            for half in range(PAIR // HEAD_WIDTH):
                start = head * GROUP_WIDTH + (pair * PAIR + half * HEAD_WIDTH)
                parts.append(
                    q_buf[:, pl.ds(pl.multiple_of(start, HEAD_WIDTH), HEAD_WIDTH)]
                )
            return jnp.concatenate(parts, axis=0)

        def scores(number, pair):
            return lax.dot_general(
                k_buf[number, :, lanes],
                q_of(pair),
                (((1,), (1,)), ((), ())),
                preferred_element_type=jnp.float32,
            )

        def put(number, pair, values):
            rows = pl.ds(pl.multiple_of(number * BALANCE_TOKENS, BALANCE_TOKENS), BALANCE_TOKENS)
            s_buf[rows, pair * PAIR : (pair + 1) * PAIR] = values
            return jnp.max(values.reshape(tops, 8, PAIR), axis=0)

        last = count - 1
        key_pos = lax.broadcasted_iota(jnp.int32, (BALANCE_TOKENS, PAIR), 0)
        query_pos = lax.broadcasted_iota(jnp.int32, (BALANCE_TOKENS, PAIR), 1) % BALANCE_TOKENS
        allowed = key_pos <= query_pos
        top = tuple(
            put(last, pair, jnp.where(allowed, scores(last, pair), -1e30)) for pair in range(pairs)
        )

        def first_pass(number, top):
            return tuple(
                jnp.maximum(top[pair], put(number, pair, scores(number, pair)))
                for pair in range(pairs)
            )

        top = lax.fori_loop(0, last, first_pass, top)
        shift = tuple(
            jnp.broadcast_to(jnp.max(t, axis=0, keepdims=True) * EXP2_SCALE, (8, PAIR)) for t in top
        )
        acc[...] = jnp.zeros_like(acc)

        def second_pass(number, total):
            rows = pl.ds(pl.multiple_of(number * BALANCE_TOKENS, BALANCE_TOKENS), BALANCE_TOKENS)
            values = v_buf[number, :, lanes]
            new_total = []
            for pair in range(pairs):
                span = slice(pair * PAIR, (pair + 1) * PAIR)
                held = s_buf[rows, span].reshape(tops, 8, PAIR)
                weight = jnp.exp2(held * EXP2_SCALE - shift[pair][None])
                new_total.append(total[pair] + jnp.sum(weight, axis=0))
                rounded = weight.reshape(BALANCE_TOKENS, PAIR).astype(jnp.bfloat16)
                acc[:, span] += lax.dot_general(
                    values,
                    rounded,
                    (((0,), (0,)), ((), ())),
                    preferred_element_type=jnp.float32,
                )
            return tuple(new_total)

        total = lax.fori_loop(
            0, count, second_pass, tuple(jnp.zeros((8, PAIR), jnp.float32) for _ in range(pairs))
        )
        for pair in range(pairs):
            inverse = 1.0 / jnp.sum(total[pair], axis=0, keepdims=True)
            scaled = acc[:, pair * PAIR : (pair + 1) * PAIR] * inverse
            for half in range(PAIR // HEAD_WIDTH):
                start = head * GROUP_WIDTH + (pair * PAIR + half * HEAD_WIDTH)
                piece = scaled[:, half * HEAD_WIDTH : (half + 1) * HEAD_WIDTH]
                o_buf[:, pl.ds(pl.multiple_of(start, HEAD_WIDTH), HEAD_WIDTH)] = piece.T.astype(
                    o_buf.dtype
                )
        return carry

    lax.fori_loop(0, heads, one_head, 0)
    o_copy = pltpu.make_async_copy(
        o_buf,
        out_ref.at[block_rows(slot), pl.ds(first_head * GROUP_WIDTH, heads * GROUP_WIDTH)],
        o_sem,
    )
    o_copy.start()
    o_copy.wait()


def attend(source, docs, q, windows, base, shape, blocks, step, first_head, heads):
    any_spec = pl.BlockSpec(memory_space=pl.ANY)
    smem_spec = pl.BlockSpec(memory_space=pltpu.SMEM)
    operands = [source, docs, q, *windows] + ([] if base is None else [base])
    work = BALANCE_TOKENS * heads * GROUP_WIDTH * BALANCE_TOKENS
    width = heads * GROUP_WIDTH
    return pl.pallas_call(
        functools.partial(attend_kernel, blocks, step, first_head, heads),
        out_shape=jax.ShapeDtypeStruct(shape, q.dtype),
        in_specs=[smem_spec, smem_spec] + [any_spec] * (len(operands) - 2),
        out_specs=any_spec,
        scratch_shapes=[
            pltpu.VMEM((BALANCE_TOKENS, width), q.dtype),
            pltpu.VMEM((MOST_BLK, BALANCE_TOKENS, heads * HEAD_WIDTH), q.dtype),
            pltpu.VMEM((MOST_BLK, BALANCE_TOKENS, heads * HEAD_WIDTH), q.dtype),
            pltpu.VMEM((BALANCE_TOKENS, width), q.dtype),
            pltpu.VMEM((MOST_BLK * BALANCE_TOKENS, GROUP_WIDTH), jnp.float32),
            pltpu.VMEM((HEAD_WIDTH, GROUP_WIDTH), jnp.float32),
            pltpu.SemaphoreType.DMA,
            pltpu.SemaphoreType.DMA((MOST_BLK, 2)),
            pltpu.SemaphoreType.DMA,
        ],
        input_output_aliases={} if base is None else {len(operands) - 1: 0},
        compiler_params=pltpu.CompilerParams(vmem_limit_bytes=VMEM_LIMIT),
        cost_estimate=pl.CostEstimate(
            flops=4 * work * MOST_BLK, bytes_accessed=6 * 2**20, transcendentals=work * MOST_BLK // 128
        ),
        name=f"attend_{step}_{first_head}",
    )(*operands)


def on_device(query_matrix, key_matrix, value_matrix, block_source, documents):
    dp_count = lax.axis_size("dp")
    sp_count = lax.axis_size("sp")
    sp = lax.axis_index("sp")
    tok_dev = query_matrix.shape[1]
    blocks = tok_dev // BALANCE_TOKENS
    assert blocks == dp_count and dp_count & (dp_count - 1) == 0
    q = query_matrix.reshape(tok_dev, QUERY_HEADS * HEAD_WIDTH)
    k = key_matrix.reshape(tok_dev, KEY_VALUE_HEADS * HEAD_WIDTH)
    v = value_matrix.reshape(tok_dev, KEY_VALUE_HEADS * HEAD_WIDTH)

    def swap_dp(x, step):
        return lax.ppermute(x, "dp", [(i, i ^ step) for i in range(dp_count)])

    def ahead(x):
        return lax.ppermute(x, "sp", [(i, i + 2) for i in range(sp_count - 2)])

    def swap_core(x):
        return lax.ppermute(x, "sp", [(i, i ^ 1) for i in range(sp_count)])

    own = list(pack_kv(block_source, k, v, blocks))
    own = [own[0]] + [swap_dp(own[step], step) for step in range(1, blocks)]
    parts = 2
    moved = pack_q(block_source, q, blocks, parts)
    moved = [[swap_dp(x, step + 1) for x in group] for step, group in enumerate(moved)]
    back_two = [ahead(x) for x in own]
    back_one = [
        swap_core(jnp.where(sp % 2 == 0, mine, theirs)) for mine, theirs in zip(own, back_two)
    ]
    windows = [*back_two, *back_one, *own]

    call = functools.partial(
        attend, block_source, documents, windows=windows, shape=q.shape, blocks=blocks
    )
    out = call(q, base=None, step=0, first_head=0, heads=KEY_VALUE_HEADS)
    heads = KEY_VALUE_HEADS // parts
    for part in range(parts):
        for step in (3, 1, 2):
            out = call(
                moved[step - 1][part], base=out, step=step, first_head=part * heads, heads=heads
            )
    return out.reshape(1, tok_dev, QUERY_HEADS * HEAD_WIDTH)


def solution(mesh):
    placed = (P("dp", "sp", None), P("dp", "sp", None), P("dp", "sp", None), P(), P("dp", None))
    return jax.shard_map(
        on_device, mesh=mesh, in_specs=placed, out_specs=P("dp", "sp", None), check_vma=False
    )
```

```python
import functools
import math

import jax
import jax.numpy as jnp
from jax import lax
from jax.experimental import pallas as pl
from jax.experimental.pallas import tpu as pltpu
from jax.sharding import PartitionSpec as P

QUERY_HEADS = 64
KEY_VALUE_HEADS = 8
HEAD_WIDTH = 128
BALANCE_TOKENS = 128
MOST_BLK = 8
GROUP_HEADS = QUERY_HEADS // KEY_VALUE_HEADS
GROUP_WIDTH = GROUP_HEADS * HEAD_WIDTH
PAIR = 256
EXP2_SCALE = math.log2(math.e) / math.sqrt(HEAD_WIDTH)
VMEM_LIMIT = 40 * 1024 * 1024


def position():
    return lax.axis_index("dp"), lax.axis_index("sp")


def leaving_slot(source_ref, blocks, dp, sp, other):
    slot = jnp.int32(0)
    for place in range(blocks):
        entry = source_ref[sp, other * blocks + place]
        slot = jnp.where(entry // blocks == dp, entry % blocks, slot)
    return slot


def landing_slot(source_ref, blocks, dp, sp, other):
    slot = jnp.int32(0)
    for place in range(blocks):
        entry = source_ref[sp, dp * blocks + place]
        slot = jnp.where(entry // blocks == other, place, slot)
    return slot


def block_rows(slot):
    return pl.ds(pl.multiple_of(slot * BALANCE_TOKENS, BALANCE_TOKENS), BALANCE_TOKENS)


def pack_kv_kernel(blocks, source_ref, k_ref, v_ref, *rest):
    outs, (buf, sem) = rest[:blocks], rest[blocks:]
    dp, sp = position()
    reads, writes = [], []
    for order, step in enumerate([*range(1, blocks), 0]):
        rows = block_rows(leaving_slot(source_ref, blocks, dp, sp, dp ^ step))
        for which, ref in enumerate((k_ref, v_ref)):
            place, number = buf.at[order, which], 2 * order + which
            reads.append(pltpu.make_async_copy(ref.at[rows], place, sem.at[number, 0]))
            writes.append(
                pltpu.make_async_copy(place, outs[step].at[which], sem.at[number, 1])
            )
    for copy in reads:
        copy.start()
    for read, write in zip(reads, writes):
        read.wait()
        write.start()
    for copy in writes:
        copy.wait()


def pack_kv(source, k, v, blocks):
    width = k.shape[1]
    hbm = pl.BlockSpec(memory_space=pltpu.HBM)
    return pl.pallas_call(
        functools.partial(pack_kv_kernel, blocks),
        out_shape=[jax.ShapeDtypeStruct((2, BALANCE_TOKENS, width), k.dtype)] * blocks,
        in_specs=[pl.BlockSpec(memory_space=pltpu.SMEM), hbm, hbm],
        out_specs=[hbm] * blocks,
        scratch_shapes=[
            pltpu.VMEM((blocks, 2, BALANCE_TOKENS, width), k.dtype),
            pltpu.SemaphoreType.DMA((2 * blocks, 2)),
        ],
        compiler_params=pltpu.CompilerParams(vmem_limit_bytes=VMEM_LIMIT),
        cost_estimate=pl.CostEstimate(flops=0, bytes_accessed=4 * 2**20, transcendentals=0),
        name="pack_kv",
    )(source, k, v)


def pack_q_kernel(blocks, step, first, source_ref, q_ref, out_ref, buf, turned, sem):
    dp, sp = position()
    rows = block_rows(leaving_slot(source_ref, blocks, dp, sp, dp ^ step))
    width = buf.shape[1]
    groups = width // GROUP_WIDTH
    reads, writes = [], []
    for group in range(groups):
        span = pl.ds(group * GROUP_WIDTH, GROUP_WIDTH)
        reads.append(
            pltpu.make_async_copy(
                q_ref.at[rows, pl.ds(first + group * GROUP_WIDTH, GROUP_WIDTH)],
                buf.at[:, span],
                sem.at[group, 0],
            )
        )
        writes.append(
            pltpu.make_async_copy(turned.at[span], out_ref.at[span], sem.at[group, 1])
        )
    for copy in reads:
        copy.start()
    for group in range(groups):
        reads[group].wait()
        for head in range(GROUP_HEADS):
            start = group * GROUP_WIDTH + head * HEAD_WIDTH
            turned[start : start + HEAD_WIDTH] = buf[:, start : start + HEAD_WIDTH].T
        writes[group].start()
    for copy in writes:
        copy.wait()


def pack_q(source, q, blocks, step, first_head, heads):
    width = heads * GROUP_WIDTH
    hbm = pl.BlockSpec(memory_space=pltpu.HBM)
    return pl.pallas_call(
        functools.partial(pack_q_kernel, blocks, step, first_head * GROUP_WIDTH),
        out_shape=jax.ShapeDtypeStruct((width, BALANCE_TOKENS), q.dtype),
        in_specs=[pl.BlockSpec(memory_space=pltpu.SMEM), hbm],
        out_specs=hbm,
        scratch_shapes=[
            pltpu.VMEM((BALANCE_TOKENS, width), q.dtype),
            pltpu.VMEM((width, BALANCE_TOKENS), q.dtype),
            pltpu.SemaphoreType.DMA((heads, 2)),
        ],
        compiler_params=pltpu.CompilerParams(vmem_limit_bytes=VMEM_LIMIT),
        cost_estimate=pl.CostEstimate(
            flops=0, bytes_accessed=4 * width * BALANCE_TOKENS, transcendentals=0
        ),
        name=f"pack_q_{step}_{first_head}",
    )(source, q)


def attend_kernel(blocks, step, first_head, heads, *refs):
    source_ref, doc_ref, q_ref = refs[:3]
    windows = refs[3 : 3 + 3 * blocks]
    has_base = step != 0 or first_head != 0
    out_ref = refs[3 + 3 * blocks + has_base]
    q_buf, k_buf, v_buf, o_buf, s_buf, vt_buf, q_sem, kv_sem, o_sem = refs[
        4 + 3 * blocks + has_base :
    ]
    dp, sp = position()
    q_copy = pltpu.make_async_copy(q_ref, q_buf, q_sem)
    q_copy.start()
    slot = landing_slot(source_ref, blocks, dp, sp, dp ^ step)
    block = sp * blocks + slot
    count = jnp.int32(1)
    for back in range(1, MOST_BLK):
        same = (block >= back) & (doc_ref[0, jnp.maximum(block - back, 0)] == doc_ref[0, block])
        count = count + same.astype(jnp.int32)
    odd = count % 2 == 1
    half = (count + 1) // 2
    fetched = 2 * half
    first = block - fetched + 1
    kv_lanes = pl.ds(first_head * HEAD_WIDTH, heads * HEAD_WIDTH)

    def fetch(number, carry):
        wanted = jnp.maximum(first + number, 0)
        column = wanted // blocks
        entry = source_ref[column, dp * blocks + wanted % blocks]
        code = (column - sp + 2) * blocks + ((entry // blocks) ^ dp)
        rows = block_rows(number)
        for index, window in enumerate(windows):

            @pl.when(code == index)
            def _():
                pltpu.make_async_copy(
                    window.at[0, :, kv_lanes], k_buf.at[rows], kv_sem.at[number, 0]
                ).start()
                pltpu.make_async_copy(
                    window.at[1, :, kv_lanes], v_buf.at[rows], kv_sem.at[number, 1]
                ).start()

        return carry

    lax.fori_loop(0, fetched, fetch, 0)

    def arrive(number, carry):
        rows = block_rows(number)
        pltpu.make_async_copy(
            windows[0].at[0, :, kv_lanes], k_buf.at[rows], kv_sem.at[number, 0]
        ).wait()
        pltpu.make_async_copy(
            windows[0].at[1, :, kv_lanes], v_buf.at[rows], kv_sem.at[number, 1]
        ).wait()
        return carry

    lax.fori_loop(0, fetched, arrive, 0)
    q_copy.wait()

    pairs = GROUP_WIDTH // PAIR
    eights = PAIR // 8

    def one_head(chunks, head):
        lanes = pl.ds(pl.multiple_of(head * HEAD_WIDTH, HEAD_WIDTH), HEAD_WIDTH)
        for chunk in range(chunks):
            keys = slice(chunk * PAIR, (chunk + 1) * PAIR)
            vt_buf[:, keys] = v_buf[keys, lanes].T
        for pair in range(pairs):
            parts = []
            for member in range(PAIR // HEAD_WIDTH):
                start = head * GROUP_WIDTH + (pair * PAIR + member * HEAD_WIDTH)
                parts.append(q_buf[pl.ds(pl.multiple_of(start, HEAD_WIDTH), HEAD_WIDTH)])
            turned = jnp.concatenate(parts, axis=1)
            top = None
            for chunk in range(chunks):
                keys = slice(chunk * PAIR, (chunk + 1) * PAIR)
                held = jnp.dot(k_buf[keys, lanes], turned, preferred_element_type=jnp.float32)
                if chunk in (0, chunks - 1):
                    row = lax.broadcasted_iota(jnp.int32, (PAIR, PAIR), 0)
                    column = lax.broadcasted_iota(jnp.int32, (PAIR, PAIR), 1) % BALANCE_TOKENS
                    allowed = None
                    if chunk == chunks - 1:
                        allowed = row <= column + (PAIR - BALANCE_TOKENS)
                    if chunk == 0:
                        real = row >= jnp.where(odd, BALANCE_TOKENS, 0)
                        allowed = real if allowed is None else allowed & real
                    held = jnp.where(allowed, held, -1e30)
                s_buf[pair, keys] = held
                high = jnp.max(held.reshape(eights, 8, PAIR), axis=0)
                top = high if top is None else jnp.maximum(top, high)
            shift = jnp.max(top, axis=0, keepdims=True) * EXP2_SCALE
            total = summed = None
            for chunk in range(chunks):
                keys = slice(chunk * PAIR, (chunk + 1) * PAIR)
                weight = jnp.exp2(s_buf[pair, keys] * EXP2_SCALE - shift)
                added = jnp.sum(weight.reshape(eights, 8, PAIR), axis=0)
                total = added if total is None else total + added
                mixed = jnp.dot(
                    vt_buf[:, keys],
                    weight.astype(jnp.bfloat16),
                    preferred_element_type=jnp.float32,
                )
                summed = mixed if summed is None else summed + mixed
            scaled = summed * (1.0 / jnp.sum(total, axis=0, keepdims=True))
            for member in range(PAIR // HEAD_WIDTH):
                start = head * GROUP_WIDTH + (pair * PAIR + member * HEAD_WIDTH)
                piece = scaled[:, member * HEAD_WIDTH : (member + 1) * HEAD_WIDTH]
                o_buf[:, pl.ds(pl.multiple_of(start, HEAD_WIDTH), HEAD_WIDTH)] = piece.T.astype(
                    o_buf.dtype
                )

    for chunks in range(1, MOST_BLK * BALANCE_TOKENS // PAIR + 1):

        @pl.when(half == chunks)
        def _():
            @pl.loop(0, heads)
            def _(head):
                one_head(chunks, head)

    o_copy = pltpu.make_async_copy(
        o_buf,
        out_ref.at[block_rows(slot), pl.ds(first_head * GROUP_WIDTH, heads * GROUP_WIDTH)],
        o_sem,
    )
    o_copy.start()
    o_copy.wait()


def attend(source, docs, q, windows, base, shape, blocks, step, first_head, heads):
    hbm = pl.BlockSpec(memory_space=pltpu.HBM)
    smem = pl.BlockSpec(memory_space=pltpu.SMEM)
    operands = [source, docs, q, *windows] + ([] if base is None else [base])
    work = BALANCE_TOKENS * heads * GROUP_WIDTH * BALANCE_TOKENS
    width = heads * GROUP_WIDTH
    reach = MOST_BLK * BALANCE_TOKENS
    return pl.pallas_call(
        functools.partial(attend_kernel, blocks, step, first_head, heads),
        out_shape=jax.ShapeDtypeStruct(shape, q.dtype),
        in_specs=[smem, smem] + [hbm] * (len(operands) - 2),
        out_specs=hbm,
        scratch_shapes=[
            pltpu.VMEM((width, BALANCE_TOKENS), q.dtype),
            pltpu.VMEM((reach, heads * HEAD_WIDTH), q.dtype),
            pltpu.VMEM((reach, heads * HEAD_WIDTH), q.dtype),
            pltpu.VMEM((BALANCE_TOKENS, width), q.dtype),
            pltpu.VMEM((GROUP_WIDTH // PAIR, reach, PAIR), jnp.float32),
            pltpu.VMEM((HEAD_WIDTH, reach), q.dtype),
            pltpu.SemaphoreType.DMA,
            pltpu.SemaphoreType.DMA((MOST_BLK, 2)),
            pltpu.SemaphoreType.DMA,
        ],
        input_output_aliases={} if base is None else {len(operands) - 1: 0},
        compiler_params=pltpu.CompilerParams(vmem_limit_bytes=VMEM_LIMIT),
        cost_estimate=pl.CostEstimate(
            flops=4 * work * MOST_BLK, bytes_accessed=6 * 2**20, transcendentals=work * MOST_BLK // 128
        ),
        name=f"attend_{step}_{first_head}",
    )(*operands)


def on_device(query_matrix, key_matrix, value_matrix, block_source, documents):
    dp_count = lax.axis_size("dp")
    sp_count = lax.axis_size("sp")
    sp = lax.axis_index("sp")
    tok_dev = query_matrix.shape[1]
    blocks = tok_dev // BALANCE_TOKENS
    assert blocks == dp_count and dp_count & (dp_count - 1) == 0
    q = query_matrix.reshape(tok_dev, QUERY_HEADS * HEAD_WIDTH)
    k = key_matrix.reshape(tok_dev, KEY_VALUE_HEADS * HEAD_WIDTH)
    v = value_matrix.reshape(tok_dev, KEY_VALUE_HEADS * HEAD_WIDTH)

    def swap_dp(x, step):
        return lax.ppermute(x, "dp", [(i, i ^ step) for i in range(dp_count)])

    def ahead(x):
        return lax.ppermute(x, "sp", [(i, i + 2) for i in range(sp_count - 2)])

    def swap_core(x):
        return lax.ppermute(x, "sp", [(i, i ^ 1) for i in range(sp_count)])

    own = list(pack_kv(block_source, k, v, blocks))
    own = [own[0]] + [swap_dp(own[step], step) for step in range(1, blocks)]
    parts = 2
    heads = KEY_VALUE_HEADS // parts
    pieces = [(step, part) for part in range(parts) for step in (3, 1, 2)]
    packed = [pack_q(block_source, q, blocks, step, part * heads, heads) for step, part in pieces]
    stay = pack_q(block_source, q, blocks, 0, 0, KEY_VALUE_HEADS)
    packed, own = lax.optimization_barrier((packed, own))
    moved = [swap_dp(x, step) for x, (step, part) in zip(packed, pieces)]
    back_two = [ahead(x) for x in own]
    back_one = [
        swap_core(jnp.where(sp % 2 == 0, mine, theirs)) for mine, theirs in zip(own, back_two)
    ]
    windows = [*back_two, *back_one, *own]

    call = functools.partial(
        attend, block_source, documents, windows=windows, shape=q.shape, blocks=blocks
    )
    out = call(stay, base=None, step=0, first_head=0, heads=KEY_VALUE_HEADS)
    for x, (step, part) in zip(moved, pieces):
        out = call(x, base=out, step=step, first_head=part * heads, heads=heads)
    return out.reshape(1, tok_dev, QUERY_HEADS * HEAD_WIDTH)


def solution(mesh):
    placed = (P("dp", "sp", None), P("dp", "sp", None), P("dp", "sp", None), P(), P("dp", None))
    return jax.shard_map(
        on_device, mesh=mesh, in_specs=placed, out_specs=P("dp", "sp", None), check_vma=False
    )
```

```python
import functools
import math

import jax
import jax.numpy as jnp
from jax import lax
from jax.experimental import pallas as pl
from jax.experimental.pallas import tpu as pltpu
from jax.sharding import PartitionSpec as P

QUERY_HEADS = 64
KEY_VALUE_HEADS = 8
HEAD_WIDTH = 128
BALANCE_TOKENS = 128
MOST_BLK = 8
GROUP_HEADS = QUERY_HEADS // KEY_VALUE_HEADS
GROUP_WIDTH = GROUP_HEADS * HEAD_WIDTH
PAIR = 256
EXP2_SCALE = math.log2(math.e) / math.sqrt(HEAD_WIDTH)
VMEM_LIMIT = 64 * 1024 * 1024


def position():
    return lax.axis_index("dp"), lax.axis_index("sp")


def leaving_slot(source_ref, blocks, dp, sp, other):
    slot = jnp.int32(0)
    for place in range(blocks):
        entry = source_ref[sp, other * blocks + place]
        slot = jnp.where(entry // blocks == dp, entry % blocks, slot)
    return slot


def landing_slot(source_ref, blocks, dp, sp, other):
    slot = jnp.int32(0)
    for place in range(blocks):
        entry = source_ref[sp, dp * blocks + place]
        slot = jnp.where(entry // blocks == other, place, slot)
    return slot


def block_rows(slot):
    return pl.ds(pl.multiple_of(slot * BALANCE_TOKENS, BALANCE_TOKENS), BALANCE_TOKENS)


def pack_kv_kernel(blocks, source_ref, k_ref, v_ref, *rest):
    outs, (buf, sem) = rest[:blocks], rest[blocks:]
    dp, sp = position()
    reads, writes = [], []
    for order, step in enumerate([*range(1, blocks), 0]):
        rows = block_rows(leaving_slot(source_ref, blocks, dp, sp, dp ^ step))
        for which, ref in enumerate((k_ref, v_ref)):
            place, number = buf.at[order, which], 2 * order + which
            reads.append(pltpu.make_async_copy(ref.at[rows], place, sem.at[number, 0]))
            writes.append(
                pltpu.make_async_copy(place, outs[step].at[which], sem.at[number, 1])
            )
    for copy in reads:
        copy.start()
    for read, write in zip(reads, writes):
        read.wait()
        write.start()
    for copy in writes:
        copy.wait()


def pack_kv(source, k, v, blocks):
    width = k.shape[1]
    hbm = pl.BlockSpec(memory_space=pltpu.HBM)
    return pl.pallas_call(
        functools.partial(pack_kv_kernel, blocks),
        out_shape=[jax.ShapeDtypeStruct((2, BALANCE_TOKENS, width), k.dtype)] * blocks,
        in_specs=[pl.BlockSpec(memory_space=pltpu.SMEM), hbm, hbm],
        out_specs=[hbm] * blocks,
        scratch_shapes=[
            pltpu.VMEM((blocks, 2, BALANCE_TOKENS, width), k.dtype),
            pltpu.SemaphoreType.DMA((2 * blocks, 2)),
        ],
        compiler_params=pltpu.CompilerParams(vmem_limit_bytes=VMEM_LIMIT),
        cost_estimate=pl.CostEstimate(flops=0, bytes_accessed=4 * 2**20, transcendentals=0),
        name="pack_kv",
    )(source, k, v)


def pack_q_kernel(blocks, step, first, source_ref, q_ref, out_ref, buf, turned, sem):
    dp, sp = position()
    rows = block_rows(leaving_slot(source_ref, blocks, dp, sp, dp ^ step))
    width = buf.shape[1]
    groups = width // GROUP_WIDTH
    reads, writes = [], []
    for group in range(groups):
        span = pl.ds(group * GROUP_WIDTH, GROUP_WIDTH)
        reads.append(
            pltpu.make_async_copy(
                q_ref.at[rows, pl.ds(first + group * GROUP_WIDTH, GROUP_WIDTH)],
                buf.at[:, span],
                sem.at[group, 0],
            )
        )
        writes.append(
            pltpu.make_async_copy(turned.at[span], out_ref.at[span], sem.at[group, 1])
        )
    for copy in reads:
        copy.start()
    for group in range(groups):
        reads[group].wait()
        for head in range(GROUP_HEADS):
            start = group * GROUP_WIDTH + head * HEAD_WIDTH
            turned[start : start + HEAD_WIDTH] = buf[:, start : start + HEAD_WIDTH].T
        writes[group].start()
    for copy in writes:
        copy.wait()


def pack_q(source, q, blocks, step, first_head, heads):
    width = heads * GROUP_WIDTH
    hbm = pl.BlockSpec(memory_space=pltpu.HBM)
    return pl.pallas_call(
        functools.partial(pack_q_kernel, blocks, step, first_head * GROUP_WIDTH),
        out_shape=jax.ShapeDtypeStruct((width, BALANCE_TOKENS), q.dtype),
        in_specs=[pl.BlockSpec(memory_space=pltpu.SMEM), hbm],
        out_specs=hbm,
        scratch_shapes=[
            pltpu.VMEM((BALANCE_TOKENS, width), q.dtype),
            pltpu.VMEM((width, BALANCE_TOKENS), q.dtype),
            pltpu.SemaphoreType.DMA((heads, 2)),
        ],
        compiler_params=pltpu.CompilerParams(vmem_limit_bytes=VMEM_LIMIT),
        cost_estimate=pl.CostEstimate(
            flops=0, bytes_accessed=4 * width * BALANCE_TOKENS, transcendentals=0
        ),
        name=f"pack_q_{step}_{first_head}",
    )(source, q)


def attend_kernel(blocks, step, first_head, heads, *refs):
    source_ref, doc_ref, q_ref = refs[:3]
    windows = refs[3:8]
    has_base = step != 0 or first_head != 0
    out_ref = refs[8 + has_base]
    q_buf, k_buf, v_buf, o_buf, s_buf, vt_buf, q_sem, kv_sem, o_sem = refs[9 + has_base :]
    dp, sp = position()
    q_copy = pltpu.make_async_copy(q_ref, q_buf, q_sem)
    q_copy.start()
    slot = landing_slot(source_ref, blocks, dp, sp, dp ^ step)
    block = sp * blocks + slot
    count = jnp.int32(1)
    for back in range(1, MOST_BLK):
        same = (block >= back) & (doc_ref[0, jnp.maximum(block - back, 0)] == doc_ref[0, block])
        count = count + same.astype(jnp.int32)
    skipped = (count % 2) * BALANCE_TOKENS
    half = (count + 1) // 2
    fetched = 2 * half
    first = block - fetched + 1
    kv_lanes = pl.ds(first_head * HEAD_WIDTH, heads * HEAD_WIDTH)

    def fetch(number, carry):
        wanted = jnp.maximum(first + number, 0)
        column = wanted // blocks
        entry = source_ref[column, dp * blocks + wanted % blocks]
        partner = (entry // blocks) ^ dp
        back, stayed = sp - column, partner == 0
        rows = block_rows(number)
        choices = (
            ((back == 2) & stayed, 0),
            ((back == 2) & ~stayed, partner - 1),
            (back == 1, partner),
            ((back == 0) & stayed, 0),
            ((back == 0) & ~stayed, partner - 1),
        )
        for window, (chosen, place) in zip(windows, choices):

            @pl.when(chosen)
            def _():
                source = window.at[place]
                pltpu.make_async_copy(
                    source.at[0, :, kv_lanes], k_buf.at[rows], kv_sem.at[number, 0]
                ).start()
                pltpu.make_async_copy(
                    source.at[1, :, kv_lanes], v_buf.at[rows], kv_sem.at[number, 1]
                ).start()

        return carry

    lax.fori_loop(0, fetched, fetch, 0)

    def arrive(number, carry):
        rows = block_rows(number)
        pltpu.make_async_copy(
            windows[0].at[0, 0, :, kv_lanes], k_buf.at[rows], kv_sem.at[number, 0]
        ).wait()
        pltpu.make_async_copy(
            windows[0].at[0, 1, :, kv_lanes], v_buf.at[rows], kv_sem.at[number, 1]
        ).wait()
        return carry

    lax.fori_loop(0, fetched, arrive, 0)
    q_copy.wait()

    pairs = GROUP_WIDTH // PAIR
    eights = PAIR // 8

    def one_head(chunks, head):
        lanes = pl.ds(pl.multiple_of(head * HEAD_WIDTH, HEAD_WIDTH), HEAD_WIDTH)
        tops = [None] * pairs
        row = lax.broadcasted_iota(jnp.int32, (PAIR, PAIR), 0)
        column = lax.broadcasted_iota(jnp.int32, (PAIR, PAIR), 1) & (BALANCE_TOKENS - 1)
        for chunk in range(chunks):
            keys = slice(chunk * PAIR, (chunk + 1) * PAIR)
            allowed = None
            if chunk == chunks - 1:
                allowed = row <= column + (PAIR - BALANCE_TOKENS)
            if chunk == 0:
                real = row >= skipped
                allowed = real if allowed is None else allowed & real
            vt_buf[:, keys] = v_buf[keys, lanes].T
            for pair in range(pairs):
                parts = []
                for member in range(PAIR // HEAD_WIDTH):
                    start = head * GROUP_WIDTH + (pair * PAIR + member * HEAD_WIDTH)
                    parts.append(q_buf[pl.ds(pl.multiple_of(start, HEAD_WIDTH), HEAD_WIDTH)])
                held = jnp.dot(
                    k_buf[keys, lanes],
                    jnp.concatenate(parts, axis=1),
                    preferred_element_type=jnp.float32,
                )
                if allowed is not None:
                    held = jnp.where(allowed, held, -1e30)
                s_buf[pair, keys] = held
                high = jnp.max(held.reshape(eights, 8, PAIR), axis=0)
                tops[pair] = high if chunk == 0 else jnp.maximum(tops[pair], high)
        shifts = [jnp.max(top, axis=0, keepdims=True) * EXP2_SCALE for top in tops]

        def mix(pair):
            total = summed = None
            for chunk in range(chunks):
                keys = slice(chunk * PAIR, (chunk + 1) * PAIR)
                weight = jnp.exp2(s_buf[pair, keys] * EXP2_SCALE - shifts[pair])
                added = jnp.sum(weight.reshape(eights, 8, PAIR), axis=0)
                mixed = jnp.dot(
                    vt_buf[:, keys],
                    weight.astype(jnp.bfloat16),
                    preferred_element_type=jnp.float32,
                )
                total = added if chunk == 0 else total + added
                summed = mixed if chunk == 0 else summed + mixed
            return summed, total

        def finish(pair, summed, total):
            scaled = summed * (1.0 / jnp.sum(total, axis=0, keepdims=True))
            for member in range(PAIR // HEAD_WIDTH):
                start = head * GROUP_WIDTH + (pair * PAIR + member * HEAD_WIDTH)
                piece = scaled[:, member * HEAD_WIDTH : (member + 1) * HEAD_WIDTH]
                o_buf[:, pl.ds(pl.multiple_of(start, HEAD_WIDTH), HEAD_WIDTH)] = piece.T.astype(
                    o_buf.dtype
                )

        waiting = None
        for pair in range(pairs):
            mixed = mix(pair)
            if waiting is not None:
                finish(pair - 1, *waiting)
            waiting = mixed
        finish(pairs - 1, *waiting)

    for chunks in range(1, MOST_BLK * BALANCE_TOKENS // PAIR + 1):

        @pl.when(half == chunks)
        def _():
            @pl.loop(0, heads)
            def _(head):
                one_head(chunks, head)

    o_copy = pltpu.make_async_copy(
        o_buf,
        out_ref.at[block_rows(slot), pl.ds(first_head * GROUP_WIDTH, heads * GROUP_WIDTH)],
        o_sem,
    )
    o_copy.start()
    o_copy.wait()


def attend(source, docs, q, windows, base, shape, blocks, step, first_head, heads):
    hbm = pl.BlockSpec(memory_space=pltpu.HBM)
    smem = pl.BlockSpec(memory_space=pltpu.SMEM)
    operands = [source, docs, q, *windows] + ([] if base is None else [base])
    width = heads * GROUP_WIDTH
    reach = MOST_BLK * BALANCE_TOKENS
    return pl.pallas_call(
        functools.partial(attend_kernel, blocks, step, first_head, heads),
        out_shape=jax.ShapeDtypeStruct(shape, q.dtype),
        in_specs=[smem, smem] + [hbm] * (len(operands) - 2),
        out_specs=hbm,
        scratch_shapes=[
            pltpu.VMEM((width, BALANCE_TOKENS), q.dtype),
            pltpu.VMEM((reach, heads * HEAD_WIDTH), q.dtype),
            pltpu.VMEM((reach, heads * HEAD_WIDTH), q.dtype),
            pltpu.VMEM((BALANCE_TOKENS, width), q.dtype),
            pltpu.VMEM((GROUP_WIDTH // PAIR, reach, PAIR), jnp.float32),
            pltpu.VMEM((HEAD_WIDTH, reach), q.dtype),
            pltpu.SemaphoreType.DMA,
            pltpu.SemaphoreType.DMA((MOST_BLK, 2)),
            pltpu.SemaphoreType.DMA,
        ],
        input_output_aliases={} if base is None else {len(operands) - 1: 0},
        compiler_params=pltpu.CompilerParams(vmem_limit_bytes=VMEM_LIMIT),
        cost_estimate=pl.CostEstimate(flops=0, bytes_accessed=2**10, transcendentals=0),
        name=f"attend_{step}_{first_head}",
    )(*operands)


def on_device(query_matrix, key_matrix, value_matrix, block_source, documents):
    dp_count = lax.axis_size("dp")
    sp_count = lax.axis_size("sp")
    sp = lax.axis_index("sp")
    tok_dev = query_matrix.shape[1]
    blocks = tok_dev // BALANCE_TOKENS
    assert blocks == dp_count and dp_count & (dp_count - 1) == 0
    q = query_matrix.reshape(tok_dev, QUERY_HEADS * HEAD_WIDTH)
    k = key_matrix.reshape(tok_dev, KEY_VALUE_HEADS * HEAD_WIDTH)
    v = value_matrix.reshape(tok_dev, KEY_VALUE_HEADS * HEAD_WIDTH)

    def swap_dp(x, step):
        return lax.ppermute(x, "dp", [(i, i ^ step) for i in range(dp_count)])

    def ahead(x):
        return lax.ppermute(x, "sp", [(i, i + 2) for i in range(sp_count - 2)])

    def swap_core(x):
        return lax.ppermute(x, "sp", [(i, i ^ 1) for i in range(sp_count)])

    own = list(pack_kv(block_source, k, v, blocks))
    stays, leaves = own[0][None], own[1:]
    comes = [swap_dp(x, step) for step, x in enumerate(leaves, 1)]
    early = 3 * KEY_VALUE_HEADS // 8
    late = 3 * KEY_VALUE_HEADS // 4
    end = KEY_VALUE_HEADS
    last = blocks - 1
    opening = [(step, 0, early) for step in range(1, blocks)]
    closing = [(step, early, end) for step in range(1, last)]
    closing += [(last, early, late), (last, late, end)]

    def pack(pieces):
        return [pack_q(block_source, q, blocks, step, low, high - low) for step, low, high in pieces]

    def send(packed, pieces):
        return [swap_dp(x, step) for x, (step, _, _) in zip(packed, pieces)]

    kept = pack([(0, 0, end)])
    first, second = pack(opening), pack(closing)
    stays_two = ahead(stays)
    first, comes, stays_two = lax.optimization_barrier((first, comes, stays_two))
    comes = jnp.stack(comes)
    comes_two = ahead(comes)
    first = send(first, opening)
    first, second, comes_two = lax.optimization_barrier((first, second, comes_two))
    back_one = swap_core(
        jnp.where(
            sp % 2 == 0,
            jnp.concatenate([stays, comes]),
            jnp.concatenate([stays_two, comes_two]),
        )
    )
    second = send(second, closing)
    windows = [stays_two, comes_two, back_one, stays, comes]

    out = None
    for x, (step, low, high) in zip(
        kept + first + second, [(0, 0, end)] + opening + closing
    ):
        out = attend(
            block_source, documents, x, windows, out, q.shape, blocks, step, low, high - low
        )
    return out.reshape(1, tok_dev, QUERY_HEADS * HEAD_WIDTH)


def solution(mesh):
    placed = (P("dp", "sp", None), P("dp", "sp", None), P("dp", "sp", None), P(), P("dp", None))
    return jax.shard_map(
        on_device, mesh=mesh, in_specs=placed, out_specs=P("dp", "sp", None), check_vma=False
    )
```

```python
import functools
import math

import jax
import jax.numpy as jnp
from jax import lax
from jax.experimental import pallas as pl
from jax.experimental.pallas import tpu as pltpu
from jax.sharding import PartitionSpec as P

QUERY_HEADS = 64
KEY_VALUE_HEADS = 8
HEAD_WIDTH = 128
BALANCE_TOKENS = 128
MOST_BLK = 8
GROUP_HEADS = QUERY_HEADS // KEY_VALUE_HEADS
GROUP_WIDTH = GROUP_HEADS * HEAD_WIDTH
PAIR = 256
EXP2_SCALE = math.log2(math.e) / math.sqrt(HEAD_WIDTH)
VMEM_LIMIT = 64 * 1024 * 1024


def position():
    return lax.axis_index("dp"), lax.axis_index("sp")


def leaving_slot(source_ref, blocks, dp, sp, other):
    slot = jnp.int32(0)
    for place in range(blocks):
        entry = source_ref[sp, other * blocks + place]
        slot = jnp.where(entry // blocks == dp, entry % blocks, slot)
    return slot


def landing_slot(source_ref, blocks, dp, sp, other):
    slot = jnp.int32(0)
    for place in range(blocks):
        entry = source_ref[sp, dp * blocks + place]
        slot = jnp.where(entry // blocks == other, place, slot)
    return slot


def block_rows(slot):
    return pl.ds(pl.multiple_of(slot * BALANCE_TOKENS, BALANCE_TOKENS), BALANCE_TOKENS)


def pack_kv_kernel(blocks, source_ref, k_ref, v_ref, *rest):
    outs, (buf, sem) = rest[:blocks], rest[blocks:]
    dp, sp = position()
    reads, writes = [], []
    for order, step in enumerate([*range(1, blocks), 0]):
        rows = block_rows(leaving_slot(source_ref, blocks, dp, sp, dp ^ step))
        for which, ref in enumerate((k_ref, v_ref)):
            place, number = buf.at[order, which], 2 * order + which
            reads.append(pltpu.make_async_copy(ref.at[rows], place, sem.at[number, 0]))
            writes.append(
                pltpu.make_async_copy(place, outs[step].at[which], sem.at[number, 1])
            )
    for copy in reads:
        copy.start()
    for read, write in zip(reads, writes):
        read.wait()
        write.start()
    for copy in writes:
        copy.wait()


def pack_kv(source, k, v, blocks):
    width = k.shape[1]
    hbm = pl.BlockSpec(memory_space=pltpu.HBM)
    return pl.pallas_call(
        functools.partial(pack_kv_kernel, blocks),
        out_shape=[jax.ShapeDtypeStruct((2, BALANCE_TOKENS, width), k.dtype)] * blocks,
        in_specs=[pl.BlockSpec(memory_space=pltpu.SMEM), hbm, hbm],
        out_specs=[hbm] * blocks,
        scratch_shapes=[
            pltpu.VMEM((blocks, 2, BALANCE_TOKENS, width), k.dtype),
            pltpu.SemaphoreType.DMA((2 * blocks, 2)),
        ],
        compiler_params=pltpu.CompilerParams(vmem_limit_bytes=VMEM_LIMIT),
        cost_estimate=pl.CostEstimate(flops=0, bytes_accessed=4 * 2**20, transcendentals=0),
        name="pack_kv",
    )(source, k, v)


def pack_q_kernel(blocks, step, first, source_ref, q_ref, out_ref, buf, turned, sem):
    dp, sp = position()
    rows = block_rows(leaving_slot(source_ref, blocks, dp, sp, dp ^ step))
    groups = buf.shape[0]

    def read(group):
        lanes = pl.ds(pl.multiple_of(first + group * GROUP_WIDTH, GROUP_WIDTH), GROUP_WIDTH)
        return pltpu.make_async_copy(q_ref.at[rows, lanes], buf.at[group], sem.at[group, 0])

    def write(group):
        span = pl.ds(pl.multiple_of(group * GROUP_WIDTH, GROUP_WIDTH), GROUP_WIDTH)
        return pltpu.make_async_copy(turned.at[group], out_ref.at[span], sem.at[group, 1])

    @pl.loop(0, groups)
    def _(group):
        read(group).start()

    @pl.loop(0, groups)
    def _(group):
        read(group).wait()
        for head in range(GROUP_HEADS):
            span = slice(head * HEAD_WIDTH, (head + 1) * HEAD_WIDTH)
            turned[group, span] = buf[group, :, span].T
        write(group).start()

    @pl.loop(0, groups)
    def _(group):
        write(group).wait()


def pack_q(source, q, blocks, step, first_head, heads):
    width = heads * GROUP_WIDTH
    hbm = pl.BlockSpec(memory_space=pltpu.HBM)
    return pl.pallas_call(
        functools.partial(pack_q_kernel, blocks, step, first_head * GROUP_WIDTH),
        out_shape=jax.ShapeDtypeStruct((width, BALANCE_TOKENS), q.dtype),
        in_specs=[pl.BlockSpec(memory_space=pltpu.SMEM), hbm],
        out_specs=hbm,
        scratch_shapes=[
            pltpu.VMEM((heads, BALANCE_TOKENS, GROUP_WIDTH), q.dtype),
            pltpu.VMEM((heads, GROUP_WIDTH, BALANCE_TOKENS), q.dtype),
            pltpu.SemaphoreType.DMA((heads, 2)),
        ],
        compiler_params=pltpu.CompilerParams(vmem_limit_bytes=VMEM_LIMIT),
        cost_estimate=pl.CostEstimate(
            flops=0, bytes_accessed=4 * width * BALANCE_TOKENS, transcendentals=0
        ),
        name=f"pack_q_{step}_{first_head}",
    )(source, q)


def attend_kernel(blocks, steps, low, heads, *refs):
    count = len(steps)
    source_ref, doc_ref, *q_refs = refs[: 2 + count]
    windows = refs[2 + count : 2 + count + 3 * blocks]
    out_ref, q_buf, k_buf, v_buf, o_buf, s_buf, vt_buf, info, q_sem, kv_sem, o_sem = refs[-11:]
    tasks = count * heads
    dp, sp = position()

    def q_copy(task, which):
        rows = pl.ds(pl.multiple_of((task % heads) * GROUP_WIDTH, GROUP_WIDTH), GROUP_WIDTH)
        side = task % 2
        return pltpu.make_async_copy(q_refs[which].at[rows], q_buf.at[side], q_sem.at[side])

    def q_start(task):
        for which in range(count):

            @pl.when(task // heads == which)
            def _():
                q_copy(task, which).start()

    q_start(jnp.int32(0))

    origin = (sp - 2) * blocks
    lowest = jnp.int32(3 * blocks)
    highest = jnp.int32(0)
    for which, step in enumerate(steps):
        slot = landing_slot(source_ref, blocks, dp, sp, dp ^ step)
        block = sp * blocks + slot
        length = jnp.int32(1)
        for back in range(1, MOST_BLK):
            same = doc_ref[0, jnp.maximum(block - back, 0)] == doc_ref[0, block]
            length = length + ((block >= back) & same).astype(jnp.int32)
        half = (length + 1) // 2
        start = 2 * blocks + slot + 1 - 2 * half
        info[which, 0] = slot
        info[which, 1] = half
        info[which, 2] = start * BALANCE_TOKENS
        info[which, 3] = (length % 2) * BALANCE_TOKENS
        lowest = jnp.minimum(lowest, start)
        highest = jnp.maximum(highest, 2 * blocks + slot)

    kv_lanes = pl.ds(low * HEAD_WIDTH, heads * HEAD_WIDTH)

    def window_copies(number):
        column, step = sp - 2 + number // blocks, number % blocks
        known = jnp.maximum(column, 0)
        place = number // blocks * blocks + landing_slot(source_ref, blocks, dp, known, dp ^ step)
        wanted = (column >= 0) & (place >= lowest) & (place <= highest)
        rows = block_rows(place)
        return wanted, [
            pltpu.make_async_copy(
                windows[number].at[which, :, kv_lanes], buf.at[rows], kv_sem.at[number, which]
            )
            for which, buf in enumerate((k_buf, v_buf))
        ]

    for number in range(3 * blocks):
        wanted, copies = window_copies(number)

        @pl.when(wanted)
        def _():
            for copy in copies:
                copy.start()

    @pl.when(lowest + origin < 0)
    def _():
        rows = block_rows(lowest)
        k_buf[rows] = jnp.zeros((BALANCE_TOKENS, k_buf.shape[1]), k_buf.dtype)
        v_buf[rows] = jnp.zeros((BALANCE_TOKENS, v_buf.shape[1]), v_buf.dtype)

    for number in range(3 * blocks):
        wanted, copies = window_copies(number)

        @pl.when(wanted)
        def _():
            for copy in copies:
                copy.wait()

    pairs = GROUP_WIDTH // PAIR
    eights = PAIR // 8

    def one_task(chunks, side, head, start, skipped):
        lanes = pl.ds(pl.multiple_of(head * HEAD_WIDTH, HEAD_WIDTH), HEAD_WIDTH)
        span = pl.ds(pl.multiple_of(start, BALANCE_TOKENS), chunks * PAIR)
        tops = [None] * pairs
        row = lax.broadcasted_iota(jnp.int32, (PAIR, PAIR), 0)
        column = lax.broadcasted_iota(jnp.int32, (PAIR, PAIR), 1) & (BALANCE_TOKENS - 1)
        for pair in range(pairs):
            parts = [
                q_buf[side, pair * PAIR + member : pair * PAIR + member + HEAD_WIDTH]
                for member in range(0, PAIR, HEAD_WIDTH)
            ]
            whole = jnp.dot(
                k_buf[span, lanes],
                jnp.concatenate(parts, axis=1),
                preferred_element_type=jnp.float32,
            )
            for chunk in range(chunks):
                keys = slice(chunk * PAIR, (chunk + 1) * PAIR)
                held = whole[keys]
                allowed = None
                if chunk == chunks - 1:
                    allowed = row <= column + (PAIR - BALANCE_TOKENS)
                if chunk == 0:
                    real = row >= skipped
                    allowed = real if allowed is None else allowed & real
                if allowed is not None:
                    held = jnp.where(allowed, held, -1e30)
                s_buf[pair, keys] = held
                high = jnp.max(held.reshape(eights, 8, PAIR), axis=0)
                tops[pair] = high if chunk == 0 else jnp.maximum(tops[pair], high)
        for chunk in range(chunks):
            rows = pl.ds(pl.multiple_of(start + chunk * PAIR, BALANCE_TOKENS), PAIR)
            vt_buf[:, chunk * PAIR : (chunk + 1) * PAIR] = v_buf[rows, lanes].T
        shifts = [jnp.max(top, axis=0, keepdims=True) * EXP2_SCALE for top in tops]

        def mix(pair):
            total = summed = None
            for chunk in range(chunks):
                keys = slice(chunk * PAIR, (chunk + 1) * PAIR)
                weight = jnp.exp2(s_buf[pair, keys] * EXP2_SCALE - shifts[pair])
                added = jnp.sum(weight.reshape(eights, 8, PAIR), axis=0)
                mixed = jnp.dot(
                    vt_buf[:, keys],
                    weight.astype(jnp.bfloat16),
                    preferred_element_type=jnp.float32,
                )
                total = added if chunk == 0 else total + added
                summed = mixed if chunk == 0 else summed + mixed
            return summed, total

        def finish(pair, summed, total):
            scaled = summed * (1.0 / jnp.sum(total, axis=0, keepdims=True))
            for member in range(0, PAIR, HEAD_WIDTH):
                piece = scaled[:, member : member + HEAD_WIDTH].T.astype(o_buf.dtype)
                o_buf[side, :, pair * PAIR + member : pair * PAIR + member + HEAD_WIDTH] = piece

        waiting = None
        for pair in range(pairs):
            mixed = mix(pair)
            if waiting is not None:
                finish(pair - 1, *waiting)
            waiting = mixed
        finish(pairs - 1, *waiting)

    def o_copy(task):
        side = task % 2
        lanes = pl.ds(
            pl.multiple_of((low + task % heads) * GROUP_WIDTH, GROUP_WIDTH), GROUP_WIDTH
        )
        rows = block_rows(info[task // heads, 0])
        return pltpu.make_async_copy(o_buf.at[side], out_ref.at[rows, lanes], o_sem.at[side])

    @pl.loop(0, tasks)
    def _(task):
        @pl.when(task + 1 < tasks)
        def _():
            q_start(task + 1)

        q_copy(task, 0).wait()

        @pl.when(task >= 2)
        def _():
            o_copy(task - 2).wait()

        piece = task // heads
        half, start, skipped = info[piece, 1], info[piece, 2], info[piece, 3]
        for chunks in range(1, MOST_BLK * BALANCE_TOKENS // PAIR + 1):

            @pl.when(half == chunks)
            def _():
                one_task(chunks, task % 2, task % heads, start, skipped)

        o_copy(task).start()

    for task in range(max(tasks - 2, 0), tasks):
        o_copy(jnp.int32(task)).wait()


def attend(source, docs, pieces, windows, base, shape, blocks, steps, low, heads):
    hbm = pl.BlockSpec(memory_space=pltpu.HBM)
    smem = pl.BlockSpec(memory_space=pltpu.SMEM)
    operands = [source, docs, *pieces, *windows] + ([] if base is None else [base])
    reach = MOST_BLK * BALANCE_TOKENS
    held = 3 * blocks * BALANCE_TOKENS
    dtype = pieces[0].dtype
    return pl.pallas_call(
        functools.partial(attend_kernel, blocks, steps, low, heads),
        out_shape=jax.ShapeDtypeStruct(shape, dtype),
        in_specs=[smem, smem] + [hbm] * (len(operands) - 2),
        out_specs=hbm,
        scratch_shapes=[
            pltpu.VMEM((2, GROUP_WIDTH, BALANCE_TOKENS), dtype),
            pltpu.VMEM((held, heads * HEAD_WIDTH), dtype),
            pltpu.VMEM((held, heads * HEAD_WIDTH), dtype),
            pltpu.VMEM((2, BALANCE_TOKENS, GROUP_WIDTH), dtype),
            pltpu.VMEM((GROUP_WIDTH // PAIR, reach, PAIR), jnp.float32),
            pltpu.VMEM((HEAD_WIDTH, reach), dtype),
            pltpu.SMEM((len(steps), 4), jnp.int32),
            pltpu.SemaphoreType.DMA((2,)),
            pltpu.SemaphoreType.DMA((3 * blocks, 2)),
            pltpu.SemaphoreType.DMA((2,)),
        ],
        input_output_aliases={} if base is None else {len(operands) - 1: 0},
        compiler_params=pltpu.CompilerParams(vmem_limit_bytes=VMEM_LIMIT),
        cost_estimate=pl.CostEstimate(flops=0, bytes_accessed=2**10, transcendentals=0),
        name=f"attend_{steps[0]}_{low}",
    )(*operands)


def on_device(query_matrix, key_matrix, value_matrix, block_source, documents):
    dp_count = lax.axis_size("dp")
    sp_count = lax.axis_size("sp")
    sp = lax.axis_index("sp")
    tok_dev = query_matrix.shape[1]
    blocks = tok_dev // BALANCE_TOKENS
    assert blocks == dp_count == 4
    q = query_matrix.reshape(tok_dev, QUERY_HEADS * HEAD_WIDTH)
    k = key_matrix.reshape(tok_dev, KEY_VALUE_HEADS * HEAD_WIDTH)
    v = value_matrix.reshape(tok_dev, KEY_VALUE_HEADS * HEAD_WIDTH)

    def swap_dp(x, step):
        return lax.ppermute(x, "dp", [(i, i ^ step) for i in range(dp_count)])

    def ahead(x):
        return lax.ppermute(x, "sp", [(i, i + 2) for i in range(sp_count - 2)])

    def swap_core(mine, theirs):
        x = jnp.where(sp % 2 == 0, mine, theirs)
        return lax.ppermute(x, "sp", [(i, i ^ 1) for i in range(sp_count)])

    def pack(step, low, heads):
        return pack_q(block_source, q, blocks, step, low, heads)

    all_heads = KEY_VALUE_HEADS
    cut = 5 * KEY_VALUE_HEADS // 8
    kept = pack(0, 0, all_heads)
    near = [pack(1, 0, all_heads), pack(2, 0, all_heads)]
    far = [pack(3, 0, cut), pack(3, cut, all_heads - cut)]

    own = list(pack_kv(block_source, k, v, blocks))
    own[1:] = [swap_dp(own[step], step) for step in range(1, blocks)]
    two = [None] * blocks
    two[0] = ahead(own[0])
    near, own[1], own[2] = lax.optimization_barrier((near, own[1], own[2]))
    two[1], two[2] = ahead(own[1]), ahead(own[2])
    near, kept, own[3], two[0] = lax.optimization_barrier((near, kept, own[3], two[0]))
    two[3] = ahead(own[3])
    near = [swap_dp(x, step) for step, x in enumerate(near, 1)]
    far, two[2] = lax.optimization_barrier((far, two[2]))
    one = [swap_core(mine, theirs) for mine, theirs in zip(own, two)]
    far, one = lax.optimization_barrier((far, one))
    far = [swap_dp(x, 3) for x in far]
    windows = [*two, *one, *own]

    call = functools.partial(attend, block_source, documents, windows=windows, shape=q.shape)
    out = call([kept], base=None, blocks=blocks, steps=(0,), low=0, heads=all_heads)
    out = call(near, base=out, blocks=blocks, steps=(1, 2), low=0, heads=all_heads)
    out = call(far[:1], base=out, blocks=blocks, steps=(3,), low=0, heads=cut)
    out = call(far[1:], base=out, blocks=blocks, steps=(3,), low=cut, heads=all_heads - cut)
    return out.reshape(1, tok_dev, QUERY_HEADS * HEAD_WIDTH)


def solution(mesh):
    placed = (P("dp", "sp", None), P("dp", "sp", None), P("dp", "sp", None), P(), P("dp", None))
    return jax.shard_map(
        on_device, mesh=mesh, in_specs=placed, out_specs=P("dp", "sp", None), check_vma=False
    )
```

```python
import functools
import math

import jax
import jax.numpy as jnp
from jax import lax
from jax.experimental import pallas as pl
from jax.experimental.pallas import tpu as pltpu
from jax.sharding import PartitionSpec as P

QUERY_HEADS = 64
KEY_VALUE_HEADS = 8
HEAD_WIDTH = 128
BALANCE_TOKENS = 128
MOST_BLK = 8
GROUP_HEADS = QUERY_HEADS // KEY_VALUE_HEADS
GROUP_WIDTH = GROUP_HEADS * HEAD_WIDTH
PAIR = 256
EXP2_SCALE = math.log2(math.e) / math.sqrt(HEAD_WIDTH)
VMEM_LIMIT = 64 * 1024 * 1024


def position():
    return lax.axis_index("dp"), lax.axis_index("sp")


def leaving_slot(source_ref, blocks, dp, sp, other):
    slot = jnp.int32(0)
    for place in range(blocks):
        entry = source_ref[sp, other * blocks + place]
        slot = jnp.where(entry // blocks == dp, entry % blocks, slot)
    return slot


def landing_slot(source_ref, blocks, dp, sp, other):
    slot = jnp.int32(0)
    for place in range(blocks):
        entry = source_ref[sp, dp * blocks + place]
        slot = jnp.where(entry // blocks == other, place, slot)
    return slot


def block_rows(slot):
    return pl.ds(pl.multiple_of(slot * BALANCE_TOKENS, BALANCE_TOKENS), BALANCE_TOKENS)


def pack_kv_kernel(blocks, source_ref, k_ref, v_ref, *rest):
    outs, (buf, sem) = rest[:blocks], rest[blocks:]
    dp, sp = position()
    reads, writes = [], []
    for order, step in enumerate([*range(1, blocks), 0]):
        rows = block_rows(leaving_slot(source_ref, blocks, dp, sp, dp ^ step))
        for which, ref in enumerate((k_ref, v_ref)):
            place, number = buf.at[order, which], 2 * order + which
            reads.append(pltpu.make_async_copy(ref.at[rows], place, sem.at[number, 0]))
            writes.append(
                pltpu.make_async_copy(place, outs[step].at[which], sem.at[number, 1])
            )
    for copy in reads:
        copy.start()
    for read, write in zip(reads, writes):
        read.wait()
        write.start()
    for copy in writes:
        copy.wait()


def pack_kv(source, k, v, blocks):
    width = k.shape[1]
    hbm = pl.BlockSpec(memory_space=pltpu.HBM)
    return pl.pallas_call(
        functools.partial(pack_kv_kernel, blocks),
        out_shape=[jax.ShapeDtypeStruct((2, BALANCE_TOKENS, width), k.dtype)] * blocks,
        in_specs=[pl.BlockSpec(memory_space=pltpu.SMEM), hbm, hbm],
        out_specs=[hbm] * blocks,
        scratch_shapes=[
            pltpu.VMEM((blocks, 2, BALANCE_TOKENS, width), k.dtype),
            pltpu.SemaphoreType.DMA((2 * blocks, 2)),
        ],
        compiler_params=pltpu.CompilerParams(vmem_limit_bytes=VMEM_LIMIT),
        cost_estimate=pl.CostEstimate(flops=0, bytes_accessed=4 * 2**20, transcendentals=0),
        name="pack_kv",
    )(source, k, v)


def pack_q_kernel(blocks, step, first, source_ref, q_ref, out_ref, buf, turned, sem):
    dp, sp = position()
    rows = block_rows(leaving_slot(source_ref, blocks, dp, sp, dp ^ step))
    groups = buf.shape[0]

    def read(group):
        lanes = pl.ds(pl.multiple_of(first + group * GROUP_WIDTH, GROUP_WIDTH), GROUP_WIDTH)
        return pltpu.make_async_copy(q_ref.at[rows, lanes], buf.at[group], sem.at[group, 0])

    def write(group):
        span = pl.ds(pl.multiple_of(group * GROUP_WIDTH, GROUP_WIDTH), GROUP_WIDTH)
        return pltpu.make_async_copy(turned.at[group], out_ref.at[span], sem.at[group, 1])

    @pl.loop(0, groups)
    def _(group):
        read(group).start()

    @pl.loop(0, groups)
    def _(group):
        read(group).wait()
        for head in range(GROUP_HEADS):
            span = slice(head * HEAD_WIDTH, (head + 1) * HEAD_WIDTH)
            turned[group, span] = buf[group, :, span].T
        write(group).start()

    @pl.loop(0, groups)
    def _(group):
        write(group).wait()


def pack_q(source, q, blocks, step, first_head, heads):
    width = heads * GROUP_WIDTH
    hbm = pl.BlockSpec(memory_space=pltpu.HBM)
    return pl.pallas_call(
        functools.partial(pack_q_kernel, blocks, step, first_head * GROUP_WIDTH),
        out_shape=jax.ShapeDtypeStruct((width, BALANCE_TOKENS), q.dtype),
        in_specs=[pl.BlockSpec(memory_space=pltpu.SMEM), hbm],
        out_specs=hbm,
        scratch_shapes=[
            pltpu.VMEM((heads, BALANCE_TOKENS, GROUP_WIDTH), q.dtype),
            pltpu.VMEM((heads, GROUP_WIDTH, BALANCE_TOKENS), q.dtype),
            pltpu.SemaphoreType.DMA((heads, 2)),
        ],
        compiler_params=pltpu.CompilerParams(vmem_limit_bytes=VMEM_LIMIT),
        cost_estimate=pl.CostEstimate(
            flops=0, bytes_accessed=4 * width * BALANCE_TOKENS, transcendentals=0
        ),
        name=f"pack_q_{step}_{first_head}",
    )(source, q)


def attend_kernel(blocks, steps, low, heads, *refs):
    count = len(steps)
    source_ref, doc_ref, *q_refs = refs[: 2 + count]
    windows = refs[2 + count : 2 + count + 3 * blocks]
    out_ref, q_buf, k_buf, v_buf, o_buf, s_buf, vt_buf, info, q_sem, kv_sem, o_sem = refs[-11:]
    tasks = count * heads
    dp, sp = position()

    def q_copy(task, which):
        rows = pl.ds(pl.multiple_of((task % heads) * GROUP_WIDTH, GROUP_WIDTH), GROUP_WIDTH)
        side = task % 2
        return pltpu.make_async_copy(q_refs[which].at[rows], q_buf.at[side], q_sem.at[side])

    def q_start(task):
        for which in range(count):

            @pl.when(task // heads == which)
            def _():
                q_copy(task, which).start()

    q_start(jnp.int32(0))

    origin = (sp - 2) * blocks
    lowest = jnp.int32(3 * blocks)
    highest = jnp.int32(0)
    for which, step in enumerate(steps):
        slot = landing_slot(source_ref, blocks, dp, sp, dp ^ step)
        block = sp * blocks + slot
        length = jnp.int32(1)
        for back in range(1, MOST_BLK):
            same = doc_ref[0, jnp.maximum(block - back, 0)] == doc_ref[0, block]
            length = length + ((block >= back) & same).astype(jnp.int32)
        half = (length + 1) // 2
        start = 2 * blocks + slot + 1 - 2 * half
        info[which, 0] = slot
        info[which, 1] = half
        info[which, 2] = start * BALANCE_TOKENS
        info[which, 3] = (length % 2) * BALANCE_TOKENS
        lowest = jnp.minimum(lowest, start)
        highest = jnp.maximum(highest, 2 * blocks + slot)

    kv_lanes = pl.ds(low * HEAD_WIDTH, heads * HEAD_WIDTH)

    def window_copies(number):
        column, step = sp - 2 + number // blocks, number % blocks
        known = jnp.maximum(column, 0)
        place = number // blocks * blocks + landing_slot(source_ref, blocks, dp, known, dp ^ step)
        wanted = (column >= 0) & (place >= lowest) & (place <= highest)
        rows = block_rows(place)
        return wanted, [
            pltpu.make_async_copy(
                windows[number].at[which, :, kv_lanes], buf.at[rows], kv_sem.at[number, which]
            )
            for which, buf in enumerate((k_buf, v_buf))
        ]

    for number in range(3 * blocks):
        wanted, copies = window_copies(number)

        @pl.when(wanted)
        def _():
            for copy in copies:
                copy.start()

    @pl.when(lowest + origin < 0)
    def _():
        rows = block_rows(lowest)
        k_buf[rows] = jnp.zeros((BALANCE_TOKENS, k_buf.shape[1]), k_buf.dtype)
        v_buf[rows] = jnp.zeros((BALANCE_TOKENS, v_buf.shape[1]), v_buf.dtype)

    for number in range(3 * blocks):
        wanted, copies = window_copies(number)

        @pl.when(wanted)
        def _():
            for copy in copies:
                copy.wait()

    pairs = GROUP_WIDTH // PAIR
    eights = PAIR // 8
    tiles = BALANCE_TOKENS // 8

    def one_task(chunks, side, head, start, skipped):
        lanes = pl.ds(pl.multiple_of(head * HEAD_WIDTH, HEAD_WIDTH), HEAD_WIDTH)
        span = pl.ds(pl.multiple_of(start, BALANCE_TOKENS), chunks * PAIR)
        tops = [None] * pairs
        lower, upper = slice(0, BALANCE_TOKENS), slice(BALANCE_TOKENS, PAIR)
        row = lax.broadcasted_iota(jnp.int32, (BALANCE_TOKENS, PAIR), 0)
        column = lax.broadcasted_iota(jnp.int32, (BALANCE_TOKENS, PAIR), 1)
        allowed = row <= (column & (BALANCE_TOKENS - 1))
        for pair in range(pairs):
            parts = [
                q_buf[side, pair * PAIR + member : pair * PAIR + member + HEAD_WIDTH]
                for member in range(0, PAIR, HEAD_WIDTH)
            ]
            whole = jnp.dot(
                k_buf[span, lanes],
                jnp.concatenate(parts, axis=1),
                preferred_element_type=jnp.float32,
            )
            for chunk in range(chunks):
                for part in (lower, upper):
                    base = chunk * PAIR + part.start
                    keys = slice(base, base + BALANCE_TOKENS)
                    held = whole[keys]
                    if chunk == 0 and part is lower:
                        held = jnp.where(skipped > 0, -1e30, held)
                    if chunk == chunks - 1 and part is upper:
                        held = jnp.where(allowed, held, -1e30)
                    s_buf[pair, keys] = held
                    high = jnp.max(held.reshape(tiles, 8, PAIR), axis=0)
                    tops[pair] = high if base == 0 else jnp.maximum(tops[pair], high)
        for chunk in range(chunks):
            rows = pl.ds(pl.multiple_of(start + chunk * PAIR, BALANCE_TOKENS), PAIR)
            vt_buf[:, chunk * PAIR : (chunk + 1) * PAIR] = v_buf[rows, lanes].T
        shifts = [jnp.max(top, axis=0, keepdims=True) * EXP2_SCALE for top in tops]

        def mix(pair):
            total = summed = None
            for chunk in range(chunks):
                keys = slice(chunk * PAIR, (chunk + 1) * PAIR)
                weight = jnp.exp2(s_buf[pair, keys] * EXP2_SCALE - shifts[pair])
                added = jnp.sum(weight.reshape(eights, 8, PAIR), axis=0)
                mixed = jnp.dot(
                    vt_buf[:, keys],
                    weight.astype(jnp.bfloat16),
                    preferred_element_type=jnp.float32,
                )
                total = added if chunk == 0 else total + added
                summed = mixed if chunk == 0 else summed + mixed
            return summed, total

        def finish(pair, summed, total):
            scaled = summed * (1.0 / jnp.sum(total, axis=0, keepdims=True))
            scaled = scaled.astype(o_buf.dtype)
            for member in range(0, PAIR, HEAD_WIDTH):
                piece = scaled[:, member : member + HEAD_WIDTH].T
                o_buf[side, :, pair * PAIR + member : pair * PAIR + member + HEAD_WIDTH] = piece

        waiting = None
        for pair in range(pairs):
            mixed = mix(pair)
            if waiting is not None:
                finish(pair - 1, *waiting)
            waiting = mixed
        finish(pairs - 1, *waiting)

    def o_copy(task):
        side = task % 2
        lanes = pl.ds(
            pl.multiple_of((low + task % heads) * GROUP_WIDTH, GROUP_WIDTH), GROUP_WIDTH
        )
        rows = block_rows(info[task // heads, 0])
        return pltpu.make_async_copy(o_buf.at[side], out_ref.at[rows, lanes], o_sem.at[side])

    @pl.loop(0, tasks)
    def _(task):
        @pl.when(task + 1 < tasks)
        def _():
            q_start(task + 1)

        q_copy(task, 0).wait()

        @pl.when(task >= 2)
        def _():
            o_copy(task - 2).wait()

        piece = task // heads
        half, start, skipped = info[piece, 1], info[piece, 2], info[piece, 3]
        for chunks in range(1, MOST_BLK * BALANCE_TOKENS // PAIR + 1):

            @pl.when(half == chunks)
            def _():
                one_task(chunks, task % 2, task % heads, start, skipped)

        o_copy(task).start()

    for task in range(max(tasks - 2, 0), tasks):
        o_copy(jnp.int32(task)).wait()


def attend(source, docs, pieces, windows, base, shape, blocks, steps, low, heads):
    hbm = pl.BlockSpec(memory_space=pltpu.HBM)
    smem = pl.BlockSpec(memory_space=pltpu.SMEM)
    operands = [source, docs, *pieces, *windows] + ([] if base is None else [base])
    reach = MOST_BLK * BALANCE_TOKENS
    held = 3 * blocks * BALANCE_TOKENS
    dtype = pieces[0].dtype
    return pl.pallas_call(
        functools.partial(attend_kernel, blocks, steps, low, heads),
        out_shape=jax.ShapeDtypeStruct(shape, dtype),
        in_specs=[smem, smem] + [hbm] * (len(operands) - 2),
        out_specs=hbm,
        scratch_shapes=[
            pltpu.VMEM((2, GROUP_WIDTH, BALANCE_TOKENS), dtype),
            pltpu.VMEM((held, heads * HEAD_WIDTH), dtype),
            pltpu.VMEM((held, heads * HEAD_WIDTH), dtype),
            pltpu.VMEM((2, BALANCE_TOKENS, GROUP_WIDTH), dtype),
            pltpu.VMEM((GROUP_WIDTH // PAIR, reach, PAIR), jnp.float32),
            pltpu.VMEM((HEAD_WIDTH, reach), dtype),
            pltpu.SMEM((len(steps), 4), jnp.int32),
            pltpu.SemaphoreType.DMA((2,)),
            pltpu.SemaphoreType.DMA((3 * blocks, 2)),
            pltpu.SemaphoreType.DMA((2,)),
        ],
        input_output_aliases={} if base is None else {len(operands) - 1: 0},
        compiler_params=pltpu.CompilerParams(vmem_limit_bytes=VMEM_LIMIT),
        cost_estimate=pl.CostEstimate(flops=0, bytes_accessed=2**10, transcendentals=0),
        name=f"attend_{steps[0]}_{low}",
    )(*operands)


def on_device(query_matrix, key_matrix, value_matrix, block_source, documents):
    dp_count = lax.axis_size("dp")
    sp_count = lax.axis_size("sp")
    sp = lax.axis_index("sp")
    tok_dev = query_matrix.shape[1]
    blocks = tok_dev // BALANCE_TOKENS
    assert blocks == dp_count == 4
    q = query_matrix.reshape(tok_dev, QUERY_HEADS * HEAD_WIDTH)
    k = key_matrix.reshape(tok_dev, KEY_VALUE_HEADS * HEAD_WIDTH)
    v = value_matrix.reshape(tok_dev, KEY_VALUE_HEADS * HEAD_WIDTH)

    def swap_dp(x, step):
        return lax.ppermute(x, "dp", [(i, i ^ step) for i in range(dp_count)])

    def ahead(x):
        return lax.ppermute(x, "sp", [(i, i + 2) for i in range(sp_count - 2)])

    def swap_core(mine, theirs):
        x = jnp.where(sp % 2 == 0, mine, theirs)
        return lax.ppermute(x, "sp", [(i, i ^ 1) for i in range(sp_count)])

    def pack(source, step, low, heads):
        return pack_q(source, q, blocks, step, low, heads)

    tie = lax.optimization_barrier
    all_heads = KEY_VALUE_HEADS
    cut = 5 * KEY_VALUE_HEADS // 8
    own = list(pack_kv(block_source, k, v, blocks))
    own[1:] = [swap_dp(own[step], step) for step in range(1, blocks)]
    two = [None] * blocks
    two[0] = ahead(own[0])
    near = [pack(block_source, step, 0, all_heads) for step in (1, 2)]
    near, source, own[1] = tie((near, block_source, own[1]))
    two[1] = ahead(own[1])
    kept = pack(source, 0, 0, all_heads)
    far = [pack(source, 3, 0, cut), pack(source, 3, cut, all_heads - cut)]
    near, kept, far, own[2], own[3], two[0], two[1] = tie(
        (near, kept, far, own[2], own[3], two[0], two[1])
    )
    near = [swap_dp(x, step) for step, x in enumerate(near, 1)]
    two[2], two[3] = ahead(own[2]), ahead(own[3])
    one = [swap_core(mine, theirs) for mine, theirs in zip(own, two)]
    windows = [*two, *one, *own]

    call = functools.partial(attend, block_source, documents, windows=windows, shape=q.shape)
    out = call([kept], base=None, blocks=blocks, steps=(0,), low=0, heads=all_heads)
    far, near, out = tie((far, near, out))
    far = [swap_dp(x, 3) for x in far]
    out = call(near, base=out, blocks=blocks, steps=(1, 2), low=0, heads=all_heads)
    out = call(far[:1], base=out, blocks=blocks, steps=(3,), low=0, heads=cut)
    out = call(far[1:], base=out, blocks=blocks, steps=(3,), low=cut, heads=all_heads - cut)
    return out.reshape(1, tok_dev, QUERY_HEADS * HEAD_WIDTH)


def solution(mesh):
    placed = (P("dp", "sp", None), P("dp", "sp", None), P("dp", "sp", None), P(), P("dp", None))
    return jax.shard_map(
        on_device, mesh=mesh, in_specs=placed, out_specs=P("dp", "sp", None), check_vma=False
    )
```

```python
import functools
import math

import jax
import jax.numpy as jnp
from jax import lax
from jax.experimental import pallas as pl
from jax.experimental.pallas import tpu as pltpu
from jax.sharding import PartitionSpec as P

QUERY_HEADS = 64
KEY_VALUE_HEADS = 8
HEAD_WIDTH = 128
BALANCE_TOKENS = 128
MOST_BLK = 8
GROUP_HEADS = QUERY_HEADS // KEY_VALUE_HEADS
GROUP_WIDTH = GROUP_HEADS * HEAD_WIDTH
PAIR = 256
EXP2_SCALE = math.log2(math.e) / math.sqrt(HEAD_WIDTH)
VMEM_LIMIT = 64 * 1024 * 1024


def position():
    return lax.axis_index("dp"), lax.axis_index("sp")


def leaving_slot(source_ref, blocks, dp, sp, other):
    slot = jnp.int32(0)
    for place in range(blocks):
        entry = source_ref[sp, other * blocks + place]
        slot = jnp.where(entry // blocks == dp, entry % blocks, slot)
    return slot


def landing_slot(source_ref, blocks, dp, sp, other):
    slot = jnp.int32(0)
    for place in range(blocks):
        entry = source_ref[sp, dp * blocks + place]
        slot = jnp.where(entry // blocks == other, place, slot)
    return slot


def block_rows(slot):
    return pl.ds(pl.multiple_of(slot * BALANCE_TOKENS, BALANCE_TOKENS), BALANCE_TOKENS)


def pack_kv_kernel(blocks, source_ref, k_ref, v_ref, *rest):
    outs, (buf, sem) = rest[:blocks], rest[blocks:]
    dp, sp = position()
    reads, writes = [], []
    for order, step in enumerate([*range(1, blocks), 0]):
        rows = block_rows(leaving_slot(source_ref, blocks, dp, sp, dp ^ step))
        for which, ref in enumerate((k_ref, v_ref)):
            place, number = buf.at[order, which], 2 * order + which
            reads.append(pltpu.make_async_copy(ref.at[rows], place, sem.at[number, 0]))
            writes.append(
                pltpu.make_async_copy(place, outs[step].at[which], sem.at[number, 1])
            )
    for copy in reads:
        copy.start()
    for read, write in zip(reads, writes):
        read.wait()
        write.start()
    for copy in writes:
        copy.wait()


def pack_kv(source, k, v, blocks):
    width = k.shape[1]
    hbm = pl.BlockSpec(memory_space=pltpu.HBM)
    return pl.pallas_call(
        functools.partial(pack_kv_kernel, blocks),
        out_shape=[jax.ShapeDtypeStruct((2, BALANCE_TOKENS, width), k.dtype)] * blocks,
        in_specs=[pl.BlockSpec(memory_space=pltpu.SMEM), hbm, hbm],
        out_specs=[hbm] * blocks,
        scratch_shapes=[
            pltpu.VMEM((blocks, 2, BALANCE_TOKENS, width), k.dtype),
            pltpu.SemaphoreType.DMA((2 * blocks, 2)),
        ],
        compiler_params=pltpu.CompilerParams(vmem_limit_bytes=VMEM_LIMIT),
        cost_estimate=pl.CostEstimate(flops=0, bytes_accessed=4 * 2**20, transcendentals=0),
        name="pack_kv",
    )(source, k, v)


def pack_q_kernel(blocks, step, first, source_ref, q_ref, out_ref, buf, turned, sem):
    dp, sp = position()
    rows = block_rows(leaving_slot(source_ref, blocks, dp, sp, dp ^ step))
    groups = buf.shape[0]

    def read(group):
        lanes = pl.ds(pl.multiple_of(first + group * GROUP_WIDTH, GROUP_WIDTH), GROUP_WIDTH)
        return pltpu.make_async_copy(q_ref.at[rows, lanes], buf.at[group], sem.at[group, 0])

    def write(group):
        span = pl.ds(pl.multiple_of(group * GROUP_WIDTH, GROUP_WIDTH), GROUP_WIDTH)
        return pltpu.make_async_copy(turned.at[group], out_ref.at[span], sem.at[group, 1])

    @pl.loop(0, groups)
    def _(group):
        read(group).start()

    @pl.loop(0, groups)
    def _(group):
        read(group).wait()
        for head in range(GROUP_HEADS):
            span = slice(head * HEAD_WIDTH, (head + 1) * HEAD_WIDTH)
            turned[group, span] = buf[group, :, span].T
        write(group).start()

    @pl.loop(0, groups)
    def _(group):
        write(group).wait()


def pack_q(source, q, blocks, step, first_head, heads):
    width = heads * GROUP_WIDTH
    hbm = pl.BlockSpec(memory_space=pltpu.HBM)
    return pl.pallas_call(
        functools.partial(pack_q_kernel, blocks, step, first_head * GROUP_WIDTH),
        out_shape=jax.ShapeDtypeStruct((width, BALANCE_TOKENS), q.dtype),
        in_specs=[pl.BlockSpec(memory_space=pltpu.SMEM), hbm],
        out_specs=hbm,
        scratch_shapes=[
            pltpu.VMEM((heads, BALANCE_TOKENS, GROUP_WIDTH), q.dtype),
            pltpu.VMEM((heads, GROUP_WIDTH, BALANCE_TOKENS), q.dtype),
            pltpu.SemaphoreType.DMA((heads, 2)),
        ],
        compiler_params=pltpu.CompilerParams(vmem_limit_bytes=VMEM_LIMIT),
        cost_estimate=pl.CostEstimate(
            flops=0, bytes_accessed=4 * width * BALANCE_TOKENS, transcendentals=0
        ),
        name=f"pack_q_{step}_{first_head}",
    )(source, q)


def attend_kernel(blocks, steps, low, heads, *refs):
    count = len(steps)
    source_ref, doc_ref, *q_refs = refs[: 2 + count]
    windows = refs[2 + count : 2 + count + 3 * blocks]
    out_ref, q_buf, k_buf, v_buf, o_buf, s_buf, vt_buf, info, q_sem, kv_sem, o_sem = refs[-11:]
    tasks = count * heads
    dp, sp = position()

    def q_copy(task, which):
        rows = pl.ds(pl.multiple_of((task % heads) * GROUP_WIDTH, GROUP_WIDTH), GROUP_WIDTH)
        side = task % 2
        return pltpu.make_async_copy(q_refs[which].at[rows], q_buf.at[side], q_sem.at[side])

    def q_start(task):
        for which in range(count):

            @pl.when(task // heads == which)
            def _():
                q_copy(task, which).start()

    q_start(jnp.int32(0))

    origin = (sp - 2) * blocks
    lowest = jnp.int32(3 * blocks)
    highest = jnp.int32(0)
    for which, step in enumerate(steps):
        slot = landing_slot(source_ref, blocks, dp, sp, dp ^ step)
        block = sp * blocks + slot
        length = jnp.int32(1)
        for back in range(1, MOST_BLK):
            same = doc_ref[0, jnp.maximum(block - back, 0)] == doc_ref[0, block]
            length = length + ((block >= back) & same).astype(jnp.int32)
        half = (length + 1) // 2
        start = 2 * blocks + slot + 1 - 2 * half
        info[which, 0] = slot
        info[which, 1] = half
        info[which, 2] = start * BALANCE_TOKENS
        info[which, 3] = (length % 2) * BALANCE_TOKENS
        lowest = jnp.minimum(lowest, start)
        highest = jnp.maximum(highest, 2 * blocks + slot)

    kv_lanes = pl.ds(low * HEAD_WIDTH, heads * HEAD_WIDTH)

    def window_copies(number):
        column, step = sp - 2 + number // blocks, number % blocks
        known = jnp.maximum(column, 0)
        place = number // blocks * blocks + landing_slot(source_ref, blocks, dp, known, dp ^ step)
        wanted = (column >= 0) & (place >= lowest) & (place <= highest)
        rows = block_rows(place)
        return wanted, [
            pltpu.make_async_copy(
                windows[number].at[which, :, kv_lanes], buf.at[rows], kv_sem.at[number, which]
            )
            for which, buf in enumerate((k_buf, v_buf))
        ]

    fetches = [window_copies(number) for number in range(3 * blocks)]
    for wanted, copies in fetches:

        @pl.when(wanted)
        def _():
            for copy in copies:
                copy.start()

    @pl.when(lowest + origin < 0)
    def _():
        rows = block_rows(lowest)
        k_buf[rows] = jnp.zeros((BALANCE_TOKENS, k_buf.shape[1]), k_buf.dtype)
        v_buf[rows] = jnp.zeros((BALANCE_TOKENS, v_buf.shape[1]), v_buf.dtype)

    for wanted, copies in fetches:

        @pl.when(wanted)
        def _():
            for copy in copies:
                copy.wait()

    pairs = GROUP_WIDTH // PAIR
    eights = PAIR // 8
    tiles = BALANCE_TOKENS // 8

    def one_task(chunks, side, head, start, skipped):
        lanes = pl.ds(pl.multiple_of(head * HEAD_WIDTH, HEAD_WIDTH), HEAD_WIDTH)
        span = pl.ds(pl.multiple_of(start, BALANCE_TOKENS), chunks * PAIR)
        tops = [None] * pairs
        lower, upper = slice(0, BALANCE_TOKENS), slice(BALANCE_TOKENS, PAIR)
        row = lax.broadcasted_iota(jnp.int32, (BALANCE_TOKENS, PAIR), 0)
        column = lax.broadcasted_iota(jnp.int32, (BALANCE_TOKENS, PAIR), 1)
        allowed = row <= (column & (BALANCE_TOKENS - 1))
        for pair in range(pairs):
            parts = [
                q_buf[side, pair * PAIR + member : pair * PAIR + member + HEAD_WIDTH]
                for member in range(0, PAIR, HEAD_WIDTH)
            ]
            whole = jnp.dot(
                k_buf[span, lanes],
                jnp.concatenate(parts, axis=1),
                preferred_element_type=jnp.float32,
            )
            for chunk in range(chunks):
                for part in (lower, upper):
                    base = chunk * PAIR + part.start
                    keys = slice(base, base + BALANCE_TOKENS)
                    held = whole[keys]
                    if chunk == 0 and part is lower:
                        held = jnp.where(skipped > 0, -1e30, held)
                    if chunk == chunks - 1 and part is upper:
                        held = jnp.where(allowed, held, -1e30)
                    s_buf[pair, keys] = held
                    high = jnp.max(held.reshape(tiles, 8, PAIR), axis=0)
                    tops[pair] = high if base == 0 else jnp.maximum(tops[pair], high)
        for chunk in range(chunks):
            rows = pl.ds(pl.multiple_of(start + chunk * PAIR, BALANCE_TOKENS), PAIR)
            vt_buf[:, chunk * PAIR : (chunk + 1) * PAIR] = v_buf[rows, lanes].T
        shifts = [jnp.max(top, axis=0, keepdims=True) * EXP2_SCALE for top in tops]

        def mix(pair):
            total = summed = None
            for chunk in range(chunks):
                keys = slice(chunk * PAIR, (chunk + 1) * PAIR)
                weight = jnp.exp2(s_buf[pair, keys] * EXP2_SCALE - shifts[pair])
                added = jnp.sum(weight.reshape(eights, 8, PAIR), axis=0)
                mixed = jnp.dot(
                    vt_buf[:, keys],
                    weight.astype(jnp.bfloat16),
                    preferred_element_type=jnp.float32,
                )
                total = added if chunk == 0 else total + added
                summed = mixed if chunk == 0 else summed + mixed
            return summed, total

        def finish(pair, summed, total):
            scaled = summed * (1.0 / jnp.sum(total, axis=0, keepdims=True))
            scaled = scaled.astype(o_buf.dtype)
            for member in range(0, PAIR, HEAD_WIDTH):
                piece = scaled[:, member : member + HEAD_WIDTH].T
                o_buf[side, :, pair * PAIR + member : pair * PAIR + member + HEAD_WIDTH] = piece

        waiting = None
        for pair in range(pairs):
            mixed = mix(pair)
            if waiting is not None:
                finish(pair - 1, *waiting)
            waiting = mixed
        finish(pairs - 1, *waiting)

    def o_copy(task):
        side = task % 2
        lanes = pl.ds(
            pl.multiple_of((low + task % heads) * GROUP_WIDTH, GROUP_WIDTH), GROUP_WIDTH
        )
        rows = block_rows(info[task // heads, 0])
        return pltpu.make_async_copy(o_buf.at[side], out_ref.at[rows, lanes], o_sem.at[side])

    @pl.loop(0, tasks)
    def _(task):
        @pl.when(task + 1 < tasks)
        def _():
            q_start(task + 1)

        q_copy(task, 0).wait()

        @pl.when(task >= 2)
        def _():
            o_copy(task - 2).wait()

        piece = task // heads
        half, start, skipped = info[piece, 1], info[piece, 2], info[piece, 3]
        for chunks in range(1, MOST_BLK * BALANCE_TOKENS // PAIR + 1):

            @pl.when(half == chunks)
            def _():
                one_task(chunks, task % 2, task % heads, start, skipped)

        o_copy(task).start()

    for task in range(max(tasks - 2, 0), tasks):
        o_copy(jnp.int32(task)).wait()


def attend(source, docs, pieces, windows, base, shape, blocks, steps, low, heads):
    hbm = pl.BlockSpec(memory_space=pltpu.HBM)
    smem = pl.BlockSpec(memory_space=pltpu.SMEM)
    operands = [source, docs, *pieces, *windows] + ([] if base is None else [base])
    reach = MOST_BLK * BALANCE_TOKENS
    held = 3 * blocks * BALANCE_TOKENS
    dtype = pieces[0].dtype
    return pl.pallas_call(
        functools.partial(attend_kernel, blocks, steps, low, heads),
        out_shape=jax.ShapeDtypeStruct(shape, dtype),
        in_specs=[smem, smem] + [hbm] * (len(operands) - 2),
        out_specs=hbm,
        scratch_shapes=[
            pltpu.VMEM((2, GROUP_WIDTH, BALANCE_TOKENS), dtype),
            pltpu.VMEM((held, heads * HEAD_WIDTH), dtype),
            pltpu.VMEM((held, heads * HEAD_WIDTH), dtype),
            pltpu.VMEM((2, BALANCE_TOKENS, GROUP_WIDTH), dtype),
            pltpu.VMEM((GROUP_WIDTH // PAIR, reach, PAIR), jnp.float32),
            pltpu.VMEM((HEAD_WIDTH, reach), dtype),
            pltpu.SMEM((len(steps), 4), jnp.int32),
            pltpu.SemaphoreType.DMA((2,)),
            pltpu.SemaphoreType.DMA((3 * blocks, 2)),
            pltpu.SemaphoreType.DMA((2,)),
        ],
        input_output_aliases={} if base is None else {len(operands) - 1: 0},
        compiler_params=pltpu.CompilerParams(vmem_limit_bytes=VMEM_LIMIT),
        cost_estimate=pl.CostEstimate(flops=0, bytes_accessed=2**10, transcendentals=0),
        name=f"attend_{steps[0]}_{low}",
    )(*operands)


def on_device(query_matrix, key_matrix, value_matrix, block_source, documents):
    dp_count = lax.axis_size("dp")
    sp_count = lax.axis_size("sp")
    sp = lax.axis_index("sp")
    tok_dev = query_matrix.shape[1]
    blocks = tok_dev // BALANCE_TOKENS
    assert blocks == dp_count == 4
    q = query_matrix.reshape(tok_dev, QUERY_HEADS * HEAD_WIDTH)
    k = key_matrix.reshape(tok_dev, KEY_VALUE_HEADS * HEAD_WIDTH)
    v = value_matrix.reshape(tok_dev, KEY_VALUE_HEADS * HEAD_WIDTH)

    def swap_dp(x, step):
        return lax.ppermute(x, "dp", [(i, i ^ step) for i in range(dp_count)])

    def ahead(x):
        return lax.ppermute(x, "sp", [(i, i + 2) for i in range(sp_count - 2)])

    def swap_core(mine, theirs):
        x = jnp.where(sp % 2 == 0, mine, theirs)
        return lax.ppermute(x, "sp", [(i, i ^ 1) for i in range(sp_count)])

    def pack(source, step, low, heads):
        return pack_q(source, q, blocks, step, low, heads)

    tie = lax.optimization_barrier
    all_heads = KEY_VALUE_HEADS
    cut = 6 * KEY_VALUE_HEADS // 8
    own = list(pack_kv(block_source, k, v, blocks))
    two = [None] * blocks
    own[1], own[2] = swap_dp(own[1], 1), swap_dp(own[2], 2)
    two[0] = ahead(own[0])
    near = [pack(block_source, step, 0, all_heads) for step in (1, 2)]
    near, source, *own[1:] = tie((near, block_source, *own[1:]))
    own[3] = swap_dp(own[3], 3)
    two[1], two[2] = ahead(own[1]), ahead(own[2])
    kept = pack(source, 0, 0, all_heads)
    far = [pack(source, 3, 0, cut), pack(source, 3, cut, all_heads - cut)]
    near, kept, far, own[3], two[0] = tie((near, kept, far, own[3], two[0]))
    near = [swap_dp(x, step) for step, x in enumerate(near, 1)]
    two[3] = ahead(own[3])
    one = [swap_core(mine, theirs) for mine, theirs in zip(own, two)]
    windows = [*two, *one, *own]

    call = functools.partial(attend, block_source, documents, windows=windows, shape=q.shape)
    out = call([kept], base=None, blocks=blocks, steps=(0,), low=0, heads=all_heads)
    far, near, out = tie((far, near, out))
    far = [swap_dp(x, 3) for x in far]
    out = call(near, base=out, blocks=blocks, steps=(1, 2), low=0, heads=all_heads)
    out = call(far[:1], base=out, blocks=blocks, steps=(3,), low=0, heads=cut)
    out = call(far[1:], base=out, blocks=blocks, steps=(3,), low=cut, heads=all_heads - cut)
    return out.reshape(1, tok_dev, QUERY_HEADS * HEAD_WIDTH)


def solution(mesh):
    placed = (P("dp", "sp", None), P("dp", "sp", None), P("dp", "sp", None), P(), P("dp", None))
    return jax.shard_map(
        on_device, mesh=mesh, in_specs=placed, out_specs=P("dp", "sp", None), check_vma=False
    )
```

```python
import functools
import math

import jax
import jax.numpy as jnp
from jax import lax
from jax.experimental import pallas as pl
from jax.experimental.pallas import tpu as pltpu
from jax.sharding import PartitionSpec as P

QUERY_HEADS = 64
KEY_VALUE_HEADS = 8
HEAD_WIDTH = 128
BALANCE_TOKENS = 128
MOST_BLK = 8
GROUP_HEADS = QUERY_HEADS // KEY_VALUE_HEADS
GROUP_WIDTH = GROUP_HEADS * HEAD_WIDTH
PAIR = 256
EXP2_SCALE = math.log2(math.e) / math.sqrt(HEAD_WIDTH)
WINDOW_OF = (
    ((0, 0), (1, 0), (1, 1), (2, 0)),
    ((3, 0), (4, 0), (4, 1), (4, 2)),
    ((5, 0), (6, 0), (6, 1), (7, 0)),
)
WINDOWS = 8
VMEM_LIMIT = 64 * 1024 * 1024


def position():
    return lax.axis_index("dp"), lax.axis_index("sp")


def leaving_slot(source_ref, blocks, dp, sp, other):
    slot = jnp.int32(0)
    for place in range(blocks):
        entry = source_ref[sp, other * blocks + place]
        slot = jnp.where(entry // blocks == dp, entry % blocks, slot)
    return slot


def landing_slot(source_ref, blocks, dp, sp, other):
    slot = jnp.int32(0)
    for place in range(blocks):
        entry = source_ref[sp, dp * blocks + place]
        slot = jnp.where(entry // blocks == other, place, slot)
    return slot


def block_rows(slot):
    return pl.ds(pl.multiple_of(slot * BALANCE_TOKENS, BALANCE_TOKENS), BALANCE_TOKENS)


def pack_kv_kernel(blocks, source_ref, k_ref, v_ref, *rest):
    outs, (buf, sem) = rest[:blocks], rest[blocks:]
    dp, sp = position()
    reads, writes = [], []
    for order, step in enumerate([*range(1, blocks), 0]):
        rows = block_rows(leaving_slot(source_ref, blocks, dp, sp, dp ^ step))
        for which, ref in enumerate((k_ref, v_ref)):
            place, number = buf.at[order, which], 2 * order + which
            reads.append(pltpu.make_async_copy(ref.at[rows], place, sem.at[number, 0]))
            writes.append(
                pltpu.make_async_copy(place, outs[step].at[which], sem.at[number, 1])
            )
    for copy in reads:
        copy.start()
    for read, write in zip(reads, writes):
        read.wait()
        write.start()
    for copy in writes:
        copy.wait()


def pack_kv(source, k, v, blocks):
    width = k.shape[1]
    hbm = pl.BlockSpec(memory_space=pltpu.HBM)
    return pl.pallas_call(
        functools.partial(pack_kv_kernel, blocks),
        out_shape=[jax.ShapeDtypeStruct((2, BALANCE_TOKENS, width), k.dtype)] * blocks,
        in_specs=[pl.BlockSpec(memory_space=pltpu.SMEM), hbm, hbm],
        out_specs=[hbm] * blocks,
        scratch_shapes=[
            pltpu.VMEM((blocks, 2, BALANCE_TOKENS, width), k.dtype),
            pltpu.SemaphoreType.DMA((2 * blocks, 2)),
        ],
        compiler_params=pltpu.CompilerParams(vmem_limit_bytes=VMEM_LIMIT),
        cost_estimate=pl.CostEstimate(flops=0, bytes_accessed=4 * 2**20, transcendentals=0),
        name="pack_kv",
    )(source, k, v)


def pack_q_kernel(blocks, step, first, source_ref, q_ref, out_ref, buf, turned, sem):
    dp, sp = position()
    rows = block_rows(leaving_slot(source_ref, blocks, dp, sp, dp ^ step))
    groups = buf.shape[0]

    def read(group):
        lanes = pl.ds(pl.multiple_of(first + group * GROUP_WIDTH, GROUP_WIDTH), GROUP_WIDTH)
        return pltpu.make_async_copy(q_ref.at[rows, lanes], buf.at[group], sem.at[group, 0])

    def write(group):
        span = pl.ds(pl.multiple_of(group * GROUP_WIDTH, GROUP_WIDTH), GROUP_WIDTH)
        return pltpu.make_async_copy(turned.at[group], out_ref.at[span], sem.at[group, 1])

    @pl.loop(0, groups)
    def _(group):
        read(group).start()

    @pl.loop(0, groups)
    def _(group):
        read(group).wait()
        for head in range(GROUP_HEADS):
            span = slice(head * HEAD_WIDTH, (head + 1) * HEAD_WIDTH)
            turned[group, span] = buf[group, :, span].T
        write(group).start()

    @pl.loop(0, groups)
    def _(group):
        write(group).wait()


def pack_q(source, q, blocks, step, first_head, heads):
    width = heads * GROUP_WIDTH
    hbm = pl.BlockSpec(memory_space=pltpu.HBM)
    return pl.pallas_call(
        functools.partial(pack_q_kernel, blocks, step, first_head * GROUP_WIDTH),
        out_shape=jax.ShapeDtypeStruct((width, BALANCE_TOKENS), q.dtype),
        in_specs=[pl.BlockSpec(memory_space=pltpu.SMEM), hbm],
        out_specs=hbm,
        scratch_shapes=[
            pltpu.VMEM((heads, BALANCE_TOKENS, GROUP_WIDTH), q.dtype),
            pltpu.VMEM((heads, GROUP_WIDTH, BALANCE_TOKENS), q.dtype),
            pltpu.SemaphoreType.DMA((heads, 2)),
        ],
        compiler_params=pltpu.CompilerParams(vmem_limit_bytes=VMEM_LIMIT),
        cost_estimate=pl.CostEstimate(
            flops=0, bytes_accessed=4 * width * BALANCE_TOKENS, transcendentals=0
        ),
        name=f"pack_q_{step}_{first_head}",
    )(source, q)


def attend_kernel(blocks, steps, low, heads, *refs):
    count = len(steps)
    source_ref, doc_ref, *q_refs = refs[: 2 + count]
    windows = refs[2 + count : 2 + count + WINDOWS]
    out_ref, q_buf, k_buf, v_buf, o_buf, s_buf, vt_buf, info, q_sem, kv_sem, o_sem = refs[-11:]
    tasks = count * heads
    dp, sp = position()

    def q_copy(task, which):
        rows = pl.ds(pl.multiple_of((task % heads) * GROUP_WIDTH, GROUP_WIDTH), GROUP_WIDTH)
        side = task % 2
        return pltpu.make_async_copy(q_refs[which].at[rows], q_buf.at[side], q_sem.at[side])

    def q_start(task):
        for which in range(count):

            @pl.when(task // heads == which)
            def _():
                q_copy(task, which).start()

    q_start(jnp.int32(0))

    origin = (sp - 2) * blocks
    lowest = jnp.int32(3 * blocks)
    highest = jnp.int32(0)
    for which, step in enumerate(steps):
        slot = landing_slot(source_ref, blocks, dp, sp, dp ^ step)
        block = sp * blocks + slot
        length = jnp.int32(1)
        for back in range(1, MOST_BLK):
            same = doc_ref[0, jnp.maximum(block - back, 0)] == doc_ref[0, block]
            length = length + ((block >= back) & same).astype(jnp.int32)
        half = (length + 1) // 2
        start = 2 * blocks + slot + 1 - 2 * half
        info[which, 0] = slot
        info[which, 1] = half
        info[which, 2] = start * BALANCE_TOKENS
        info[which, 3] = (length % 2) * BALANCE_TOKENS
        lowest = jnp.minimum(lowest, start)
        highest = jnp.maximum(highest, 2 * blocks + slot)

    kv_lanes = pl.ds(low * HEAD_WIDTH, heads * HEAD_WIDTH)

    def window_copies(number):
        column, step = sp - 2 + number // blocks, number % blocks
        known = jnp.maximum(column, 0)
        place = number // blocks * blocks + landing_slot(source_ref, blocks, dp, known, dp ^ step)
        wanted = (column >= 0) & (place >= lowest) & (place <= highest)
        rows = block_rows(place)
        index, inner = WINDOW_OF[number // blocks][step]
        return wanted, [
            pltpu.make_async_copy(
                windows[index].at[inner, which, :, kv_lanes],
                buf.at[rows],
                kv_sem.at[number, which],
            )
            for which, buf in enumerate((k_buf, v_buf))
        ]

    fetches = [window_copies(number) for number in range(3 * blocks)]
    for wanted, copies in fetches:

        @pl.when(wanted)
        def _():
            for copy in copies:
                copy.start()

    @pl.when(lowest + origin < 0)
    def _():
        rows = block_rows(lowest)
        k_buf[rows] = jnp.zeros((BALANCE_TOKENS, k_buf.shape[1]), k_buf.dtype)
        v_buf[rows] = jnp.zeros((BALANCE_TOKENS, v_buf.shape[1]), v_buf.dtype)

    for wanted, copies in fetches:

        @pl.when(wanted)
        def _():
            for copy in copies:
                copy.wait()

    pairs = GROUP_WIDTH // PAIR
    eights = PAIR // 8
    tiles = BALANCE_TOKENS // 8

    def one_task(chunks, side, head, start, skipped):
        lanes = pl.ds(pl.multiple_of(head * HEAD_WIDTH, HEAD_WIDTH), HEAD_WIDTH)
        span = pl.ds(pl.multiple_of(start, BALANCE_TOKENS), chunks * PAIR)
        lower, upper = slice(0, BALANCE_TOKENS), slice(BALANCE_TOKENS, PAIR)
        row = lax.broadcasted_iota(jnp.int32, (BALANCE_TOKENS, PAIR), 0)
        column = lax.broadcasted_iota(jnp.int32, (BALANCE_TOKENS, PAIR), 1)
        allowed = row <= (column & (BALANCE_TOKENS - 1))
        tops = [None] * pairs
        totals = [None] * pairs
        sums = [None] * pairs
        shifts = [None] * pairs

        def rows_of(chunk):
            return pl.ds(pl.multiple_of(start + chunk * PAIR, BALANCE_TOKENS), PAIR)

        def score(pair, chunk):
            parts = [
                q_buf[side, pair * PAIR + member : pair * PAIR + member + HEAD_WIDTH]
                for member in range(0, PAIR, HEAD_WIDTH)
            ]
            whole = jnp.dot(
                k_buf[rows_of(chunk), lanes],
                jnp.concatenate(parts, axis=1),
                preferred_element_type=jnp.float32,
            )
            for part in (lower, upper):
                base = chunk * PAIR + part.start
                held = whole[part]
                if chunk == 0 and part is lower:
                    held = jnp.where(skipped > 0, -1e30, held)
                if chunk == chunks - 1 and part is upper:
                    held = jnp.where(allowed, held, -1e30)
                s_buf[pair, base : base + BALANCE_TOKENS] = held
                high = jnp.max(held.reshape(tiles, 8, PAIR), axis=0)
                tops[pair] = high if base == 0 else jnp.maximum(tops[pair], high)

        def settle(pair):
            shifts[pair] = jnp.max(tops[pair], axis=0, keepdims=True) * EXP2_SCALE

        def mix(pair, chunk):
            keys = slice(chunk * PAIR, (chunk + 1) * PAIR)
            weight = jnp.exp2(s_buf[pair, keys] * EXP2_SCALE - shifts[pair])
            added = jnp.sum(weight.reshape(eights, 8, PAIR), axis=0)
            mixed = jnp.dot(
                vt_buf[:, keys],
                weight.astype(jnp.bfloat16),
                preferred_element_type=jnp.float32,
            )
            totals[pair] = added if chunk == 0 else totals[pair] + added
            sums[pair] = mixed if chunk == 0 else sums[pair] + mixed

        def finish(pair):
            scaled = sums[pair] * (1.0 / jnp.sum(totals[pair], axis=0, keepdims=True))
            scaled = scaled.astype(o_buf.dtype)
            for member in range(0, PAIR, HEAD_WIDTH):
                piece = scaled[:, member : member + HEAD_WIDTH].T
                o_buf[side, :, pair * PAIR + member : pair * PAIR + member + HEAD_WIDTH] = piece

        for chunk in range(chunks):
            score(0, chunk)
            vt_buf[:, chunk * PAIR : (chunk + 1) * PAIR] = v_buf[rows_of(chunk), lanes].T
        for pair in range(pairs):
            settle(pair)
            for chunk in range(chunks):
                if pair + 1 < pairs:
                    score(pair + 1, chunk)
                mix(pair, chunk)
            if pair:
                finish(pair - 1)
        finish(pairs - 1)

    def o_copy(task):
        side = task % 2
        lanes = pl.ds(
            pl.multiple_of((low + task % heads) * GROUP_WIDTH, GROUP_WIDTH), GROUP_WIDTH
        )
        rows = block_rows(info[task // heads, 0])
        return pltpu.make_async_copy(o_buf.at[side], out_ref.at[rows, lanes], o_sem.at[side])

    @pl.loop(0, tasks)
    def _(task):
        @pl.when(task + 1 < tasks)
        def _():
            q_start(task + 1)

        q_copy(task, 0).wait()

        @pl.when(task >= 2)
        def _():
            o_copy(task - 2).wait()

        piece = task // heads
        half, start, skipped = info[piece, 1], info[piece, 2], info[piece, 3]
        for chunks in range(1, MOST_BLK * BALANCE_TOKENS // PAIR + 1):

            @pl.when(half == chunks)
            def _():
                one_task(chunks, task % 2, task % heads, start, skipped)

        o_copy(task).start()

    for task in range(max(tasks - 2, 0), tasks):
        o_copy(jnp.int32(task)).wait()


def attend(source, docs, pieces, windows, base, shape, blocks, steps, low, heads):
    hbm = pl.BlockSpec(memory_space=pltpu.HBM)
    smem = pl.BlockSpec(memory_space=pltpu.SMEM)
    operands = [source, docs, *pieces, *windows] + ([] if base is None else [base])
    reach = MOST_BLK * BALANCE_TOKENS
    held = 3 * blocks * BALANCE_TOKENS
    dtype = pieces[0].dtype
    return pl.pallas_call(
        functools.partial(attend_kernel, blocks, steps, low, heads),
        out_shape=jax.ShapeDtypeStruct(shape, dtype),
        in_specs=[smem, smem] + [hbm] * (len(operands) - 2),
        out_specs=hbm,
        scratch_shapes=[
            pltpu.VMEM((2, GROUP_WIDTH, BALANCE_TOKENS), dtype),
            pltpu.VMEM((held, heads * HEAD_WIDTH), dtype),
            pltpu.VMEM((held, heads * HEAD_WIDTH), dtype),
            pltpu.VMEM((2, BALANCE_TOKENS, GROUP_WIDTH), dtype),
            pltpu.VMEM((GROUP_WIDTH // PAIR, reach, PAIR), jnp.float32),
            pltpu.VMEM((HEAD_WIDTH, reach), dtype),
            pltpu.SMEM((len(steps), 4), jnp.int32),
            pltpu.SemaphoreType.DMA((2,)),
            pltpu.SemaphoreType.DMA((3 * blocks, 2)),
            pltpu.SemaphoreType.DMA((2,)),
        ],
        input_output_aliases={} if base is None else {len(operands) - 1: 0},
        compiler_params=pltpu.CompilerParams(vmem_limit_bytes=VMEM_LIMIT),
        cost_estimate=pl.CostEstimate(flops=0, bytes_accessed=2**10, transcendentals=0),
        name=f"attend_{steps[0]}_{low}",
    )(*operands)


def on_device(query_matrix, key_matrix, value_matrix, block_source, documents):
    dp_count = lax.axis_size("dp")
    sp_count = lax.axis_size("sp")
    sp = lax.axis_index("sp")
    tok_dev = query_matrix.shape[1]
    blocks = tok_dev // BALANCE_TOKENS
    assert blocks == dp_count == 4
    q = query_matrix.reshape(tok_dev, QUERY_HEADS * HEAD_WIDTH)
    k = key_matrix.reshape(tok_dev, KEY_VALUE_HEADS * HEAD_WIDTH)
    v = value_matrix.reshape(tok_dev, KEY_VALUE_HEADS * HEAD_WIDTH)

    def swap_dp(x, step):
        return lax.ppermute(x, "dp", [(i, i ^ step) for i in range(dp_count)])

    def ahead(x):
        return lax.ppermute(x, "sp", [(i, i + 2) for i in range(sp_count - 2)])

    def swap_core(mine, theirs):
        x = jnp.where(sp % 2 == 0, mine, theirs)
        return lax.ppermute(x, "sp", [(i, i ^ 1) for i in range(sp_count)])

    def pack(source, step, low, heads):
        return pack_q(source, q, blocks, step, low, heads)

    tie = lax.optimization_barrier
    all_heads = KEY_VALUE_HEADS
    cut = 6 * KEY_VALUE_HEADS // 8
    stay, *own = pack_kv(block_source, k, v, blocks)
    stay = stay[None]
    own[0], own[1] = swap_dp(own[0], 1), swap_dp(own[1], 2)
    stay_two = ahead(stay)
    near = [pack(block_source, step, 0, all_heads) for step in (1, 2)]
    near, source, stay_two, *own = tie((near, block_source, stay_two, *own))
    far_own = swap_dp(own[2], 3)
    near_own = jnp.stack(own[:2])
    near_two = ahead(near_own)
    stay_one = swap_core(stay, stay_two)
    kept = pack(source, 0, 0, all_heads)
    far = [pack(source, 3, 0, cut), pack(source, 3, cut, all_heads - cut)]
    near, kept, far, far_own, stay_one = tie((near, kept, far, far_own, stay_one))
    near = [swap_dp(x, step) for step, x in enumerate(near, 1)]
    far_own = far_own[None]
    far_two = ahead(far_own)
    rest_one = swap_core(
        jnp.concatenate([near_own, far_own]), jnp.concatenate([near_two, far_two])
    )
    windows = [stay_two, near_two, far_two, stay_one, rest_one, stay, near_own, far_own]

    call = functools.partial(attend, block_source, documents, windows=windows, shape=q.shape)
    out = call([kept], base=None, blocks=blocks, steps=(0,), low=0, heads=all_heads)
    far, near, out = tie((far, near, out))
    far = [swap_dp(x, 3) for x in far]
    out = call(near, base=out, blocks=blocks, steps=(1, 2), low=0, heads=all_heads)
    out = call(far[:1], base=out, blocks=blocks, steps=(3,), low=0, heads=cut)
    out = call(far[1:], base=out, blocks=blocks, steps=(3,), low=cut, heads=all_heads - cut)
    return out.reshape(1, tok_dev, QUERY_HEADS * HEAD_WIDTH)


def solution(mesh):
    placed = (P("dp", "sp", None), P("dp", "sp", None), P("dp", "sp", None), P(), P("dp", None))
    return jax.shard_map(
        on_device, mesh=mesh, in_specs=placed, out_specs=P("dp", "sp", None), check_vma=False
    )
```

```python
import functools
import math

import jax
import jax.numpy as jnp
from jax import lax
from jax.experimental import pallas as pl
from jax.experimental.pallas import tpu as pltpu
from jax.sharding import PartitionSpec as P

QUERY_HEADS = 64
KEY_VALUE_HEADS = 8
HEAD_WIDTH = 128
BALANCE_TOKENS = 128
MOST_BLK = 8
GROUP_HEADS = QUERY_HEADS // KEY_VALUE_HEADS
GROUP_WIDTH = GROUP_HEADS * HEAD_WIDTH
PAIR = 256
EXP2_SCALE = math.log2(math.e) / math.sqrt(HEAD_WIDTH)
WINDOW_OF = (
    ((0, 0), (1, 0), (2, 0), (3, 0)),
    ((4, 0), (5, 0), (6, 0), (4, 1)),
    ((7, 0), (8, 0), (9, 0), (10, 0)),
)
WINDOWS = 11
VMEM_LIMIT = 64 * 1024 * 1024


def position():
    return lax.axis_index("dp"), lax.axis_index("sp")


def leaving_slot(source_ref, blocks, dp, sp, other):
    slot = jnp.int32(0)
    for place in range(blocks):
        entry = source_ref[sp, other * blocks + place]
        slot = jnp.where(entry // blocks == dp, entry % blocks, slot)
    return slot


def landing_slot(source_ref, blocks, dp, sp, other):
    slot = jnp.int32(0)
    for place in range(blocks):
        entry = source_ref[sp, dp * blocks + place]
        slot = jnp.where(entry // blocks == other, place, slot)
    return slot


def block_rows(slot):
    return pl.ds(pl.multiple_of(slot * BALANCE_TOKENS, BALANCE_TOKENS), BALANCE_TOKENS)


def pack_kv_kernel(blocks, source_ref, k_ref, v_ref, *rest):
    outs, (buf, sem) = rest[:blocks], rest[blocks:]
    dp, sp = position()
    reads, writes = [], []
    for order, step in enumerate([*range(1, blocks), 0]):
        rows = block_rows(leaving_slot(source_ref, blocks, dp, sp, dp ^ step))
        for which, ref in enumerate((k_ref, v_ref)):
            place, number = buf.at[order, which], 2 * order + which
            reads.append(pltpu.make_async_copy(ref.at[rows], place, sem.at[number, 0]))
            writes.append(
                pltpu.make_async_copy(place, outs[step].at[which], sem.at[number, 1])
            )
    for copy in reads:
        copy.start()
    for read, write in zip(reads, writes):
        read.wait()
        write.start()
    for copy in writes:
        copy.wait()


def pack_kv(source, k, v, blocks):
    width = k.shape[1]
    hbm = pl.BlockSpec(memory_space=pltpu.HBM)
    return pl.pallas_call(
        functools.partial(pack_kv_kernel, blocks),
        out_shape=[jax.ShapeDtypeStruct((2, BALANCE_TOKENS, width), k.dtype)] * blocks,
        in_specs=[pl.BlockSpec(memory_space=pltpu.SMEM), hbm, hbm],
        out_specs=[hbm] * blocks,
        scratch_shapes=[
            pltpu.VMEM((blocks, 2, BALANCE_TOKENS, width), k.dtype),
            pltpu.SemaphoreType.DMA((2 * blocks, 2)),
        ],
        compiler_params=pltpu.CompilerParams(vmem_limit_bytes=VMEM_LIMIT),
        cost_estimate=pl.CostEstimate(flops=0, bytes_accessed=4 * 2**20, transcendentals=0),
        name="pack_kv",
    )(source, k, v)


def pack_q_kernel(blocks, step, first, source_ref, q_ref, out_ref, buf, turned, sem):
    dp, sp = position()
    rows = block_rows(leaving_slot(source_ref, blocks, dp, sp, dp ^ step))
    groups = buf.shape[0]

    def read(group):
        lanes = pl.ds(pl.multiple_of(first + group * GROUP_WIDTH, GROUP_WIDTH), GROUP_WIDTH)
        return pltpu.make_async_copy(q_ref.at[rows, lanes], buf.at[group], sem.at[group, 0])

    def write(group):
        span = pl.ds(pl.multiple_of(group * GROUP_WIDTH, GROUP_WIDTH), GROUP_WIDTH)
        return pltpu.make_async_copy(turned.at[group], out_ref.at[span], sem.at[group, 1])

    @pl.loop(0, groups)
    def _(group):
        read(group).start()

    @pl.loop(0, groups)
    def _(group):
        read(group).wait()
        for head in range(GROUP_HEADS):
            span = slice(head * HEAD_WIDTH, (head + 1) * HEAD_WIDTH)
            turned[group, span] = buf[group, :, span].T
        write(group).start()

    @pl.loop(0, groups)
    def _(group):
        write(group).wait()


def pack_q(source, q, blocks, step, first_head, heads):
    width = heads * GROUP_WIDTH
    hbm = pl.BlockSpec(memory_space=pltpu.HBM)
    return pl.pallas_call(
        functools.partial(pack_q_kernel, blocks, step, first_head * GROUP_WIDTH),
        out_shape=jax.ShapeDtypeStruct((width, BALANCE_TOKENS), q.dtype),
        in_specs=[pl.BlockSpec(memory_space=pltpu.SMEM), hbm],
        out_specs=hbm,
        scratch_shapes=[
            pltpu.VMEM((heads, BALANCE_TOKENS, GROUP_WIDTH), q.dtype),
            pltpu.VMEM((heads, GROUP_WIDTH, BALANCE_TOKENS), q.dtype),
            pltpu.SemaphoreType.DMA((heads, 2)),
        ],
        compiler_params=pltpu.CompilerParams(vmem_limit_bytes=VMEM_LIMIT),
        cost_estimate=pl.CostEstimate(
            flops=0, bytes_accessed=4 * width * BALANCE_TOKENS, transcendentals=0
        ),
        name=f"pack_q_{step}_{first_head}",
    )(source, q)


def attend_kernel(blocks, steps, low, heads, *refs):
    count = len(steps)
    source_ref, doc_ref, *q_refs = refs[: 2 + count]
    windows = refs[2 + count : 2 + count + WINDOWS]
    out_ref, q_buf, k_buf, v_buf, o_buf, s_buf, vt_buf, info, q_sem, kv_sem, o_sem = refs[-11:]
    tasks = count * heads
    dp, sp = position()

    def q_copy(task, which):
        rows = pl.ds(pl.multiple_of((task % heads) * GROUP_WIDTH, GROUP_WIDTH), GROUP_WIDTH)
        side = task % 2
        return pltpu.make_async_copy(q_refs[which].at[rows], q_buf.at[side], q_sem.at[side])

    def q_start(task):
        for which in range(count):

            @pl.when(task // heads == which)
            def _():
                q_copy(task, which).start()

    q_start(jnp.int32(0))

    origin = (sp - 2) * blocks
    lowest = jnp.int32(3 * blocks)
    highest = jnp.int32(0)
    for which, step in enumerate(steps):
        slot = landing_slot(source_ref, blocks, dp, sp, dp ^ step)
        block = sp * blocks + slot
        length = jnp.int32(1)
        for back in range(1, MOST_BLK):
            same = doc_ref[0, jnp.maximum(block - back, 0)] == doc_ref[0, block]
            length = length + ((block >= back) & same).astype(jnp.int32)
        half = (length + 1) // 2
        start = 2 * blocks + slot + 1 - 2 * half
        info[which, 0] = slot
        info[which, 1] = half
        info[which, 2] = start * BALANCE_TOKENS
        info[which, 3] = (length % 2) * BALANCE_TOKENS
        lowest = jnp.minimum(lowest, start)
        highest = jnp.maximum(highest, 2 * blocks + slot)

    kv_lanes = pl.ds(low * HEAD_WIDTH, heads * HEAD_WIDTH)

    def window_copies(number):
        column, step = sp - 2 + number // blocks, number % blocks
        known = jnp.maximum(column, 0)
        place = number // blocks * blocks + landing_slot(source_ref, blocks, dp, known, dp ^ step)
        wanted = (column >= 0) & (place >= lowest) & (place <= highest)
        rows = block_rows(place)
        index, inner = WINDOW_OF[number // blocks][step]
        return wanted, [
            pltpu.make_async_copy(
                windows[index].at[inner, which, :, kv_lanes],
                buf.at[rows],
                kv_sem.at[number, which],
            )
            for which, buf in enumerate((k_buf, v_buf))
        ]

    fetches = [window_copies(number) for number in range(3 * blocks)]
    for wanted, copies in fetches:

        @pl.when(wanted)
        def _():
            for copy in copies:
                copy.start()

    @pl.when(lowest + origin < 0)
    def _():
        rows = block_rows(lowest)
        k_buf[rows] = jnp.zeros((BALANCE_TOKENS, k_buf.shape[1]), k_buf.dtype)
        v_buf[rows] = jnp.zeros((BALANCE_TOKENS, v_buf.shape[1]), v_buf.dtype)

    for wanted, copies in fetches:

        @pl.when(wanted)
        def _():
            for copy in copies:
                copy.wait()

    pairs = GROUP_WIDTH // PAIR
    eights = PAIR // 8
    tiles = BALANCE_TOKENS // 8

    def one_task(chunks, side, head, start, skipped):
        lanes = pl.ds(pl.multiple_of(head * HEAD_WIDTH, HEAD_WIDTH), HEAD_WIDTH)
        span = pl.ds(pl.multiple_of(start, BALANCE_TOKENS), chunks * PAIR)
        lower, upper = slice(0, BALANCE_TOKENS), slice(BALANCE_TOKENS, PAIR)
        row = lax.broadcasted_iota(jnp.int32, (BALANCE_TOKENS, PAIR), 0)
        column = lax.broadcasted_iota(jnp.int32, (BALANCE_TOKENS, PAIR), 1)
        allowed = row <= (column & (BALANCE_TOKENS - 1))
        tops = [None] * pairs
        totals = [None] * pairs
        sums = [None] * pairs
        shifts = [None] * pairs

        def rows_of(chunk):
            return pl.ds(pl.multiple_of(start + chunk * PAIR, BALANCE_TOKENS), PAIR)

        def score(pair, chunk):
            parts = [
                q_buf[side, pair * PAIR + member : pair * PAIR + member + HEAD_WIDTH]
                for member in range(0, PAIR, HEAD_WIDTH)
            ]
            whole = jnp.dot(
                k_buf[rows_of(chunk), lanes],
                jnp.concatenate(parts, axis=1),
                preferred_element_type=jnp.float32,
            )
            for part in (lower, upper):
                base = chunk * PAIR + part.start
                held = whole[part]
                if chunk == 0 and part is lower:
                    held = jnp.where(skipped > 0, -1e30, held)
                if chunk == chunks - 1 and part is upper:
                    held = jnp.where(allowed, held, -1e30)
                s_buf[pair, base : base + BALANCE_TOKENS] = held
                high = jnp.max(held.reshape(tiles, 8, PAIR), axis=0)
                tops[pair] = high if base == 0 else jnp.maximum(tops[pair], high)

        def settle(pair):
            shifts[pair] = jnp.max(tops[pair], axis=0, keepdims=True) * EXP2_SCALE

        def mix(pair, chunk):
            keys = slice(chunk * PAIR, (chunk + 1) * PAIR)
            weight = jnp.exp2(s_buf[pair, keys] * EXP2_SCALE - shifts[pair])
            added = jnp.sum(weight.reshape(eights, 8, PAIR), axis=0)
            mixed = jnp.dot(
                vt_buf[:, keys],
                weight.astype(jnp.bfloat16),
                preferred_element_type=jnp.float32,
            )
            totals[pair] = added if chunk == 0 else totals[pair] + added
            sums[pair] = mixed if chunk == 0 else sums[pair] + mixed

        def finish(pair):
            scaled = sums[pair] * (1.0 / jnp.sum(totals[pair], axis=0, keepdims=True))
            scaled = scaled.astype(o_buf.dtype)
            for member in range(0, PAIR, HEAD_WIDTH):
                piece = scaled[:, member : member + HEAD_WIDTH].T
                o_buf[side, :, pair * PAIR + member : pair * PAIR + member + HEAD_WIDTH] = piece

        for chunk in range(chunks):
            score(0, chunk)
            vt_buf[:, chunk * PAIR : (chunk + 1) * PAIR] = v_buf[rows_of(chunk), lanes].T
        for pair in range(pairs):
            settle(pair)
            for chunk in range(chunks):
                if pair + 1 < pairs:
                    score(pair + 1, chunk)
                mix(pair, chunk)
            if pair:
                finish(pair - 1)
        finish(pairs - 1)

    def o_copy(task):
        side = task % 2
        lanes = pl.ds(
            pl.multiple_of((low + task % heads) * GROUP_WIDTH, GROUP_WIDTH), GROUP_WIDTH
        )
        rows = block_rows(info[task // heads, 0])
        return pltpu.make_async_copy(o_buf.at[side], out_ref.at[rows, lanes], o_sem.at[side])

    @pl.loop(0, tasks)
    def _(task):
        @pl.when(task + 1 < tasks)
        def _():
            q_start(task + 1)

        q_copy(task, 0).wait()

        @pl.when(task >= 2)
        def _():
            o_copy(task - 2).wait()

        piece = task // heads
        half, start, skipped = info[piece, 1], info[piece, 2], info[piece, 3]
        for chunks in range(1, MOST_BLK * BALANCE_TOKENS // PAIR + 1):

            @pl.when(half == chunks)
            def _():
                one_task(chunks, task % 2, task % heads, start, skipped)

        o_copy(task).start()

    for task in range(max(tasks - 2, 0), tasks):
        o_copy(jnp.int32(task)).wait()


def attend(source, docs, pieces, windows, base, shape, blocks, steps, low, heads):
    hbm = pl.BlockSpec(memory_space=pltpu.HBM)
    smem = pl.BlockSpec(memory_space=pltpu.SMEM)
    operands = [source, docs, *pieces, *windows] + ([] if base is None else [base])
    reach = MOST_BLK * BALANCE_TOKENS
    held = 3 * blocks * BALANCE_TOKENS
    dtype = pieces[0].dtype
    return pl.pallas_call(
        functools.partial(attend_kernel, blocks, steps, low, heads),
        out_shape=jax.ShapeDtypeStruct(shape, dtype),
        in_specs=[smem, smem] + [hbm] * (len(operands) - 2),
        out_specs=hbm,
        scratch_shapes=[
            pltpu.VMEM((2, GROUP_WIDTH, BALANCE_TOKENS), dtype),
            pltpu.VMEM((held, heads * HEAD_WIDTH), dtype),
            pltpu.VMEM((held, heads * HEAD_WIDTH), dtype),
            pltpu.VMEM((2, BALANCE_TOKENS, GROUP_WIDTH), dtype),
            pltpu.VMEM((GROUP_WIDTH // PAIR, reach, PAIR), jnp.float32),
            pltpu.VMEM((HEAD_WIDTH, reach), dtype),
            pltpu.SMEM((len(steps), 4), jnp.int32),
            pltpu.SemaphoreType.DMA((2,)),
            pltpu.SemaphoreType.DMA((3 * blocks, 2)),
            pltpu.SemaphoreType.DMA((2,)),
        ],
        input_output_aliases={} if base is None else {len(operands) - 1: 0},
        compiler_params=pltpu.CompilerParams(vmem_limit_bytes=VMEM_LIMIT),
        cost_estimate=pl.CostEstimate(flops=0, bytes_accessed=2**10, transcendentals=0),
        name=f"attend_{steps[0]}_{low}",
    )(*operands)


def on_device(query_matrix, key_matrix, value_matrix, block_source, documents):
    dp_count = lax.axis_size("dp")
    sp_count = lax.axis_size("sp")
    sp = lax.axis_index("sp")
    tok_dev = query_matrix.shape[1]
    blocks = tok_dev // BALANCE_TOKENS
    assert blocks == dp_count == 4
    q = query_matrix.reshape(tok_dev, QUERY_HEADS * HEAD_WIDTH)
    k = key_matrix.reshape(tok_dev, KEY_VALUE_HEADS * HEAD_WIDTH)
    v = value_matrix.reshape(tok_dev, KEY_VALUE_HEADS * HEAD_WIDTH)

    def swap_dp(x, step):
        return lax.ppermute(x, "dp", [(i, i ^ step) for i in range(dp_count)])

    def ahead(x):
        return lax.ppermute(x, "sp", [(i, i + 2) for i in range(sp_count - 2)])

    def swap_core(mine, theirs):
        x = jnp.where(sp % 2 == 0, mine, theirs)
        return lax.ppermute(x, "sp", [(i, i ^ 1) for i in range(sp_count)])

    def pack(source, step, low, heads):
        return pack_q(source, q, blocks, step, low, heads)

    tie = lax.optimization_barrier
    all_heads = KEY_VALUE_HEADS
    cut = 6 * KEY_VALUE_HEADS // 8
    own = list(pack_kv(block_source, k, v, blocks))
    two = [None] * blocks
    own[3] = swap_dp(own[3], 3)
    two[0] = ahead(own[0])
    near = [pack(block_source, step, 0, all_heads) for step in (1, 2)]
    near, two[0], *own[1:] = tie((near, two[0], *own[1:]))
    own[1], own[2] = swap_dp(own[1], 1), swap_dp(own[2], 2)
    two[3] = ahead(own[3])
    near, source, two[3], own[1], own[2] = tie((near, block_source, two[3], own[1], own[2]))
    near = [swap_dp(x, step) for step, x in enumerate(near, 1)]
    two[1], two[2] = ahead(own[1]), ahead(own[2])
    kept = pack(source, 0, 0, all_heads)
    far = [pack(source, 3, 0, cut), pack(source, 3, cut, all_heads - cut)]
    kept, far, two[1] = tie((kept, far, two[1]))
    one = [
        swap_core(jnp.stack([own[0], own[3]]), jnp.stack([two[0], two[3]])),
        swap_core(own[1][None], two[1][None]),
        swap_core(own[2][None], two[2][None]),
    ]
    windows = [*(x[None] for x in two), *one, *(x[None] for x in own)]

    call = functools.partial(attend, block_source, documents, windows=windows, shape=q.shape)
    out = call([kept], base=None, blocks=blocks, steps=(0,), low=0, heads=all_heads)
    far, near, out = tie((far, near, out))
    far = [swap_dp(x, 3) for x in far]
    out = call(near, base=out, blocks=blocks, steps=(1, 2), low=0, heads=all_heads)
    out = call(far[:1], base=out, blocks=blocks, steps=(3,), low=0, heads=cut)
    out = call(far[1:], base=out, blocks=blocks, steps=(3,), low=cut, heads=all_heads - cut)
    return out.reshape(1, tok_dev, QUERY_HEADS * HEAD_WIDTH)


def solution(mesh):
    placed = (P("dp", "sp", None), P("dp", "sp", None), P("dp", "sp", None), P(), P("dp", None))
    return jax.shard_map(
        on_device, mesh=mesh, in_specs=placed, out_specs=P("dp", "sp", None), check_vma=False
    )
```

```python
import functools
import math

import jax
import jax.numpy as jnp
from jax import lax
from jax.experimental import pallas as pl
from jax.experimental.pallas import tpu as pltpu
from jax.sharding import PartitionSpec as P

QUERY_HEADS = 64
KEY_VALUE_HEADS = 8
HEAD_WIDTH = 128
BALANCE_TOKENS = 128
MOST_BLK = 8
GROUP_HEADS = QUERY_HEADS // KEY_VALUE_HEADS
GROUP_WIDTH = GROUP_HEADS * HEAD_WIDTH
PAIR = 256
EXP2_SCALE = math.log2(math.e) / math.sqrt(HEAD_WIDTH)
WINDOW_OF = (
    ((0, 0), (1, 0), (2, 0), (3, 0)),
    ((4, 0), (5, 0), (6, 0), (4, 1)),
    ((7, 0), (8, 0), (9, 0), (10, 0)),
)
WINDOWS = 11
VMEM_LIMIT = 64 * 1024 * 1024


def position():
    return lax.axis_index("dp"), lax.axis_index("sp")


def leaving_slot(source_ref, blocks, dp, sp, other):
    slot = jnp.int32(0)
    for place in range(blocks):
        entry = source_ref[sp, other * blocks + place]
        slot = jnp.where(entry // blocks == dp, entry % blocks, slot)
    return slot


def landing_slot(source_ref, blocks, dp, sp, other):
    slot = jnp.int32(0)
    for place in range(blocks):
        entry = source_ref[sp, dp * blocks + place]
        slot = jnp.where(entry // blocks == other, place, slot)
    return slot


def block_rows(slot):
    return pl.ds(pl.multiple_of(slot * BALANCE_TOKENS, BALANCE_TOKENS), BALANCE_TOKENS)


def pack_kv_kernel(blocks, source_ref, k_ref, v_ref, *rest):
    outs, (buf, sem) = rest[:blocks], rest[blocks:]
    dp, sp = position()
    reads, writes = [], []
    for order, step in enumerate([*range(1, blocks), 0]):
        rows = block_rows(leaving_slot(source_ref, blocks, dp, sp, dp ^ step))
        for which, ref in enumerate((k_ref, v_ref)):
            place, number = buf.at[order, which], 2 * order + which
            reads.append(pltpu.make_async_copy(ref.at[rows], place, sem.at[number, 0]))
            writes.append(
                pltpu.make_async_copy(place, outs[step].at[which], sem.at[number, 1])
            )
    for copy in reads:
        copy.start()
    for read, write in zip(reads, writes):
        read.wait()
        write.start()
    for copy in writes:
        copy.wait()


def pack_kv(source, k, v, blocks):
    width = k.shape[1]
    hbm = pl.BlockSpec(memory_space=pltpu.HBM)
    return pl.pallas_call(
        functools.partial(pack_kv_kernel, blocks),
        out_shape=[jax.ShapeDtypeStruct((2, BALANCE_TOKENS, width), k.dtype)] * blocks,
        in_specs=[pl.BlockSpec(memory_space=pltpu.SMEM), hbm, hbm],
        out_specs=[hbm] * blocks,
        scratch_shapes=[
            pltpu.VMEM((blocks, 2, BALANCE_TOKENS, width), k.dtype),
            pltpu.SemaphoreType.DMA((2 * blocks, 2)),
        ],
        compiler_params=pltpu.CompilerParams(vmem_limit_bytes=VMEM_LIMIT),
        cost_estimate=pl.CostEstimate(flops=0, bytes_accessed=4 * 2**20, transcendentals=0),
        name="pack_kv",
    )(source, k, v)


def pack_q_kernel(blocks, step, first, source_ref, q_ref, out_ref, buf, turned, sem):
    dp, sp = position()
    rows = block_rows(leaving_slot(source_ref, blocks, dp, sp, dp ^ step))
    groups = buf.shape[0]

    def read(group):
        lanes = pl.ds(pl.multiple_of(first + group * GROUP_WIDTH, GROUP_WIDTH), GROUP_WIDTH)
        return pltpu.make_async_copy(q_ref.at[rows, lanes], buf.at[group], sem.at[group, 0])

    def write(group):
        span = pl.ds(pl.multiple_of(group * GROUP_WIDTH, GROUP_WIDTH), GROUP_WIDTH)
        return pltpu.make_async_copy(turned.at[group], out_ref.at[span], sem.at[group, 1])

    @pl.loop(0, groups)
    def _(group):
        read(group).start()

    @pl.loop(0, groups)
    def _(group):
        read(group).wait()
        for head in range(GROUP_HEADS):
            span = slice(head * HEAD_WIDTH, (head + 1) * HEAD_WIDTH)
            turned[group, span] = buf[group, :, span].T
        write(group).start()

    @pl.loop(0, groups)
    def _(group):
        write(group).wait()


def pack_q(source, q, blocks, step, first_head, heads):
    width = heads * GROUP_WIDTH
    hbm = pl.BlockSpec(memory_space=pltpu.HBM)
    return pl.pallas_call(
        functools.partial(pack_q_kernel, blocks, step, first_head * GROUP_WIDTH),
        out_shape=jax.ShapeDtypeStruct((width, BALANCE_TOKENS), q.dtype),
        in_specs=[pl.BlockSpec(memory_space=pltpu.SMEM), hbm],
        out_specs=hbm,
        scratch_shapes=[
            pltpu.VMEM((heads, BALANCE_TOKENS, GROUP_WIDTH), q.dtype),
            pltpu.VMEM((heads, GROUP_WIDTH, BALANCE_TOKENS), q.dtype),
            pltpu.SemaphoreType.DMA((heads, 2)),
        ],
        compiler_params=pltpu.CompilerParams(vmem_limit_bytes=VMEM_LIMIT),
        cost_estimate=pl.CostEstimate(
            flops=0, bytes_accessed=4 * width * BALANCE_TOKENS, transcendentals=0
        ),
        name=f"pack_q_{step}_{first_head}",
    )(source, q)


def attend_kernel(blocks, steps, low, heads, *refs):
    count = len(steps)
    source_ref, doc_ref, *q_refs = refs[: 2 + count]
    windows = refs[2 + count : 2 + count + WINDOWS]
    out_ref, q_buf, k_buf, v_buf, o_buf, s_buf, vt_buf, info, q_sem, kv_sem, o_sem = refs[-11:]
    tasks = count * heads
    dp, sp = position()

    def q_copy(task, which):
        rows = pl.ds(pl.multiple_of((task % heads) * GROUP_WIDTH, GROUP_WIDTH), GROUP_WIDTH)
        side = task % 2
        return pltpu.make_async_copy(q_refs[which].at[rows], q_buf.at[side], q_sem.at[side])

    def q_start(task):
        for which in range(count):

            @pl.when(task // heads == which)
            def _():
                q_copy(task, which).start()

    q_start(jnp.int32(0))

    origin = (sp - 2) * blocks
    lowest = jnp.int32(3 * blocks)
    highest = jnp.int32(0)
    for which, step in enumerate(steps):
        slot = landing_slot(source_ref, blocks, dp, sp, dp ^ step)
        block = sp * blocks + slot
        length = jnp.int32(1)
        for back in range(1, MOST_BLK):
            same = doc_ref[0, jnp.maximum(block - back, 0)] == doc_ref[0, block]
            length = length + ((block >= back) & same).astype(jnp.int32)
        half = (length + 1) // 2
        start = 2 * blocks + slot + 1 - 2 * half
        info[which, 0] = slot
        info[which, 1] = half
        info[which, 2] = start * BALANCE_TOKENS
        info[which, 3] = (length % 2) * BALANCE_TOKENS
        lowest = jnp.minimum(lowest, start)
        highest = jnp.maximum(highest, 2 * blocks + slot)

    kv_lanes = pl.ds(low * HEAD_WIDTH, heads * HEAD_WIDTH)

    def window_copies(number):
        column, step = sp - 2 + number // blocks, number % blocks
        known = jnp.maximum(column, 0)
        place = number // blocks * blocks + landing_slot(source_ref, blocks, dp, known, dp ^ step)
        wanted = (column >= 0) & (place >= lowest) & (place <= highest)
        rows = block_rows(place)
        index, inner = WINDOW_OF[number // blocks][step]
        return wanted, [
            pltpu.make_async_copy(
                windows[index].at[inner, which, :, kv_lanes],
                buf.at[rows],
                kv_sem.at[number, which],
            )
            for which, buf in enumerate((k_buf, v_buf))
        ]

    fetches = [window_copies(number) for number in range(3 * blocks)]
    for wanted, copies in fetches:

        @pl.when(wanted)
        def _():
            for copy in copies:
                copy.start()

    @pl.when(lowest + origin < 0)
    def _():
        rows = block_rows(lowest)
        k_buf[rows] = jnp.zeros((BALANCE_TOKENS, k_buf.shape[1]), k_buf.dtype)
        v_buf[rows] = jnp.zeros((BALANCE_TOKENS, v_buf.shape[1]), v_buf.dtype)

    for wanted, copies in fetches:

        @pl.when(wanted)
        def _():
            for copy in copies:
                copy.wait()

    pairs = GROUP_WIDTH // PAIR
    eights = PAIR // 8
    tiles = BALANCE_TOKENS // 8

    def one_task(chunks, side, head, start, skipped):
        lanes = pl.ds(pl.multiple_of(head * HEAD_WIDTH, HEAD_WIDTH), HEAD_WIDTH)
        span = pl.ds(pl.multiple_of(start, BALANCE_TOKENS), chunks * PAIR)
        lower, upper = slice(0, BALANCE_TOKENS), slice(BALANCE_TOKENS, PAIR)
        row = lax.broadcasted_iota(jnp.int32, (BALANCE_TOKENS, PAIR), 0)
        column = lax.broadcasted_iota(jnp.int32, (BALANCE_TOKENS, PAIR), 1)
        allowed = row <= (column & (BALANCE_TOKENS - 1))
        tops = [None] * pairs
        totals = [None] * pairs
        sums = [None] * pairs
        shifts = [None] * pairs

        def rows_of(chunk):
            return pl.ds(pl.multiple_of(start + chunk * PAIR, BALANCE_TOKENS), PAIR)

        def score(pair, chunk):
            parts = [
                q_buf[side, pair * PAIR + member : pair * PAIR + member + HEAD_WIDTH]
                for member in range(0, PAIR, HEAD_WIDTH)
            ]
            whole = jnp.dot(
                k_buf[rows_of(chunk), lanes],
                jnp.concatenate(parts, axis=1),
                preferred_element_type=jnp.float32,
            )
            for part in (lower, upper):
                base = chunk * PAIR + part.start
                held = whole[part]
                if chunk == 0 and part is lower:
                    held = jnp.where(skipped > 0, -1e30, held)
                if chunk == chunks - 1 and part is upper:
                    held = jnp.where(allowed, held, -1e30)
                s_buf[pair, base : base + BALANCE_TOKENS] = held
                high = jnp.max(held.reshape(tiles, 8, PAIR), axis=0)
                tops[pair] = high if base == 0 else jnp.maximum(tops[pair], high)

        def settle(pair):
            shifts[pair] = jnp.max(tops[pair], axis=0, keepdims=True) * EXP2_SCALE

        def mix(pair, chunk):
            keys = slice(chunk * PAIR, (chunk + 1) * PAIR)
            weight = jnp.exp2(s_buf[pair, keys] * EXP2_SCALE - shifts[pair])
            added = jnp.sum(weight.reshape(eights, 8, PAIR), axis=0)
            mixed = jnp.dot(
                vt_buf[:, keys],
                weight.astype(jnp.bfloat16),
                preferred_element_type=jnp.float32,
            )
            totals[pair] = added if chunk == 0 else totals[pair] + added
            sums[pair] = mixed if chunk == 0 else sums[pair] + mixed

        def finish(pair):
            scaled = sums[pair] * (1.0 / jnp.sum(totals[pair], axis=0, keepdims=True))
            scaled = scaled.astype(o_buf.dtype)
            for member in range(0, PAIR, HEAD_WIDTH):
                piece = scaled[:, member : member + HEAD_WIDTH].T
                o_buf[side, :, pair * PAIR + member : pair * PAIR + member + HEAD_WIDTH] = piece

        for chunk in range(chunks):
            score(0, chunk)
            vt_buf[:, chunk * PAIR : (chunk + 1) * PAIR] = v_buf[rows_of(chunk), lanes].T
        for pair in range(pairs):
            settle(pair)
            for chunk in range(chunks):
                if pair + 1 < pairs:
                    score(pair + 1, chunk)
                mix(pair, chunk)
            if pair:
                finish(pair - 1)
        finish(pairs - 1)

    def o_copy(task):
        side = task % 2
        lanes = pl.ds(
            pl.multiple_of((low + task % heads) * GROUP_WIDTH, GROUP_WIDTH), GROUP_WIDTH
        )
        rows = block_rows(info[task // heads, 0])
        return pltpu.make_async_copy(o_buf.at[side], out_ref.at[rows, lanes], o_sem.at[side])

    @pl.loop(0, tasks)
    def _(task):
        @pl.when(task + 1 < tasks)
        def _():
            q_start(task + 1)

        q_copy(task, 0).wait()

        @pl.when(task >= 2)
        def _():
            o_copy(task - 2).wait()

        piece = task // heads
        half, start, skipped = info[piece, 1], info[piece, 2], info[piece, 3]
        for chunks in range(1, MOST_BLK * BALANCE_TOKENS // PAIR + 1):

            @pl.when(half == chunks)
            def _():
                one_task(chunks, task % 2, task % heads, start, skipped)

        o_copy(task).start()

    for task in range(max(tasks - 2, 0), tasks):
        o_copy(jnp.int32(task)).wait()


def attend(source, docs, pieces, windows, base, shape, blocks, steps, low, heads):
    hbm = pl.BlockSpec(memory_space=pltpu.HBM)
    smem = pl.BlockSpec(memory_space=pltpu.SMEM)
    operands = [source, docs, *pieces, *windows] + ([] if base is None else [base])
    reach = MOST_BLK * BALANCE_TOKENS
    held = 3 * blocks * BALANCE_TOKENS
    dtype = pieces[0].dtype
    return pl.pallas_call(
        functools.partial(attend_kernel, blocks, steps, low, heads),
        out_shape=jax.ShapeDtypeStruct(shape, dtype),
        in_specs=[smem, smem] + [hbm] * (len(operands) - 2),
        out_specs=hbm,
        scratch_shapes=[
            pltpu.VMEM((2, GROUP_WIDTH, BALANCE_TOKENS), dtype),
            pltpu.VMEM((held, heads * HEAD_WIDTH), dtype),
            pltpu.VMEM((held, heads * HEAD_WIDTH), dtype),
            pltpu.VMEM((2, BALANCE_TOKENS, GROUP_WIDTH), dtype),
            pltpu.VMEM((GROUP_WIDTH // PAIR, reach, PAIR), jnp.float32),
            pltpu.VMEM((HEAD_WIDTH, reach), dtype),
            pltpu.SMEM((len(steps), 4), jnp.int32),
            pltpu.SemaphoreType.DMA((2,)),
            pltpu.SemaphoreType.DMA((3 * blocks, 2)),
            pltpu.SemaphoreType.DMA((2,)),
        ],
        input_output_aliases={} if base is None else {len(operands) - 1: 0},
        compiler_params=pltpu.CompilerParams(vmem_limit_bytes=VMEM_LIMIT),
        cost_estimate=pl.CostEstimate(flops=0, bytes_accessed=2**10, transcendentals=0),
        name=f"attend_{steps[0]}_{low}",
    )(*operands)


def after(first, arrays):
    hbm = pl.BlockSpec(memory_space=pltpu.HBM)
    return pl.pallas_call(
        lambda *refs: None,
        out_shape=[jax.ShapeDtypeStruct(x.shape, x.dtype) for x in arrays],
        in_specs=[hbm] * (len(arrays) + 1),
        out_specs=[hbm] * len(arrays),
        input_output_aliases={i + 1: i for i in range(len(arrays))},
        cost_estimate=pl.CostEstimate(flops=0, bytes_accessed=2**10, transcendentals=0),
        name="after",
    )(first, *arrays)


def on_device(query_matrix, key_matrix, value_matrix, block_source, documents):
    dp_count = lax.axis_size("dp")
    sp_count = lax.axis_size("sp")
    sp = lax.axis_index("sp")
    tok_dev = query_matrix.shape[1]
    blocks = tok_dev // BALANCE_TOKENS
    assert blocks == dp_count == 4
    q = query_matrix.reshape(tok_dev, QUERY_HEADS * HEAD_WIDTH)
    k = key_matrix.reshape(tok_dev, KEY_VALUE_HEADS * HEAD_WIDTH)
    v = value_matrix.reshape(tok_dev, KEY_VALUE_HEADS * HEAD_WIDTH)

    def swap_dp(x, step):
        return lax.ppermute(x, "dp", [(i, i ^ step) for i in range(dp_count)])

    def ahead(x):
        return lax.ppermute(x, "sp", [(i, i + 2) for i in range(sp_count - 2)])

    def swap_core(mine, theirs):
        x = jnp.where(sp % 2 == 0, mine, theirs)
        return lax.ppermute(x, "sp", [(i, i ^ 1) for i in range(sp_count)])

    def pack(source, step, low, heads):
        return pack_q(source, q, blocks, step, low, heads)

    tie = lax.optimization_barrier
    all_heads = KEY_VALUE_HEADS
    cut = 6 * KEY_VALUE_HEADS // 8
    own = list(pack_kv(block_source, k, v, blocks))
    two = [None] * blocks
    own[3] = swap_dp(own[3], 3)
    two[0] = ahead(own[0])
    near = [pack(block_source, step, 0, all_heads) for step in (1, 2)]
    near, two[0], *own[1:] = tie((near, two[0], *own[1:]))
    own[1], own[2] = swap_dp(own[1], 1), swap_dp(own[2], 2)
    two[3] = ahead(own[3])
    near, source, two[3], own[1], own[2] = tie((near, block_source, two[3], own[1], own[2]))
    near = [swap_dp(x, step) for step, x in enumerate(near, 1)]
    two[1], two[2] = ahead(own[1]), ahead(own[2])
    kept = pack(source, 0, 0, all_heads)
    far = [pack(source, 3, 0, cut), pack(source, 3, cut, all_heads - cut)]
    kept, far, two[1] = tie((kept, far, two[1]))
    one = [
        swap_core(jnp.stack([own[0], own[3]]), jnp.stack([two[0], two[3]])),
        swap_core(own[1][None], two[1][None]),
        swap_core(own[2][None], two[2][None]),
    ]
    windows = [*(x[None] for x in two), *one, *(x[None] for x in own)]

    call = functools.partial(attend, block_source, documents, windows=windows, shape=q.shape)
    out = call([kept], base=None, blocks=blocks, steps=(0,), low=0, heads=all_heads)
    near, out = tie((near, out))
    seen = near[0][:HEAD_WIDTH] + near[1][:HEAD_WIDTH]
    seen = lax.ppermute(seen, "sp", [(i, i ^ 1) for i in range(sp_count)])
    far = [swap_dp(x, 3) for x in after(seen, far)]
    out = call(near, base=out, blocks=blocks, steps=(1, 2), low=0, heads=all_heads)
    out = call(far[:1], base=out, blocks=blocks, steps=(3,), low=0, heads=cut)
    out = call(far[1:], base=out, blocks=blocks, steps=(3,), low=cut, heads=all_heads - cut)
    return out.reshape(1, tok_dev, QUERY_HEADS * HEAD_WIDTH)


def solution(mesh):
    placed = (P("dp", "sp", None), P("dp", "sp", None), P("dp", "sp", None), P(), P("dp", None))
    return jax.shard_map(
        on_device, mesh=mesh, in_specs=placed, out_specs=P("dp", "sp", None), check_vma=False
    )
```

```python
import functools
import math

import jax
import jax.numpy as jnp
from jax import lax
from jax.experimental import pallas as pl
from jax.experimental.pallas import tpu as pltpu
from jax.sharding import PartitionSpec as P

QUERY_HEADS = 64
KEY_VALUE_HEADS = 8
HEAD_WIDTH = 128
BALANCE_TOKENS = 128
MOST_BLK = 8
GROUP_HEADS = QUERY_HEADS // KEY_VALUE_HEADS
GROUP_WIDTH = GROUP_HEADS * HEAD_WIDTH
PAIR = 256
SCORE_SCALE = 1 / math.sqrt(HEAD_WIDTH)
VMEM_LIMIT = 64 * 1024 * 1024


def position():
    return lax.axis_index("dp"), lax.axis_index("sp")


def leaving_slot(source_ref, blocks, dp, sp, other):
    slot = jnp.int32(0)
    for place in range(blocks):
        entry = source_ref[sp, other * blocks + place]
        slot = jnp.where(entry // blocks == dp, entry % blocks, slot)
    return slot


def landing_slot(source_ref, blocks, dp, sp, other):
    slot = jnp.int32(0)
    for place in range(blocks):
        entry = source_ref[sp, dp * blocks + place]
        slot = jnp.where(entry // blocks == other, place, slot)
    return slot


def block_rows(slot):
    return pl.ds(pl.multiple_of(slot * BALANCE_TOKENS, BALANCE_TOKENS), BALANCE_TOKENS)


def pack_kv_kernel(blocks, source_ref, k_ref, v_ref, *rest):
    outs, (buf, sem) = rest[:blocks], rest[blocks:]
    dp, sp = position()
    reads, writes = [], []
    for order, step in enumerate([*range(1, blocks), 0]):
        rows = block_rows(leaving_slot(source_ref, blocks, dp, sp, dp ^ step))
        for which, ref in enumerate((k_ref, v_ref)):
            place, number = buf.at[order, which], 2 * order + which
            reads.append(pltpu.make_async_copy(ref.at[rows], place, sem.at[number, 0]))
            writes.append(
                pltpu.make_async_copy(place, outs[step].at[which], sem.at[number, 1])
            )
    for copy in reads:
        copy.start()
    for read, write in zip(reads, writes):
        read.wait()
        write.start()
    for copy in writes:
        copy.wait()


def pack_kv(source, k, v, blocks):
    width = k.shape[1]
    hbm = pl.BlockSpec(memory_space=pltpu.HBM)
    return pl.pallas_call(
        functools.partial(pack_kv_kernel, blocks),
        out_shape=[jax.ShapeDtypeStruct((2, BALANCE_TOKENS, width), k.dtype)] * blocks,
        in_specs=[pl.BlockSpec(memory_space=pltpu.SMEM), hbm, hbm],
        out_specs=[hbm] * blocks,
        scratch_shapes=[
            pltpu.VMEM((blocks, 2, BALANCE_TOKENS, width), k.dtype),
            pltpu.SemaphoreType.DMA((2 * blocks, 2)),
        ],
        compiler_params=pltpu.CompilerParams(vmem_limit_bytes=VMEM_LIMIT),
        cost_estimate=pl.CostEstimate(flops=0, bytes_accessed=4 * 2**20, transcendentals=0),
        name="pack_kv",
    )(source, k, v)


def pack_q_kernel(blocks, step, first, source_ref, q_ref, out_ref, buf, turned, sem):
    dp, sp = position()
    rows = block_rows(leaving_slot(source_ref, blocks, dp, sp, dp ^ step))
    groups = buf.shape[0]

    def read(group):
        lanes = pl.ds(pl.multiple_of(first + group * GROUP_WIDTH, GROUP_WIDTH), GROUP_WIDTH)
        return pltpu.make_async_copy(q_ref.at[rows, lanes], buf.at[group], sem.at[group, 0])

    def write(group):
        span = pl.ds(pl.multiple_of(group * GROUP_WIDTH, GROUP_WIDTH), GROUP_WIDTH)
        return pltpu.make_async_copy(turned.at[group], out_ref.at[span], sem.at[group, 1])

    @pl.loop(0, groups)
    def _(group):
        read(group).start()

    @pl.loop(0, groups)
    def _(group):
        read(group).wait()
        for head in range(GROUP_HEADS):
            span = slice(head * HEAD_WIDTH, (head + 1) * HEAD_WIDTH)
            turned[group, span] = buf[group, :, span].T
        write(group).start()

    @pl.loop(0, groups)
    def _(group):
        write(group).wait()


def pack_q(source, q, blocks, step, first_head, heads):
    width = heads * GROUP_WIDTH
    hbm = pl.BlockSpec(memory_space=pltpu.HBM)
    return pl.pallas_call(
        functools.partial(pack_q_kernel, blocks, step, first_head * GROUP_WIDTH),
        out_shape=jax.ShapeDtypeStruct((width, BALANCE_TOKENS), q.dtype),
        in_specs=[pl.BlockSpec(memory_space=pltpu.SMEM), hbm],
        out_specs=hbm,
        scratch_shapes=[
            pltpu.VMEM((heads, BALANCE_TOKENS, GROUP_WIDTH), q.dtype),
            pltpu.VMEM((heads, GROUP_WIDTH, BALANCE_TOKENS), q.dtype),
            pltpu.SemaphoreType.DMA((heads, 2)),
        ],
        compiler_params=pltpu.CompilerParams(vmem_limit_bytes=VMEM_LIMIT),
        cost_estimate=pl.CostEstimate(
            flops=0, bytes_accessed=4 * width * BALANCE_TOKENS, transcendentals=0
        ),
        name=f"pack_q_{step}_{first_head}",
    )(source, q)


def attend_kernel(blocks, steps, low, heads, *refs):
    count = len(steps)
    source_ref, doc_ref, *q_refs = refs[: 2 + count]
    windows = refs[2 + count : 2 + count + 3 * blocks]
    out_ref, q_buf, k_buf, v_buf, o_buf, s_buf, p_buf, vt_buf, info, q_sem, kv_sem, o_sem = refs[-12:]
    tasks = count * heads
    dp, sp = position()

    def q_copy(task, which):
        rows = pl.ds(pl.multiple_of((task % heads) * GROUP_WIDTH, GROUP_WIDTH), GROUP_WIDTH)
        side = task % 2
        return pltpu.make_async_copy(q_refs[which].at[rows], q_buf.at[side], q_sem.at[side])

    def q_start(task):
        for which in range(count):

            @pl.when(task // heads == which)
            def _():
                q_copy(task, which).start()

    q_start(jnp.int32(0))

    origin = (sp - 2) * blocks
    lowest = jnp.int32(3 * blocks)
    highest = jnp.int32(0)
    for which, step in enumerate(steps):
        slot = landing_slot(source_ref, blocks, dp, sp, dp ^ step)
        block = sp * blocks + slot
        length = jnp.int32(1)
        for back in range(1, MOST_BLK):
            same = doc_ref[0, jnp.maximum(block - back, 0)] == doc_ref[0, block]
            length = length + ((block >= back) & same).astype(jnp.int32)
        half = (length + 1) // 2
        start = 2 * blocks + slot + 1 - 2 * half
        info[which, 0] = slot
        info[which, 1] = half
        info[which, 2] = start * BALANCE_TOKENS
        info[which, 3] = (length % 2) * BALANCE_TOKENS
        lowest = jnp.minimum(lowest, start)
        highest = jnp.maximum(highest, 2 * blocks + slot)

    kv_lanes = pl.ds(low * HEAD_WIDTH, heads * HEAD_WIDTH)

    def window_copies(number):
        column, step = sp - 2 + number // blocks, number % blocks
        known = jnp.maximum(column, 0)
        place = number // blocks * blocks + landing_slot(source_ref, blocks, dp, known, dp ^ step)
        wanted = (column >= 0) & (place >= lowest) & (place <= highest)
        rows = block_rows(place)
        return wanted, [
            pltpu.make_async_copy(
                windows[number].at[which, :, kv_lanes],
                buf.at[rows],
                kv_sem.at[number, which],
            )
            for which, buf in enumerate((k_buf, v_buf))
        ]

    fetches = [window_copies(number) for number in range(3 * blocks)]
    for wanted, copies in fetches:

        @pl.when(wanted)
        def _():
            for copy in copies:
                copy.start()

    @pl.when(lowest + origin < 0)
    def _():
        rows = block_rows(lowest)
        k_buf[rows] = jnp.zeros((BALANCE_TOKENS, k_buf.shape[1]), k_buf.dtype)
        v_buf[rows] = jnp.zeros((BALANCE_TOKENS, v_buf.shape[1]), v_buf.dtype)

    for wanted, copies in fetches:

        @pl.when(wanted)
        def _():
            for copy in copies:
                copy.wait()

    pairs = GROUP_WIDTH // PAIR
    tiles = BALANCE_TOKENS // 8

    def one_task(chunks, side, head, start, skipped):
        lanes = pl.ds(pl.multiple_of(head * HEAD_WIDTH, HEAD_WIDTH), HEAD_WIDTH)
        span = pl.ds(pl.multiple_of(start, BALANCE_TOKENS), chunks * PAIR)
        lower, upper = slice(0, BALANCE_TOKENS), slice(BALANCE_TOKENS, PAIR)
        row = lax.broadcasted_iota(jnp.int32, (BALANCE_TOKENS, PAIR), 0)
        column = lax.broadcasted_iota(jnp.int32, (BALANCE_TOKENS, PAIR), 1)
        allowed = row <= (column & (BALANCE_TOKENS - 1))
        tops = [None] * pairs
        totals = [None] * pairs
        shifts = [None] * pairs

        def rows_of(chunk):
            return pl.ds(pl.multiple_of(start + chunk * PAIR, BALANCE_TOKENS), PAIR)

        def score(pair, chunk):
            parts = [
                q_buf[side, pair * PAIR + member : pair * PAIR + member + HEAD_WIDTH]
                for member in range(0, PAIR, HEAD_WIDTH)
            ]
            whole = jnp.dot(
                k_buf[rows_of(chunk), lanes],
                jnp.concatenate(parts, axis=1),
                preferred_element_type=jnp.float32,
            )
            for part in (lower, upper):
                base = chunk * PAIR + part.start
                held = whole[part]
                if chunk == 0 and part is lower:
                    held = jnp.where(skipped > 0, -1e30, held)
                if chunk == chunks - 1 and part is upper:
                    held = jnp.where(allowed, held, -1e30)
                s_buf[pair, base : base + BALANCE_TOKENS] = held
                high = jnp.max(held.reshape(tiles, 8, PAIR), axis=0)
                tops[pair] = high if base == 0 else jnp.maximum(tops[pair], high)

        def settle(pair):
            shifts[pair] = jnp.max(tops[pair], axis=0, keepdims=True) * SCORE_SCALE

        def weigh(pair, chunk):
            for part in (lower, upper):
                base = chunk * PAIR + part.start
                keys = slice(base, base + BALANCE_TOKENS)
                weight = jnp.exp(s_buf[pair, keys] * SCORE_SCALE - shifts[pair])
                added = jnp.sum(weight.reshape(tiles, 8, PAIR), axis=0)
                totals[pair] = added if base == 0 else totals[pair] + added
                p_buf[pair, keys] = weight.astype(p_buf.dtype)

        def finish(pair):
            every = slice(0, chunks * PAIR)
            mixed = jnp.dot(
                vt_buf[:, every], p_buf[pair, every], preferred_element_type=jnp.float32
            )
            scaled = mixed * (1.0 / jnp.sum(totals[pair], axis=0, keepdims=True))
            scaled = scaled.astype(o_buf.dtype)
            for member in range(0, PAIR, HEAD_WIDTH):
                piece = scaled[:, member : member + HEAD_WIDTH].T
                o_buf[side, :, pair * PAIR + member : pair * PAIR + member + HEAD_WIDTH] = piece

        for chunk in range(chunks):
            score(0, chunk)
            vt_buf[:, chunk * PAIR : (chunk + 1) * PAIR] = v_buf[rows_of(chunk), lanes].T
        for pair in range(pairs):
            settle(pair)
            for chunk in range(chunks):
                if pair + 1 < pairs:
                    score(pair + 1, chunk)
                weigh(pair, chunk)
            if pair:
                finish(pair - 1)
        finish(pairs - 1)

    def o_copy(task):
        side = task % 2
        lanes = pl.ds(
            pl.multiple_of((low + task % heads) * GROUP_WIDTH, GROUP_WIDTH), GROUP_WIDTH
        )
        rows = block_rows(info[task // heads, 0])
        return pltpu.make_async_copy(o_buf.at[side], out_ref.at[rows, lanes], o_sem.at[side])

    @pl.loop(0, tasks)
    def _(task):
        @pl.when(task + 1 < tasks)
        def _():
            q_start(task + 1)

        q_copy(task, 0).wait()

        @pl.when(task >= 2)
        def _():
            o_copy(task - 2).wait()

        piece = task // heads
        half, start, skipped = info[piece, 1], info[piece, 2], info[piece, 3]
        for chunks in range(1, MOST_BLK * BALANCE_TOKENS // PAIR + 1):

            @pl.when(half == chunks)
            def _():
                one_task(chunks, task % 2, task % heads, start, skipped)

        o_copy(task).start()

    for task in range(max(tasks - 2, 0), tasks):
        o_copy(jnp.int32(task)).wait()


def attend(source, docs, pieces, windows, base, shape, blocks, steps, low, heads):
    hbm = pl.BlockSpec(memory_space=pltpu.HBM)
    smem = pl.BlockSpec(memory_space=pltpu.SMEM)
    operands = [source, docs, *pieces, *windows] + ([] if base is None else [base])
    reach = MOST_BLK * BALANCE_TOKENS
    held = 3 * blocks * BALANCE_TOKENS
    dtype = pieces[0].dtype
    return pl.pallas_call(
        functools.partial(attend_kernel, blocks, steps, low, heads),
        out_shape=jax.ShapeDtypeStruct(shape, dtype),
        in_specs=[smem, smem] + [hbm] * (len(operands) - 2),
        out_specs=hbm,
        scratch_shapes=[
            pltpu.VMEM((2, GROUP_WIDTH, BALANCE_TOKENS), dtype),
            pltpu.VMEM((held, heads * HEAD_WIDTH), dtype),
            pltpu.VMEM((held, heads * HEAD_WIDTH), dtype),
            pltpu.VMEM((2, BALANCE_TOKENS, GROUP_WIDTH), dtype),
            pltpu.VMEM((GROUP_WIDTH // PAIR, reach, PAIR), jnp.float32),
            pltpu.VMEM((GROUP_WIDTH // PAIR, reach, PAIR), dtype),
            pltpu.VMEM((HEAD_WIDTH, reach), dtype),
            pltpu.SMEM((len(steps), 4), jnp.int32),
            pltpu.SemaphoreType.DMA((2,)),
            pltpu.SemaphoreType.DMA((3 * blocks, 2)),
            pltpu.SemaphoreType.DMA((2,)),
        ],
        input_output_aliases={} if base is None else {len(operands) - 1: 0},
        compiler_params=pltpu.CompilerParams(vmem_limit_bytes=VMEM_LIMIT),
        cost_estimate=pl.CostEstimate(flops=0, bytes_accessed=2**10, transcendentals=0),
        name=f"attend_{steps[0]}_{low}",
    )(*operands)


def on_device(query_matrix, key_matrix, value_matrix, block_source, documents):
    dp_count = lax.axis_size("dp")
    sp_count = lax.axis_size("sp")
    sp = lax.axis_index("sp")
    tok_dev = query_matrix.shape[1]
    blocks = tok_dev // BALANCE_TOKENS
    assert blocks == dp_count == 4
    q = query_matrix.reshape(tok_dev, QUERY_HEADS * HEAD_WIDTH)
    k = key_matrix.reshape(tok_dev, KEY_VALUE_HEADS * HEAD_WIDTH)
    v = value_matrix.reshape(tok_dev, KEY_VALUE_HEADS * HEAD_WIDTH)

    def swap_dp(x, step):
        return lax.ppermute(x, "dp", [(i, i ^ step) for i in range(dp_count)])

    def ahead(x):
        return lax.ppermute(x, "sp", [(i, i + 2) for i in range(sp_count - 2)])

    def swap_core(mine, theirs):
        x = jnp.where(sp % 2 == 0, mine, theirs)
        return lax.ppermute(x, "sp", [(i, i ^ 1) for i in range(sp_count)])

    def pack(source, step, low, heads):
        return pack_q(source, q, blocks, step, low, heads)

    tie = lax.optimization_barrier
    all_heads = KEY_VALUE_HEADS
    cut = 6 * KEY_VALUE_HEADS // 8
    own = list(pack_kv(block_source, k, v, blocks))
    own[1:] = [swap_dp(own[step], step) for step in range(1, blocks)]
    two = [None] * blocks
    two[0] = ahead(own[0])
    near = [pack(block_source, step, 0, all_heads) for step in (1, 2)]
    near, source, own[1] = tie((near, block_source, own[1]))
    two[1] = ahead(own[1])
    kept = pack(source, 0, 0, all_heads)
    far = [pack(source, 3, 0, cut), pack(source, 3, cut, all_heads - cut)]
    near, kept, far, own[2], own[3], two[0], two[1] = tie(
        (near, kept, far, own[2], own[3], two[0], two[1])
    )
    near = [swap_dp(x, step) for step, x in enumerate(near, 1)]
    two[2], two[3] = ahead(own[2]), ahead(own[3])
    one = [swap_core(mine, theirs) for mine, theirs in zip(own, two)]
    windows = [*two, *one, *own]

    call = functools.partial(attend, block_source, documents, windows=windows, shape=q.shape)
    out = call([kept], base=None, blocks=blocks, steps=(0,), low=0, heads=all_heads)
    far, near, out = tie((far, near, out))
    far = [swap_dp(x, 3) for x in far]
    out = call(near, base=out, blocks=blocks, steps=(1, 2), low=0, heads=all_heads)
    out = call(far[:1], base=out, blocks=blocks, steps=(3,), low=0, heads=cut)
    out = call(far[1:], base=out, blocks=blocks, steps=(3,), low=cut, heads=all_heads - cut)
    return out.reshape(1, tok_dev, QUERY_HEADS * HEAD_WIDTH)


def solution(mesh):
    placed = (P("dp", "sp", None), P("dp", "sp", None), P("dp", "sp", None), P(), P("dp", None))
    return jax.shard_map(
        on_device, mesh=mesh, in_specs=placed, out_specs=P("dp", "sp", None), check_vma=False
    )
```

```python
import functools
import math

import jax
import jax.numpy as jnp
from jax import lax
from jax.experimental import pallas as pl
from jax.experimental.pallas import tpu as pltpu
from jax.sharding import PartitionSpec as P

QUERY_HEADS = 64
KEY_VALUE_HEADS = 8
HEAD_WIDTH = 128
BALANCE_TOKENS = 128
MOST_BLK = 8
GROUP_HEADS = QUERY_HEADS // KEY_VALUE_HEADS
GROUP_WIDTH = GROUP_HEADS * HEAD_WIDTH
PAIR = 256
EXP2_SCALE = math.log2(math.e) / math.sqrt(HEAD_WIDTH)
SUM_ROWS = 16
VMEM_LIMIT = 64 * 1024 * 1024


def position():
    return lax.axis_index("dp"), lax.axis_index("sp")


def leaving_slot(source_ref, blocks, dp, sp, other):
    slot = jnp.int32(0)
    for place in range(blocks):
        entry = source_ref[sp, other * blocks + place]
        slot = jnp.where(entry // blocks == dp, entry % blocks, slot)
    return slot


def landing_slot(source_ref, blocks, dp, sp, other):
    slot = jnp.int32(0)
    for place in range(blocks):
        entry = source_ref[sp, dp * blocks + place]
        slot = jnp.where(entry // blocks == other, place, slot)
    return slot


def block_rows(slot):
    return pl.ds(pl.multiple_of(slot * BALANCE_TOKENS, BALANCE_TOKENS), BALANCE_TOKENS)


def pack_kv_kernel(blocks, source_ref, k_ref, v_ref, *rest):
    outs, (buf, sem) = rest[:blocks], rest[blocks:]
    dp, sp = position()
    reads, writes = [], []
    for order, step in enumerate([*range(1, blocks), 0]):
        rows = block_rows(leaving_slot(source_ref, blocks, dp, sp, dp ^ step))
        for which, ref in enumerate((k_ref, v_ref)):
            place, number = buf.at[order, which], 2 * order + which
            reads.append(pltpu.make_async_copy(ref.at[rows], place, sem.at[number, 0]))
            writes.append(
                pltpu.make_async_copy(place, outs[step].at[which], sem.at[number, 1])
            )
    for copy in reads:
        copy.start()
    for read, write in zip(reads, writes):
        read.wait()
        write.start()
    for copy in writes:
        copy.wait()


def pack_kv(source, k, v, blocks):
    width = k.shape[1]
    hbm = pl.BlockSpec(memory_space=pltpu.HBM)
    return pl.pallas_call(
        functools.partial(pack_kv_kernel, blocks),
        out_shape=[jax.ShapeDtypeStruct((2, BALANCE_TOKENS, width), k.dtype)] * blocks,
        in_specs=[pl.BlockSpec(memory_space=pltpu.SMEM), hbm, hbm],
        out_specs=[hbm] * blocks,
        scratch_shapes=[
            pltpu.VMEM((blocks, 2, BALANCE_TOKENS, width), k.dtype),
            pltpu.SemaphoreType.DMA((2 * blocks, 2)),
        ],
        compiler_params=pltpu.CompilerParams(vmem_limit_bytes=VMEM_LIMIT),
        cost_estimate=pl.CostEstimate(flops=0, bytes_accessed=4 * 2**20, transcendentals=0),
        name="pack_kv",
    )(source, k, v)


def pack_q_kernel(blocks, step, first, source_ref, q_ref, out_ref, buf, turned, sem):
    dp, sp = position()
    rows = block_rows(leaving_slot(source_ref, blocks, dp, sp, dp ^ step))
    groups = buf.shape[0]

    def read(group):
        lanes = pl.ds(pl.multiple_of(first + group * GROUP_WIDTH, GROUP_WIDTH), GROUP_WIDTH)
        return pltpu.make_async_copy(q_ref.at[rows, lanes], buf.at[group], sem.at[group, 0])

    def write(group):
        span = pl.ds(pl.multiple_of(group * GROUP_WIDTH, GROUP_WIDTH), GROUP_WIDTH)
        return pltpu.make_async_copy(turned.at[group], out_ref.at[span], sem.at[group, 1])

    @pl.loop(0, groups)
    def _(group):
        read(group).start()

    @pl.loop(0, groups)
    def _(group):
        read(group).wait()
        for head in range(GROUP_HEADS):
            span = slice(head * HEAD_WIDTH, (head + 1) * HEAD_WIDTH)
            turned[group, span] = buf[group, :, span].T
        write(group).start()

    @pl.loop(0, groups)
    def _(group):
        write(group).wait()


def pack_q(source, q, blocks, step, first_head, heads):
    width = heads * GROUP_WIDTH
    hbm = pl.BlockSpec(memory_space=pltpu.HBM)
    return pl.pallas_call(
        functools.partial(pack_q_kernel, blocks, step, first_head * GROUP_WIDTH),
        out_shape=jax.ShapeDtypeStruct((width, BALANCE_TOKENS), q.dtype),
        in_specs=[pl.BlockSpec(memory_space=pltpu.SMEM), hbm],
        out_specs=hbm,
        scratch_shapes=[
            pltpu.VMEM((heads, BALANCE_TOKENS, GROUP_WIDTH), q.dtype),
            pltpu.VMEM((heads, GROUP_WIDTH, BALANCE_TOKENS), q.dtype),
            pltpu.SemaphoreType.DMA((heads, 2)),
        ],
        compiler_params=pltpu.CompilerParams(vmem_limit_bytes=VMEM_LIMIT),
        cost_estimate=pl.CostEstimate(
            flops=0, bytes_accessed=4 * width * BALANCE_TOKENS, transcendentals=0
        ),
        name=f"pack_q_{step}_{first_head}",
    )(source, q)


def attend_kernel(blocks, steps, low, heads, *refs):
    count = len(steps)
    source_ref, doc_ref, *q_refs = refs[: 2 + count]
    windows = refs[2 + count : 2 + count + 3 * blocks]
    out_ref, q_buf, k_buf, v_buf, o_buf, s_buf, vt_buf, info, q_sem, kv_sem, o_sem = refs[-11:]
    tasks = count * heads
    dp, sp = position()

    def q_copy(task, which):
        rows = pl.ds(pl.multiple_of((task % heads) * GROUP_WIDTH, GROUP_WIDTH), GROUP_WIDTH)
        side = task % 2
        return pltpu.make_async_copy(q_refs[which].at[rows], q_buf.at[side], q_sem.at[side])

    def q_start(task):
        for which in range(count):

            @pl.when(task // heads == which)
            def _():
                q_copy(task, which).start()

    q_start(jnp.int32(0))

    origin = (sp - 2) * blocks
    lowest = jnp.int32(3 * blocks)
    highest = jnp.int32(0)
    for which, step in enumerate(steps):
        slot = landing_slot(source_ref, blocks, dp, sp, dp ^ step)
        block = sp * blocks + slot
        length = jnp.int32(1)
        for back in range(1, MOST_BLK):
            same = doc_ref[0, jnp.maximum(block - back, 0)] == doc_ref[0, block]
            length = length + ((block >= back) & same).astype(jnp.int32)
        half = (length + 1) // 2
        start = 2 * blocks + slot + 1 - 2 * half
        info[which, 0] = slot
        info[which, 1] = half
        info[which, 2] = start * BALANCE_TOKENS
        info[which, 3] = (length % 2) * BALANCE_TOKENS
        lowest = jnp.minimum(lowest, start)
        highest = jnp.maximum(highest, 2 * blocks + slot)

    kv_lanes = pl.ds(low * HEAD_WIDTH, heads * HEAD_WIDTH)

    def window_copies(number):
        column, step = sp - 2 + number // blocks, number % blocks
        known = jnp.maximum(column, 0)
        place = number // blocks * blocks + landing_slot(source_ref, blocks, dp, known, dp ^ step)
        wanted = (column >= 0) & (place >= lowest) & (place <= highest)
        rows = block_rows(place)
        return wanted, [
            pltpu.make_async_copy(
                windows[number].at[which, :, kv_lanes],
                buf.at[rows],
                kv_sem.at[number, which],
            )
            for which, buf in enumerate((k_buf, v_buf))
        ]

    fetches = [window_copies(number) for number in range(3 * blocks)]
    for wanted, copies in fetches:

        @pl.when(wanted)
        def _():
            for copy in copies:
                copy.start()

    @pl.when(lowest + origin < 0)
    def _():
        rows = block_rows(lowest)
        k_buf[rows] = jnp.zeros((BALANCE_TOKENS, k_buf.shape[1]), k_buf.dtype)
        v_buf[rows] = jnp.zeros((BALANCE_TOKENS, v_buf.shape[1]), v_buf.dtype)

    vt_buf[HEAD_WIDTH:] = jnp.ones((SUM_ROWS, vt_buf.shape[1]), vt_buf.dtype)

    for wanted, copies in fetches:

        @pl.when(wanted)
        def _():
            for copy in copies:
                copy.wait()

    pairs = GROUP_WIDTH // PAIR
    tiles = BALANCE_TOKENS // 8

    def one_task(chunks, side, head, start, skipped):
        lanes = pl.ds(pl.multiple_of(head * HEAD_WIDTH, HEAD_WIDTH), HEAD_WIDTH)
        span = pl.ds(pl.multiple_of(start, BALANCE_TOKENS), chunks * PAIR)
        lower, upper = slice(0, BALANCE_TOKENS), slice(BALANCE_TOKENS, PAIR)
        row = lax.broadcasted_iota(jnp.int32, (BALANCE_TOKENS, PAIR), 0)
        column = lax.broadcasted_iota(jnp.int32, (BALANCE_TOKENS, PAIR), 1)
        allowed = row <= (column & (BALANCE_TOKENS - 1))
        tops = [None] * pairs
        sums = [None] * pairs
        shifts = [None] * pairs

        def rows_of(chunk):
            return pl.ds(pl.multiple_of(start + chunk * PAIR, BALANCE_TOKENS), PAIR)

        def score(pair, chunk):
            parts = [
                q_buf[side, pair * PAIR + member : pair * PAIR + member + HEAD_WIDTH]
                for member in range(0, PAIR, HEAD_WIDTH)
            ]
            whole = jnp.dot(
                k_buf[rows_of(chunk), lanes],
                jnp.concatenate(parts, axis=1),
                preferred_element_type=jnp.float32,
            )
            for part in (lower, upper):
                base = chunk * PAIR + part.start
                held = whole[part]
                if chunk == 0 and part is lower:
                    held = jnp.where(skipped > 0, -1e30, held)
                if chunk == chunks - 1 and part is upper:
                    held = jnp.where(allowed, held, -1e30)
                s_buf[pair, base : base + BALANCE_TOKENS] = held
                high = jnp.max(held.reshape(tiles, 8, PAIR), axis=0)
                tops[pair] = high if base == 0 else jnp.maximum(tops[pair], high)

        def settle(pair):
            shifts[pair] = jnp.max(tops[pair], axis=0, keepdims=True) * EXP2_SCALE

        def mix(pair, chunk):
            keys = slice(chunk * PAIR, (chunk + 1) * PAIR)
            weight = jnp.exp2(s_buf[pair, keys] * EXP2_SCALE - shifts[pair])
            mixed = jnp.dot(
                vt_buf[:, keys],
                weight.astype(jnp.bfloat16),
                preferred_element_type=jnp.float32,
            )
            sums[pair] = mixed if chunk == 0 else sums[pair] + mixed

        def finish(pair):
            total = sums[pair][HEAD_WIDTH : HEAD_WIDTH + 1]
            scaled = (sums[pair][:HEAD_WIDTH] * (1.0 / total)).astype(o_buf.dtype)
            for member in range(0, PAIR, HEAD_WIDTH):
                piece = scaled[:, member : member + HEAD_WIDTH].T
                o_buf[side, :, pair * PAIR + member : pair * PAIR + member + HEAD_WIDTH] = piece

        for chunk in range(chunks):
            score(0, chunk)
            vt_buf[:HEAD_WIDTH, chunk * PAIR : (chunk + 1) * PAIR] = v_buf[rows_of(chunk), lanes].T
        for pair in range(pairs):
            settle(pair)
            for chunk in range(chunks):
                if pair + 1 < pairs:
                    score(pair + 1, chunk)
                mix(pair, chunk)
            if pair:
                finish(pair - 1)
        finish(pairs - 1)

    def o_copy(task):
        side = task % 2
        lanes = pl.ds(
            pl.multiple_of((low + task % heads) * GROUP_WIDTH, GROUP_WIDTH), GROUP_WIDTH
        )
        rows = block_rows(info[task // heads, 0])
        return pltpu.make_async_copy(o_buf.at[side], out_ref.at[rows, lanes], o_sem.at[side])

    @pl.loop(0, tasks)
    def _(task):
        @pl.when(task + 1 < tasks)
        def _():
            q_start(task + 1)

        q_copy(task, 0).wait()

        @pl.when(task >= 2)
        def _():
            o_copy(task - 2).wait()

        piece = task // heads
        half, start, skipped = info[piece, 1], info[piece, 2], info[piece, 3]
        for chunks in range(1, MOST_BLK * BALANCE_TOKENS // PAIR + 1):

            @pl.when(half == chunks)
            def _():
                one_task(chunks, task % 2, task % heads, start, skipped)

        o_copy(task).start()

    for task in range(max(tasks - 2, 0), tasks):
        o_copy(jnp.int32(task)).wait()


def attend(source, docs, pieces, windows, base, shape, blocks, steps, low, heads):
    hbm = pl.BlockSpec(memory_space=pltpu.HBM)
    smem = pl.BlockSpec(memory_space=pltpu.SMEM)
    operands = [source, docs, *pieces, *windows] + ([] if base is None else [base])
    reach = MOST_BLK * BALANCE_TOKENS
    held = 3 * blocks * BALANCE_TOKENS
    dtype = pieces[0].dtype
    return pl.pallas_call(
        functools.partial(attend_kernel, blocks, steps, low, heads),
        out_shape=jax.ShapeDtypeStruct(shape, dtype),
        in_specs=[smem, smem] + [hbm] * (len(operands) - 2),
        out_specs=hbm,
        scratch_shapes=[
            pltpu.VMEM((2, GROUP_WIDTH, BALANCE_TOKENS), dtype),
            pltpu.VMEM((held, heads * HEAD_WIDTH), dtype),
            pltpu.VMEM((held, heads * HEAD_WIDTH), dtype),
            pltpu.VMEM((2, BALANCE_TOKENS, GROUP_WIDTH), dtype),
            pltpu.VMEM((GROUP_WIDTH // PAIR, reach, PAIR), jnp.float32),
            pltpu.VMEM((HEAD_WIDTH + SUM_ROWS, reach), dtype),
            pltpu.SMEM((len(steps), 4), jnp.int32),
            pltpu.SemaphoreType.DMA((2,)),
            pltpu.SemaphoreType.DMA((3 * blocks, 2)),
            pltpu.SemaphoreType.DMA((2,)),
        ],
        input_output_aliases={} if base is None else {len(operands) - 1: 0},
        compiler_params=pltpu.CompilerParams(vmem_limit_bytes=VMEM_LIMIT),
        cost_estimate=pl.CostEstimate(flops=0, bytes_accessed=2**10, transcendentals=0),
        name=f"attend_{steps[0]}_{low}",
    )(*operands)


def on_device(query_matrix, key_matrix, value_matrix, block_source, documents):
    dp_count = lax.axis_size("dp")
    sp_count = lax.axis_size("sp")
    sp = lax.axis_index("sp")
    tok_dev = query_matrix.shape[1]
    blocks = tok_dev // BALANCE_TOKENS
    assert blocks == dp_count == 4
    q = query_matrix.reshape(tok_dev, QUERY_HEADS * HEAD_WIDTH)
    k = key_matrix.reshape(tok_dev, KEY_VALUE_HEADS * HEAD_WIDTH)
    v = value_matrix.reshape(tok_dev, KEY_VALUE_HEADS * HEAD_WIDTH)

    def swap_dp(x, step):
        return lax.ppermute(x, "dp", [(i, i ^ step) for i in range(dp_count)])

    def ahead(x):
        return lax.ppermute(x, "sp", [(i, i + 2) for i in range(sp_count - 2)])

    def swap_core(mine, theirs):
        x = jnp.where(sp % 2 == 0, mine, theirs)
        return lax.ppermute(x, "sp", [(i, i ^ 1) for i in range(sp_count)])

    def pack(source, step, low, heads):
        return pack_q(source, q, blocks, step, low, heads)

    tie = lax.optimization_barrier
    all_heads = KEY_VALUE_HEADS
    cut = 6 * KEY_VALUE_HEADS // 8
    own = list(pack_kv(block_source, k, v, blocks))
    own[1:] = [swap_dp(own[step], step) for step in range(1, blocks)]
    two = [None] * blocks
    two[0] = ahead(own[0])
    near = [pack(block_source, step, 0, all_heads) for step in (1, 2)]
    near, source, own[1] = tie((near, block_source, own[1]))
    two[1] = ahead(own[1])
    kept = pack(source, 0, 0, all_heads)
    far = [pack(source, 3, 0, cut), pack(source, 3, cut, all_heads - cut)]
    near, kept, far, own[2], own[3], two[0], two[1] = tie(
        (near, kept, far, own[2], own[3], two[0], two[1])
    )
    near = [swap_dp(x, step) for step, x in enumerate(near, 1)]
    two[2], two[3] = ahead(own[2]), ahead(own[3])
    one = [swap_core(mine, theirs) for mine, theirs in zip(own, two)]
    windows = [*two, *one, *own]

    call = functools.partial(attend, block_source, documents, windows=windows, shape=q.shape)
    out = call([kept], base=None, blocks=blocks, steps=(0,), low=0, heads=all_heads)
    far, near, out = tie((far, near, out))
    far = [swap_dp(x, 3) for x in far]
    out = call(near, base=out, blocks=blocks, steps=(1, 2), low=0, heads=all_heads)
    out = call(far[:1], base=out, blocks=blocks, steps=(3,), low=0, heads=cut)
    out = call(far[1:], base=out, blocks=blocks, steps=(3,), low=cut, heads=all_heads - cut)
    return out.reshape(1, tok_dev, QUERY_HEADS * HEAD_WIDTH)


def solution(mesh):
    placed = (P("dp", "sp", None), P("dp", "sp", None), P("dp", "sp", None), P(), P("dp", None))
    return jax.shard_map(
        on_device, mesh=mesh, in_specs=placed, out_specs=P("dp", "sp", None), check_vma=False
    )
```

```python
import functools
import math

import jax
import jax.numpy as jnp
from jax import lax
from jax.experimental import pallas as pl
from jax.experimental.pallas import tpu as pltpu
from jax.sharding import PartitionSpec as P

QUERY_HEADS = 64
KEY_VALUE_HEADS = 8
HEAD_WIDTH = 128
BALANCE_TOKENS = 128
MOST_BLK = 8
GROUP_HEADS = QUERY_HEADS // KEY_VALUE_HEADS
GROUP_WIDTH = GROUP_HEADS * HEAD_WIDTH
PAIR = 256
EXP2_SCALE = math.log2(math.e) / math.sqrt(HEAD_WIDTH)
VMEM_LIMIT = 64 * 1024 * 1024


def position():
    return lax.axis_index("dp"), lax.axis_index("sp")


def leaving_slot(source_ref, blocks, dp, sp, other):
    slot = jnp.int32(0)
    for place in range(blocks):
        entry = source_ref[sp, other * blocks + place]
        slot = jnp.where(entry // blocks == dp, entry % blocks, slot)
    return slot


def landing_slot(source_ref, blocks, dp, sp, other):
    slot = jnp.int32(0)
    for place in range(blocks):
        entry = source_ref[sp, dp * blocks + place]
        slot = jnp.where(entry // blocks == other, place, slot)
    return slot


def block_rows(slot):
    return pl.ds(pl.multiple_of(slot * BALANCE_TOKENS, BALANCE_TOKENS), BALANCE_TOKENS)


def pack_kv_kernel(blocks, source_ref, k_ref, v_ref, *rest):
    outs, (buf, sem) = rest[:blocks], rest[blocks:]
    dp, sp = position()
    reads, writes = [], []
    for order, step in enumerate([*range(1, blocks), 0]):
        rows = block_rows(leaving_slot(source_ref, blocks, dp, sp, dp ^ step))
        for which, ref in enumerate((k_ref, v_ref)):
            place, number = buf.at[order, which], 2 * order + which
            reads.append(pltpu.make_async_copy(ref.at[rows], place, sem.at[number, 0]))
            writes.append(
                pltpu.make_async_copy(place, outs[step].at[which], sem.at[number, 1])
            )
    for copy in reads:
        copy.start()
    for read, write in zip(reads, writes):
        read.wait()
        write.start()
    for copy in writes:
        copy.wait()


def pack_kv(source, k, v, blocks):
    width = k.shape[1]
    hbm = pl.BlockSpec(memory_space=pltpu.HBM)
    return pl.pallas_call(
        functools.partial(pack_kv_kernel, blocks),
        out_shape=[jax.ShapeDtypeStruct((2, BALANCE_TOKENS, width), k.dtype)] * blocks,
        in_specs=[pl.BlockSpec(memory_space=pltpu.SMEM), hbm, hbm],
        out_specs=[hbm] * blocks,
        scratch_shapes=[
            pltpu.VMEM((blocks, 2, BALANCE_TOKENS, width), k.dtype),
            pltpu.SemaphoreType.DMA((2 * blocks, 2)),
        ],
        compiler_params=pltpu.CompilerParams(vmem_limit_bytes=VMEM_LIMIT),
        cost_estimate=pl.CostEstimate(flops=0, bytes_accessed=4 * 2**20, transcendentals=0),
        name="pack_kv",
    )(source, k, v)


def pack_q_kernel(blocks, step, first, source_ref, q_ref, out_ref, buf, turned, sem):
    dp, sp = position()
    rows = block_rows(leaving_slot(source_ref, blocks, dp, sp, dp ^ step))
    groups = buf.shape[0]

    def read(group):
        lanes = pl.ds(pl.multiple_of(first + group * GROUP_WIDTH, GROUP_WIDTH), GROUP_WIDTH)
        return pltpu.make_async_copy(q_ref.at[rows, lanes], buf.at[group], sem.at[group, 0])

    def write(group):
        span = pl.ds(pl.multiple_of(group * GROUP_WIDTH, GROUP_WIDTH), GROUP_WIDTH)
        return pltpu.make_async_copy(turned.at[group], out_ref.at[span], sem.at[group, 1])

    @pl.loop(0, groups)
    def _(group):
        read(group).start()

    @pl.loop(0, groups)
    def _(group):
        read(group).wait()
        for head in range(GROUP_HEADS):
            span = slice(head * HEAD_WIDTH, (head + 1) * HEAD_WIDTH)
            turned[group, span] = buf[group, :, span].T
        write(group).start()

    @pl.loop(0, groups)
    def _(group):
        write(group).wait()


def pack_q(source, q, blocks, step, first_head, heads):
    width = heads * GROUP_WIDTH
    hbm = pl.BlockSpec(memory_space=pltpu.HBM)
    return pl.pallas_call(
        functools.partial(pack_q_kernel, blocks, step, first_head * GROUP_WIDTH),
        out_shape=jax.ShapeDtypeStruct((width, BALANCE_TOKENS), q.dtype),
        in_specs=[pl.BlockSpec(memory_space=pltpu.SMEM), hbm],
        out_specs=hbm,
        scratch_shapes=[
            pltpu.VMEM((heads, BALANCE_TOKENS, GROUP_WIDTH), q.dtype),
            pltpu.VMEM((heads, GROUP_WIDTH, BALANCE_TOKENS), q.dtype),
            pltpu.SemaphoreType.DMA((heads, 2)),
        ],
        compiler_params=pltpu.CompilerParams(vmem_limit_bytes=VMEM_LIMIT),
        cost_estimate=pl.CostEstimate(
            flops=0, bytes_accessed=4 * width * BALANCE_TOKENS, transcendentals=0
        ),
        name=f"pack_q_{step}_{first_head}",
    )(source, q)


def attend_kernel(blocks, steps, low, heads, rest, *refs):
    count = len(steps)
    whole = (count - (rest > 0)) * heads
    tasks = whole + rest
    source_ref, doc_ref, *q_refs = refs[: 2 + count]
    windows = refs[2 + count : 2 + count + 3 * blocks]
    out_ref, q_buf, k_buf, v_buf, o_buf, s_buf, vt_buf, info, q_sem, kv_sem, o_sem = refs[-11:]
    dp, sp = position()

    def piece_of(task):
        return jnp.where(task < whole, task // heads, count - 1)

    def head_of(task):
        return jnp.where(task < whole, task % heads, task - whole + heads - rest)

    def q_copy(task, which):
        rows = pl.ds(pl.multiple_of(head_of(task) * GROUP_WIDTH, GROUP_WIDTH), GROUP_WIDTH)
        side = task % 2
        return pltpu.make_async_copy(q_refs[which].at[rows], q_buf.at[side], q_sem.at[side])

    def q_start(task):
        for which in range(count):

            @pl.when(piece_of(task) == which)
            def _():
                q_copy(task, which).start()

    q_start(jnp.int32(0))

    origin = (sp - 2) * blocks
    lowest = jnp.int32(3 * blocks)
    highest = jnp.int32(0)
    for which, step in enumerate(steps):
        slot = landing_slot(source_ref, blocks, dp, sp, dp ^ step)
        block = sp * blocks + slot
        length = jnp.int32(1)
        for back in range(1, MOST_BLK):
            same = doc_ref[0, jnp.maximum(block - back, 0)] == doc_ref[0, block]
            length = length + ((block >= back) & same).astype(jnp.int32)
        half = (length + 1) // 2
        start = 2 * blocks + slot + 1 - 2 * half
        info[which, 0] = slot
        info[which, 1] = half
        info[which, 2] = start * BALANCE_TOKENS
        info[which, 3] = (length % 2) * BALANCE_TOKENS
        lowest = jnp.minimum(lowest, start)
        highest = jnp.maximum(highest, 2 * blocks + slot)

    kv_lanes = pl.ds(low * HEAD_WIDTH, heads * HEAD_WIDTH)

    def window_copies(number):
        column, step = sp - 2 + number // blocks, number % blocks
        known = jnp.maximum(column, 0)
        place = number // blocks * blocks + landing_slot(source_ref, blocks, dp, known, dp ^ step)
        wanted = (column >= 0) & (place >= lowest) & (place <= highest)
        rows = block_rows(place)
        return wanted, [
            pltpu.make_async_copy(
                windows[number].at[which, :, kv_lanes],
                buf.at[rows],
                kv_sem.at[number, which],
            )
            for which, buf in enumerate((k_buf, v_buf))
        ]

    fetches = [window_copies(number) for number in range(3 * blocks)]
    for wanted, copies in fetches:

        @pl.when(wanted)
        def _():
            for copy in copies:
                copy.start()

    @pl.when(lowest + origin < 0)
    def _():
        rows = block_rows(lowest)
        k_buf[rows] = jnp.zeros((BALANCE_TOKENS, k_buf.shape[1]), k_buf.dtype)
        v_buf[rows] = jnp.zeros((BALANCE_TOKENS, v_buf.shape[1]), v_buf.dtype)

    for wanted, copies in fetches:

        @pl.when(wanted)
        def _():
            for copy in copies:
                copy.wait()

    pairs = GROUP_WIDTH // PAIR
    tiles = BALANCE_TOKENS // 8

    def one_task(chunks, side, head, start, skipped):
        lanes = pl.ds(pl.multiple_of(head * HEAD_WIDTH, HEAD_WIDTH), HEAD_WIDTH)
        span = pl.ds(pl.multiple_of(start, BALANCE_TOKENS), chunks * PAIR)
        lower, upper = slice(0, BALANCE_TOKENS), slice(BALANCE_TOKENS, PAIR)
        row = lax.broadcasted_iota(jnp.int32, (BALANCE_TOKENS, PAIR), 0)
        column = lax.broadcasted_iota(jnp.int32, (BALANCE_TOKENS, PAIR), 1)
        allowed = row <= (column & (BALANCE_TOKENS - 1))
        tops = [None] * pairs
        totals = [None] * pairs
        sums = [None] * pairs
        shifts = [None] * pairs

        def rows_of(chunk):
            return pl.ds(pl.multiple_of(start + chunk * PAIR, BALANCE_TOKENS), PAIR)

        def score(pair, chunk):
            parts = [
                q_buf[side, pair * PAIR + member : pair * PAIR + member + HEAD_WIDTH]
                for member in range(0, PAIR, HEAD_WIDTH)
            ]
            product = jnp.dot(
                k_buf[rows_of(chunk), lanes],
                jnp.concatenate(parts, axis=1),
                preferred_element_type=jnp.float32,
            )
            for part in (lower, upper):
                base = chunk * PAIR + part.start
                held = product[part]
                if chunk == 0 and part is lower:
                    held = jnp.where(skipped > 0, -1e30, held)
                if chunk == chunks - 1 and part is upper:
                    held = jnp.where(allowed, held, -1e30)
                s_buf[pair, base : base + BALANCE_TOKENS] = held
                high = jnp.max(held.reshape(tiles, 8, PAIR), axis=0)
                tops[pair] = high if base == 0 else jnp.maximum(tops[pair], high)

        def settle(pair):
            shifts[pair] = jnp.max(tops[pair], axis=0, keepdims=True) * EXP2_SCALE

        def mix(pair, chunk):
            keys = slice(chunk * PAIR, (chunk + 1) * PAIR)
            weight = jnp.exp2(s_buf[pair, keys] * EXP2_SCALE - shifts[pair])
            mixed = jnp.dot(
                vt_buf[:, keys],
                weight.astype(jnp.bfloat16),
                preferred_element_type=jnp.float32,
            )
            added = jnp.sum(weight.reshape(PAIR // 8, 8, PAIR), axis=0)
            totals[pair] = added if chunk == 0 else totals[pair] + added
            sums[pair] = mixed if chunk == 0 else sums[pair] + mixed

        def finish(pair):
            scaled = sums[pair] * (1.0 / jnp.sum(totals[pair], axis=0, keepdims=True))
            scaled = scaled.astype(o_buf.dtype)
            for member in range(0, PAIR, HEAD_WIDTH):
                piece = scaled[:, member : member + HEAD_WIDTH].T
                o_buf[side, :, pair * PAIR + member : pair * PAIR + member + HEAD_WIDTH] = piece

        for chunk in range(chunks):
            score(0, chunk)
            vt_buf[:, chunk * PAIR : (chunk + 1) * PAIR] = v_buf[rows_of(chunk), lanes].T
        for pair in range(pairs):
            settle(pair)
            for chunk in range(chunks):
                if pair + 1 < pairs:
                    score(pair + 1, chunk)
                mix(pair, chunk)
            if pair:
                finish(pair - 1)
        finish(pairs - 1)

    def o_copy(task):
        side = task % 2
        lanes = pl.ds(
            pl.multiple_of((low + head_of(task)) * GROUP_WIDTH, GROUP_WIDTH), GROUP_WIDTH
        )
        rows = block_rows(info[piece_of(task), 0])
        return pltpu.make_async_copy(o_buf.at[side], out_ref.at[rows, lanes], o_sem.at[side])

    @pl.loop(0, tasks)
    def _(task):
        @pl.when(task + 1 < tasks)
        def _():
            q_start(task + 1)

        q_copy(task, 0).wait()

        @pl.when(task >= 2)
        def _():
            o_copy(task - 2).wait()

        piece = piece_of(task)
        half, start, skipped = info[piece, 1], info[piece, 2], info[piece, 3]
        for chunks in range(1, MOST_BLK * BALANCE_TOKENS // PAIR + 1):

            @pl.when(half == chunks)
            def _():
                one_task(chunks, task % 2, head_of(task), start, skipped)

        o_copy(task).start()

    for task in range(max(tasks - 2, 0), tasks):
        o_copy(jnp.int32(task)).wait()


def attend(source, docs, pieces, windows, base, shape, blocks, steps, low, heads, rest=0):
    hbm = pl.BlockSpec(memory_space=pltpu.HBM)
    smem = pl.BlockSpec(memory_space=pltpu.SMEM)
    operands = [source, docs, *pieces, *windows] + ([] if base is None else [base])
    reach = MOST_BLK * BALANCE_TOKENS
    held = 3 * blocks * BALANCE_TOKENS
    dtype = pieces[0].dtype
    return pl.pallas_call(
        functools.partial(attend_kernel, blocks, steps, low, heads, rest),
        out_shape=jax.ShapeDtypeStruct(shape, dtype),
        in_specs=[smem, smem] + [hbm] * (len(operands) - 2),
        out_specs=hbm,
        scratch_shapes=[
            pltpu.VMEM((2, GROUP_WIDTH, BALANCE_TOKENS), dtype),
            pltpu.VMEM((held, heads * HEAD_WIDTH), dtype),
            pltpu.VMEM((held, heads * HEAD_WIDTH), dtype),
            pltpu.VMEM((2, BALANCE_TOKENS, GROUP_WIDTH), dtype),
            pltpu.VMEM((GROUP_WIDTH // PAIR, reach, PAIR), jnp.float32),
            pltpu.VMEM((HEAD_WIDTH, reach), dtype),
            pltpu.SMEM((len(steps), 4), jnp.int32),
            pltpu.SemaphoreType.DMA((2,)),
            pltpu.SemaphoreType.DMA((3 * blocks, 2)),
            pltpu.SemaphoreType.DMA((2,)),
        ],
        input_output_aliases={} if base is None else {len(operands) - 1: 0},
        compiler_params=pltpu.CompilerParams(vmem_limit_bytes=VMEM_LIMIT),
        cost_estimate=pl.CostEstimate(flops=0, bytes_accessed=2**10, transcendentals=0),
        name=f"attend_{steps[0]}_{low}",
    )(*operands)


def on_device(query_matrix, key_matrix, value_matrix, block_source, documents):
    dp_count = lax.axis_size("dp")
    sp_count = lax.axis_size("sp")
    sp = lax.axis_index("sp")
    tok_dev = query_matrix.shape[1]
    blocks = tok_dev // BALANCE_TOKENS
    assert blocks == dp_count == 4
    q = query_matrix.reshape(tok_dev, QUERY_HEADS * HEAD_WIDTH)
    k = key_matrix.reshape(tok_dev, KEY_VALUE_HEADS * HEAD_WIDTH)
    v = value_matrix.reshape(tok_dev, KEY_VALUE_HEADS * HEAD_WIDTH)

    def swap_dp(x, step):
        return lax.ppermute(x, "dp", [(i, i ^ step) for i in range(dp_count)])

    def ahead(x):
        return lax.ppermute(x, "sp", [(i, i + 2) for i in range(sp_count - 2)])

    def swap_core(mine, theirs):
        x = jnp.where(sp % 2 == 0, mine, theirs)
        return lax.ppermute(x, "sp", [(i, i ^ 1) for i in range(sp_count)])

    def pack(source, step, low, heads):
        return pack_q(source, q, blocks, step, low, heads)

    tie = lax.optimization_barrier
    all_heads = KEY_VALUE_HEADS
    cut = 5 * KEY_VALUE_HEADS // 8
    own = list(pack_kv(block_source, k, v, blocks))
    own[1:] = [swap_dp(own[step], step) for step in range(1, blocks)]
    two = [None] * blocks
    two[0] = ahead(own[0])
    near = [pack(block_source, step, 0, all_heads) for step in (1, 2)]
    near, source, own[1] = tie((near, block_source, own[1]))
    two[1] = ahead(own[1])
    kept = pack(source, 0, 0, all_heads)
    far = [pack(source, 3, 0, cut), pack(source, 3, cut, all_heads - cut)]
    near, kept, far, own[2], own[3], two[0], two[1] = tie(
        (near, kept, far, own[2], own[3], two[0], two[1])
    )
    near = [swap_dp(x, step) for step, x in enumerate(near, 1)]
    two[2], two[3] = ahead(own[2]), ahead(own[3])
    one = [swap_core(mine, theirs) for mine, theirs in zip(own, two)]
    windows = [*two, *one, *own]

    call = functools.partial(attend, block_source, documents, windows=windows, shape=q.shape)
    out = call([kept], base=None, blocks=blocks, steps=(0,), low=0, heads=cut)
    far, near, out = tie((far, near, out))
    far = [swap_dp(x, 3) for x in far]
    out = call(
        [*near, kept],
        base=out,
        blocks=blocks,
        steps=(1, 2, 0),
        low=0,
        heads=all_heads,
        rest=all_heads - cut,
    )
    out = call(far[:1], base=out, blocks=blocks, steps=(3,), low=0, heads=cut)
    out = call(far[1:], base=out, blocks=blocks, steps=(3,), low=cut, heads=all_heads - cut)
    return out.reshape(1, tok_dev, QUERY_HEADS * HEAD_WIDTH)


def solution(mesh):
    placed = (P("dp", "sp", None), P("dp", "sp", None), P("dp", "sp", None), P(), P("dp", None))
    return jax.shard_map(
        on_device, mesh=mesh, in_specs=placed, out_specs=P("dp", "sp", None), check_vma=False
    )
```

```python
import functools
import math

import jax
import jax.numpy as jnp
from jax import lax
from jax.experimental import pallas as pl
from jax.experimental.pallas import tpu as pltpu
from jax.sharding import PartitionSpec as P

QUERY_HEADS = 64
KEY_VALUE_HEADS = 8
HEAD_WIDTH = 128
BALANCE_TOKENS = 128
MOST_BLK = 8
GROUP_HEADS = QUERY_HEADS // KEY_VALUE_HEADS
GROUP_WIDTH = GROUP_HEADS * HEAD_WIDTH
PAIR = 256
EXP2_SCALE = math.log2(math.e) / math.sqrt(HEAD_WIDTH)
VMEM_LIMIT = 64 * 1024 * 1024


def position():
    return lax.axis_index("dp"), lax.axis_index("sp")


def leaving_slot(source_ref, blocks, dp, sp, other):
    slot = jnp.int32(0)
    for place in range(blocks):
        entry = source_ref[sp, other * blocks + place]
        slot = jnp.where(entry // blocks == dp, entry % blocks, slot)
    return slot


def landing_slot(source_ref, blocks, dp, sp, other):
    slot = jnp.int32(0)
    for place in range(blocks):
        entry = source_ref[sp, dp * blocks + place]
        slot = jnp.where(entry // blocks == other, place, slot)
    return slot


def block_rows(slot):
    return pl.ds(pl.multiple_of(slot * BALANCE_TOKENS, BALANCE_TOKENS), BALANCE_TOKENS)


def pack_kv_kernel(blocks, source_ref, k_ref, v_ref, *rest):
    outs, (buf, sem) = rest[:blocks], rest[blocks:]
    dp, sp = position()
    reads, writes = [], []
    for order, step in enumerate([*range(1, blocks), 0]):
        rows = block_rows(leaving_slot(source_ref, blocks, dp, sp, dp ^ step))
        for which, ref in enumerate((k_ref, v_ref)):
            place, number = buf.at[order, which], 2 * order + which
            reads.append(pltpu.make_async_copy(ref.at[rows], place, sem.at[number, 0]))
            writes.append(
                pltpu.make_async_copy(place, outs[step].at[which], sem.at[number, 1])
            )
    for copy in reads:
        copy.start()
    for read, write in zip(reads, writes):
        read.wait()
        write.start()
    for copy in writes:
        copy.wait()


def pack_kv(source, k, v, blocks):
    width = k.shape[1]
    hbm = pl.BlockSpec(memory_space=pltpu.HBM)
    return pl.pallas_call(
        functools.partial(pack_kv_kernel, blocks),
        out_shape=[jax.ShapeDtypeStruct((2, BALANCE_TOKENS, width), k.dtype)] * blocks,
        in_specs=[pl.BlockSpec(memory_space=pltpu.SMEM), hbm, hbm],
        out_specs=[hbm] * blocks,
        scratch_shapes=[
            pltpu.VMEM((blocks, 2, BALANCE_TOKENS, width), k.dtype),
            pltpu.SemaphoreType.DMA((2 * blocks, 2)),
        ],
        compiler_params=pltpu.CompilerParams(vmem_limit_bytes=VMEM_LIMIT),
        cost_estimate=pl.CostEstimate(flops=0, bytes_accessed=4 * 2**20, transcendentals=0),
        name="pack_kv",
    )(source, k, v)


def pack_q_kernel(blocks, step, first, source_ref, q_ref, out_ref, buf, turned, sem):
    dp, sp = position()
    rows = block_rows(leaving_slot(source_ref, blocks, dp, sp, dp ^ step))
    groups = buf.shape[0]

    def read(group):
        lanes = pl.ds(pl.multiple_of(first + group * GROUP_WIDTH, GROUP_WIDTH), GROUP_WIDTH)
        return pltpu.make_async_copy(q_ref.at[rows, lanes], buf.at[group], sem.at[group, 0])

    def write(group):
        span = pl.ds(pl.multiple_of(group * GROUP_WIDTH, GROUP_WIDTH), GROUP_WIDTH)
        return pltpu.make_async_copy(turned.at[group], out_ref.at[span], sem.at[group, 1])

    @pl.loop(0, groups)
    def _(group):
        read(group).start()

    @pl.loop(0, groups)
    def _(group):
        read(group).wait()
        for head in range(GROUP_HEADS):
            span = slice(head * HEAD_WIDTH, (head + 1) * HEAD_WIDTH)
            turned[group, span] = buf[group, :, span].T
        write(group).start()

    @pl.loop(0, groups)
    def _(group):
        write(group).wait()


def pack_q(source, q, blocks, step, first_head, heads):
    width = heads * GROUP_WIDTH
    hbm = pl.BlockSpec(memory_space=pltpu.HBM)
    return pl.pallas_call(
        functools.partial(pack_q_kernel, blocks, step, first_head * GROUP_WIDTH),
        out_shape=jax.ShapeDtypeStruct((width, BALANCE_TOKENS), q.dtype),
        in_specs=[pl.BlockSpec(memory_space=pltpu.SMEM), hbm],
        out_specs=hbm,
        scratch_shapes=[
            pltpu.VMEM((heads, BALANCE_TOKENS, GROUP_WIDTH), q.dtype),
            pltpu.VMEM((heads, GROUP_WIDTH, BALANCE_TOKENS), q.dtype),
            pltpu.SemaphoreType.DMA((heads, 2)),
        ],
        compiler_params=pltpu.CompilerParams(vmem_limit_bytes=VMEM_LIMIT),
        cost_estimate=pl.CostEstimate(
            flops=0, bytes_accessed=4 * width * BALANCE_TOKENS, transcendentals=0
        ),
        name=f"pack_q_{step}_{first_head}",
    )(source, q)


def attend_kernel(blocks, steps, low, heads, rest, *refs):
    count = len(steps)
    whole = (count - (rest > 0)) * heads
    tasks = whole + rest
    source_ref, doc_ref, *q_refs = refs[: 2 + count]
    windows = refs[2 + count : 2 + count + 3 * blocks]
    out_ref, q_buf, k_buf, v_buf, o_buf, s_buf, vt_buf, info, q_sem, kv_sem, o_sem = refs[-11:]
    dp, sp = position()

    def piece_of(task):
        return jnp.where(task < whole, task // heads, count - 1)

    def head_of(task):
        return jnp.where(task < whole, task % heads, task - whole + heads - rest)

    def q_copy(task, which):
        rows = pl.ds(pl.multiple_of(head_of(task) * GROUP_WIDTH, GROUP_WIDTH), GROUP_WIDTH)
        side = task % 2
        return pltpu.make_async_copy(q_refs[which].at[rows], q_buf.at[side], q_sem.at[side])

    def q_start(task):
        for which in range(count):

            @pl.when(piece_of(task) == which)
            def _():
                q_copy(task, which).start()

    q_start(jnp.int32(0))

    origin = (sp - 2) * blocks
    lowest = jnp.int32(3 * blocks)
    highest = jnp.int32(0)
    for which, step in enumerate(steps):
        slot = landing_slot(source_ref, blocks, dp, sp, dp ^ step)
        block = sp * blocks + slot
        length = jnp.int32(1)
        for back in range(1, MOST_BLK):
            same = doc_ref[0, jnp.maximum(block - back, 0)] == doc_ref[0, block]
            length = length + ((block >= back) & same).astype(jnp.int32)
        half = (length + 1) // 2
        start = 2 * blocks + slot + 1 - 2 * half
        info[which, 0] = slot
        info[which, 1] = half
        info[which, 2] = start * BALANCE_TOKENS
        info[which, 3] = (length % 2) * BALANCE_TOKENS
        lowest = jnp.minimum(lowest, start)
        highest = jnp.maximum(highest, 2 * blocks + slot)

    kv_lanes = pl.ds(low * HEAD_WIDTH, heads * HEAD_WIDTH)

    def window_copies(number):
        column, step = sp - 2 + number // blocks, number % blocks
        known = jnp.maximum(column, 0)
        place = number // blocks * blocks + landing_slot(source_ref, blocks, dp, known, dp ^ step)
        wanted = (column >= 0) & (place >= lowest) & (place <= highest)
        rows = block_rows(place)
        return wanted, [
            pltpu.make_async_copy(
                windows[number].at[which, :, kv_lanes],
                buf.at[rows],
                kv_sem.at[number, which],
            )
            for which, buf in enumerate((k_buf, v_buf))
        ]

    fetches = [window_copies(number) for number in range(3 * blocks)]
    for wanted, copies in fetches:

        @pl.when(wanted)
        def _():
            for copy in copies:
                copy.start()

    @pl.when(lowest + origin < 0)
    def _():
        rows = block_rows(lowest)
        k_buf[rows] = jnp.zeros((BALANCE_TOKENS, k_buf.shape[1]), k_buf.dtype)
        v_buf[rows] = jnp.zeros((BALANCE_TOKENS, v_buf.shape[1]), v_buf.dtype)

    for wanted, copies in fetches:

        @pl.when(wanted)
        def _():
            for copy in copies:
                copy.wait()

    pairs = GROUP_WIDTH // PAIR
    tiles = BALANCE_TOKENS // 8

    def one_task(chunks, side, head, start, skipped):
        lanes = pl.ds(pl.multiple_of(head * HEAD_WIDTH, HEAD_WIDTH), HEAD_WIDTH)
        span = pl.ds(pl.multiple_of(start, BALANCE_TOKENS), chunks * PAIR)
        lower, upper = slice(0, BALANCE_TOKENS), slice(BALANCE_TOKENS, PAIR)
        row = lax.broadcasted_iota(jnp.int32, (BALANCE_TOKENS, PAIR), 0)
        column = lax.broadcasted_iota(jnp.int32, (BALANCE_TOKENS, PAIR), 1)
        allowed = row <= (column & (BALANCE_TOKENS - 1))
        tops = [None] * pairs
        totals = [None] * pairs
        sums = [None] * pairs
        shifts = [None] * pairs

        def rows_of(chunk):
            return pl.ds(pl.multiple_of(start + chunk * PAIR, BALANCE_TOKENS), PAIR)

        def score(pair, chunk):
            parts = [
                q_buf[side, pair * PAIR + member : pair * PAIR + member + HEAD_WIDTH]
                for member in range(0, PAIR, HEAD_WIDTH)
            ]
            product = jnp.dot(
                k_buf[rows_of(chunk), lanes],
                jnp.concatenate(parts, axis=1),
                preferred_element_type=jnp.float32,
            )
            for part in (lower, upper):
                base = chunk * PAIR + part.start
                held = product[part]
                if chunk == 0 and part is lower:
                    held = jnp.where(skipped > 0, -1e30, held)
                if chunk == chunks - 1 and part is upper:
                    held = jnp.where(allowed, held, -1e30)
                s_buf[pair, base : base + BALANCE_TOKENS] = held
                high = jnp.max(held.reshape(tiles, 8, PAIR), axis=0)
                tops[pair] = high if base == 0 else jnp.maximum(tops[pair], high)

        def settle(pair):
            shifts[pair] = jnp.max(tops[pair], axis=0, keepdims=True) * EXP2_SCALE

        def mix(pair, chunk):
            keys = slice(chunk * PAIR, (chunk + 1) * PAIR)
            weight = jnp.exp2(s_buf[pair, keys] * EXP2_SCALE - shifts[pair])
            mixed = jnp.dot(
                vt_buf[:, keys],
                weight.astype(jnp.bfloat16),
                preferred_element_type=jnp.float32,
            )
            added = jnp.sum(weight.reshape(PAIR // 8, 8, PAIR), axis=0)
            totals[pair] = added if chunk == 0 else totals[pair] + added
            sums[pair] = mixed if chunk == 0 else sums[pair] + mixed

        def finish(pair):
            scaled = sums[pair] * (1.0 / jnp.sum(totals[pair], axis=0, keepdims=True))
            scaled = scaled.astype(o_buf.dtype)
            for member in range(0, PAIR, HEAD_WIDTH):
                piece = scaled[:, member : member + HEAD_WIDTH].T
                o_buf[side, :, pair * PAIR + member : pair * PAIR + member + HEAD_WIDTH] = piece

        for chunk in range(chunks):
            score(0, chunk)
            vt_buf[:, chunk * PAIR : (chunk + 1) * PAIR] = v_buf[rows_of(chunk), lanes].T
        for pair in range(pairs):
            settle(pair)
            for chunk in range(chunks):
                if pair + 1 < pairs:
                    score(pair + 1, chunk)
                mix(pair, chunk)
            if pair:
                finish(pair - 1)
        finish(pairs - 1)

    def o_copy(task):
        side = task % 2
        lanes = pl.ds(
            pl.multiple_of((low + head_of(task)) * GROUP_WIDTH, GROUP_WIDTH), GROUP_WIDTH
        )
        rows = block_rows(info[piece_of(task), 0])
        return pltpu.make_async_copy(o_buf.at[side], out_ref.at[rows, lanes], o_sem.at[side])

    @pl.loop(0, tasks)
    def _(task):
        @pl.when(task + 1 < tasks)
        def _():
            q_start(task + 1)

        q_copy(task, 0).wait()

        @pl.when(task >= 2)
        def _():
            o_copy(task - 2).wait()

        piece = piece_of(task)
        half, start, skipped = info[piece, 1], info[piece, 2], info[piece, 3]
        for chunks in range(1, MOST_BLK * BALANCE_TOKENS // PAIR + 1):

            @pl.when(half == chunks)
            def _():
                one_task(chunks, task % 2, head_of(task), start, skipped)

        o_copy(task).start()

    for task in range(max(tasks - 2, 0), tasks):
        o_copy(jnp.int32(task)).wait()


def attend(source, docs, pieces, windows, base, shape, blocks, steps, low, heads, rest=0):
    hbm = pl.BlockSpec(memory_space=pltpu.HBM)
    smem = pl.BlockSpec(memory_space=pltpu.SMEM)
    operands = [source, docs, *pieces, *windows] + ([] if base is None else [base])
    reach = MOST_BLK * BALANCE_TOKENS
    held = 3 * blocks * BALANCE_TOKENS
    dtype = pieces[0].dtype
    return pl.pallas_call(
        functools.partial(attend_kernel, blocks, steps, low, heads, rest),
        out_shape=jax.ShapeDtypeStruct(shape, dtype),
        in_specs=[smem, smem] + [hbm] * (len(operands) - 2),
        out_specs=hbm,
        scratch_shapes=[
            pltpu.VMEM((2, GROUP_WIDTH, BALANCE_TOKENS), dtype),
            pltpu.VMEM((held, heads * HEAD_WIDTH), dtype),
            pltpu.VMEM((held, heads * HEAD_WIDTH), dtype),
            pltpu.VMEM((2, BALANCE_TOKENS, GROUP_WIDTH), dtype),
            pltpu.VMEM((GROUP_WIDTH // PAIR, reach, PAIR), jnp.float32),
            pltpu.VMEM((HEAD_WIDTH, reach), dtype),
            pltpu.SMEM((len(steps), 4), jnp.int32),
            pltpu.SemaphoreType.DMA((2,)),
            pltpu.SemaphoreType.DMA((3 * blocks, 2)),
            pltpu.SemaphoreType.DMA((2,)),
        ],
        input_output_aliases={} if base is None else {len(operands) - 1: 0},
        compiler_params=pltpu.CompilerParams(vmem_limit_bytes=VMEM_LIMIT),
        cost_estimate=pl.CostEstimate(flops=0, bytes_accessed=2**10, transcendentals=0),
        name=f"attend_{steps[0]}_{low}",
    )(*operands)


def on_device(query_matrix, key_matrix, value_matrix, block_source, documents):
    dp_count = lax.axis_size("dp")
    sp_count = lax.axis_size("sp")
    sp = lax.axis_index("sp")
    tok_dev = query_matrix.shape[1]
    blocks = tok_dev // BALANCE_TOKENS
    assert blocks == dp_count == 4
    q = query_matrix.reshape(tok_dev, QUERY_HEADS * HEAD_WIDTH)
    k = key_matrix.reshape(tok_dev, KEY_VALUE_HEADS * HEAD_WIDTH)
    v = value_matrix.reshape(tok_dev, KEY_VALUE_HEADS * HEAD_WIDTH)

    def swap_dp(x, step):
        return lax.ppermute(x, "dp", [(i, i ^ step) for i in range(dp_count)])

    def ahead(x):
        return lax.ppermute(x, "sp", [(i, i + 2) for i in range(sp_count - 2)])

    def swap_core(mine, theirs):
        x = jnp.where(sp % 2 == 0, mine, theirs)
        return lax.ppermute(x, "sp", [(i, i ^ 1) for i in range(sp_count)])

    def pack(source, step, low, heads):
        return pack_q(source, q, blocks, step, low, heads)

    tie = lax.optimization_barrier
    all_heads = KEY_VALUE_HEADS
    cut = 5 * KEY_VALUE_HEADS // 8
    own = list(pack_kv(block_source, k, v, blocks))
    own[1:] = [swap_dp(own[step], step) for step in range(1, blocks)]
    two = [None] * blocks
    two[0] = ahead(own[0])
    near = [pack(block_source, step, 0, all_heads) for step in (1, 2)]
    near, source, own[1] = tie((near, block_source, own[1]))
    two[1] = ahead(own[1])
    kept = pack(source, 0, 0, all_heads)
    near, kept, source, own[2], own[3], two[0], two[1] = tie(
        (near, kept, source, own[2], own[3], two[0], two[1])
    )
    near = [swap_dp(x, step) for step, x in enumerate(near, 1)]
    two[2], two[3] = ahead(own[2]), ahead(own[3])
    source, two[3] = tie((source, two[3]))
    far = [pack(source, 3, 0, cut), pack(source, 3, cut, all_heads - cut)]
    far, two[2] = tie((far, two[2]))
    one = [swap_core(mine, theirs) for mine, theirs in zip(own, two)]
    windows = [*two, *one, *own]

    call = functools.partial(attend, block_source, documents, windows=windows, shape=q.shape)
    out = call([kept], base=None, blocks=blocks, steps=(0,), low=0, heads=cut)
    far, near, out = tie((far, near, out))
    far = [swap_dp(x, 3) for x in far]
    out = call(
        [*near, kept],
        base=out,
        blocks=blocks,
        steps=(1, 2, 0),
        low=0,
        heads=all_heads,
        rest=all_heads - cut,
    )
    out = call(far[:1], base=out, blocks=blocks, steps=(3,), low=0, heads=cut)
    out = call(far[1:], base=out, blocks=blocks, steps=(3,), low=cut, heads=all_heads - cut)
    return out.reshape(1, tok_dev, QUERY_HEADS * HEAD_WIDTH)


def solution(mesh):
    placed = (P("dp", "sp", None), P("dp", "sp", None), P("dp", "sp", None), P(), P("dp", None))
    return jax.shard_map(
        on_device, mesh=mesh, in_specs=placed, out_specs=P("dp", "sp", None), check_vma=False
    )
```

```python
import functools
import math

import jax
import jax.numpy as jnp
from jax import lax
from jax.experimental import pallas as pl
from jax.experimental.pallas import tpu as pltpu
from jax.sharding import PartitionSpec as P

QUERY_HEADS = 64
KEY_VALUE_HEADS = 8
HEAD_WIDTH = 128
BALANCE_TOKENS = 128
MOST_BLK = 8
GROUP_HEADS = QUERY_HEADS // KEY_VALUE_HEADS
GROUP_WIDTH = GROUP_HEADS * HEAD_WIDTH
PAIR = 256
EXP2_SCALE = math.log2(math.e) / math.sqrt(HEAD_WIDTH)
SUM_ROWS = 16
VMEM_LIMIT = 64 * 1024 * 1024


def position():
    return lax.axis_index("dp"), lax.axis_index("sp")


def leaving_slot(source_ref, blocks, dp, sp, other):
    slot = jnp.int32(0)
    for place in range(blocks):
        entry = source_ref[sp, other * blocks + place]
        slot = jnp.where(entry // blocks == dp, entry % blocks, slot)
    return slot


def landing_slot(source_ref, blocks, dp, sp, other):
    slot = jnp.int32(0)
    for place in range(blocks):
        entry = source_ref[sp, dp * blocks + place]
        slot = jnp.where(entry // blocks == other, place, slot)
    return slot


def block_rows(slot):
    return pl.ds(pl.multiple_of(slot * BALANCE_TOKENS, BALANCE_TOKENS), BALANCE_TOKENS)


def pack_kv_kernel(blocks, source_ref, k_ref, v_ref, *rest):
    outs, (buf, sem) = rest[:blocks], rest[blocks:]
    dp, sp = position()
    reads, writes = [], []
    for order, step in enumerate([*range(1, blocks), 0]):
        rows = block_rows(leaving_slot(source_ref, blocks, dp, sp, dp ^ step))
        for which, ref in enumerate((k_ref, v_ref)):
            place, number = buf.at[order, which], 2 * order + which
            reads.append(pltpu.make_async_copy(ref.at[rows], place, sem.at[number, 0]))
            writes.append(
                pltpu.make_async_copy(place, outs[step].at[which], sem.at[number, 1])
            )
    for copy in reads:
        copy.start()
    for read, write in zip(reads, writes):
        read.wait()
        write.start()
    for copy in writes:
        copy.wait()


def pack_kv(source, k, v, blocks):
    width = k.shape[1]
    hbm = pl.BlockSpec(memory_space=pltpu.HBM)
    return pl.pallas_call(
        functools.partial(pack_kv_kernel, blocks),
        out_shape=[jax.ShapeDtypeStruct((2, BALANCE_TOKENS, width), k.dtype)] * blocks,
        in_specs=[pl.BlockSpec(memory_space=pltpu.SMEM), hbm, hbm],
        out_specs=[hbm] * blocks,
        scratch_shapes=[
            pltpu.VMEM((blocks, 2, BALANCE_TOKENS, width), k.dtype),
            pltpu.SemaphoreType.DMA((2 * blocks, 2)),
        ],
        compiler_params=pltpu.CompilerParams(vmem_limit_bytes=VMEM_LIMIT),
        cost_estimate=pl.CostEstimate(flops=0, bytes_accessed=4 * 2**20, transcendentals=0),
        name="pack_kv",
    )(source, k, v)


def pack_q_kernel(blocks, step, first, source_ref, q_ref, out_ref, buf, turned, sem):
    dp, sp = position()
    rows = block_rows(leaving_slot(source_ref, blocks, dp, sp, dp ^ step))
    groups = buf.shape[0]

    def read(group):
        lanes = pl.ds(pl.multiple_of(first + group * GROUP_WIDTH, GROUP_WIDTH), GROUP_WIDTH)
        return pltpu.make_async_copy(q_ref.at[rows, lanes], buf.at[group], sem.at[group, 0])

    def write(group):
        span = pl.ds(pl.multiple_of(group * GROUP_WIDTH, GROUP_WIDTH), GROUP_WIDTH)
        return pltpu.make_async_copy(turned.at[group], out_ref.at[span], sem.at[group, 1])

    @pl.loop(0, groups)
    def _(group):
        read(group).start()

    @pl.loop(0, groups)
    def _(group):
        read(group).wait()
        for head in range(GROUP_HEADS):
            span = slice(head * HEAD_WIDTH, (head + 1) * HEAD_WIDTH)
            turned[group, span] = buf[group, :, span].T
        write(group).start()

    @pl.loop(0, groups)
    def _(group):
        write(group).wait()


def pack_q(source, q, blocks, step, first_head, heads):
    width = heads * GROUP_WIDTH
    hbm = pl.BlockSpec(memory_space=pltpu.HBM)
    return pl.pallas_call(
        functools.partial(pack_q_kernel, blocks, step, first_head * GROUP_WIDTH),
        out_shape=jax.ShapeDtypeStruct((width, BALANCE_TOKENS), q.dtype),
        in_specs=[pl.BlockSpec(memory_space=pltpu.SMEM), hbm],
        out_specs=hbm,
        scratch_shapes=[
            pltpu.VMEM((heads, BALANCE_TOKENS, GROUP_WIDTH), q.dtype),
            pltpu.VMEM((heads, GROUP_WIDTH, BALANCE_TOKENS), q.dtype),
            pltpu.SemaphoreType.DMA((heads, 2)),
        ],
        compiler_params=pltpu.CompilerParams(vmem_limit_bytes=VMEM_LIMIT),
        cost_estimate=pl.CostEstimate(
            flops=0, bytes_accessed=4 * width * BALANCE_TOKENS, transcendentals=0
        ),
        name=f"pack_q_{step}_{first_head}",
    )(source, q)


def attend_kernel(blocks, steps, low, heads, rest, *refs):
    count = len(steps)
    whole = (count - (rest > 0)) * heads
    tasks = whole + rest
    source_ref, doc_ref, *q_refs = refs[: 2 + count]
    windows = refs[2 + count : 2 + count + 3 * blocks]
    out_ref, q_buf, k_buf, v_buf, o_buf, s_buf, vt_buf, info, q_sem, kv_sem, o_sem = refs[-11:]
    dp, sp = position()

    def piece_of(task):
        return jnp.where(task < whole, task // heads, count - 1)

    def head_of(task):
        return jnp.where(task < whole, task % heads, task - whole + heads - rest)

    def q_copy(task, which):
        rows = pl.ds(pl.multiple_of(head_of(task) * GROUP_WIDTH, GROUP_WIDTH), GROUP_WIDTH)
        side = task % 2
        return pltpu.make_async_copy(q_refs[which].at[rows], q_buf.at[side], q_sem.at[side])

    def q_start(task):
        for which in range(count):

            @pl.when(piece_of(task) == which)
            def _():
                q_copy(task, which).start()

    q_start(jnp.int32(0))

    origin = (sp - 2) * blocks
    lowest = jnp.int32(3 * blocks)
    highest = jnp.int32(0)
    for which, step in enumerate(steps):
        slot = landing_slot(source_ref, blocks, dp, sp, dp ^ step)
        block = sp * blocks + slot
        length = jnp.int32(1)
        for back in range(1, MOST_BLK):
            same = doc_ref[0, jnp.maximum(block - back, 0)] == doc_ref[0, block]
            length = length + ((block >= back) & same).astype(jnp.int32)
        half = (length + 1) // 2
        start = 2 * blocks + slot + 1 - 2 * half
        info[which, 0] = slot
        info[which, 1] = half
        info[which, 2] = start * BALANCE_TOKENS
        info[which, 3] = (length % 2) * BALANCE_TOKENS
        lowest = jnp.minimum(lowest, start)
        highest = jnp.maximum(highest, 2 * blocks + slot)

    kv_lanes = pl.ds(low * HEAD_WIDTH, heads * HEAD_WIDTH)

    def window_copies(number):
        column, step = sp - 2 + number // blocks, number % blocks
        known = jnp.maximum(column, 0)
        place = number // blocks * blocks + landing_slot(source_ref, blocks, dp, known, dp ^ step)
        wanted = (column >= 0) & (place >= lowest) & (place <= highest)
        rows = block_rows(place)
        return wanted, [
            pltpu.make_async_copy(
                windows[number].at[which, :, kv_lanes],
                buf.at[rows],
                kv_sem.at[number, which],
            )
            for which, buf in enumerate((k_buf, v_buf))
        ]

    fetches = [window_copies(number) for number in range(3 * blocks)]
    for wanted, copies in fetches:

        @pl.when(wanted)
        def _():
            for copy in copies:
                copy.start()

    @pl.when(lowest + origin < 0)
    def _():
        rows = block_rows(lowest)
        k_buf[rows] = jnp.zeros((BALANCE_TOKENS, k_buf.shape[1]), k_buf.dtype)
        v_buf[rows] = jnp.zeros((BALANCE_TOKENS, v_buf.shape[1]), v_buf.dtype)

    vt_buf[HEAD_WIDTH:] = jnp.ones((SUM_ROWS, vt_buf.shape[1]), vt_buf.dtype)

    for wanted, copies in fetches:

        @pl.when(wanted)
        def _():
            for copy in copies:
                copy.wait()

    pairs = GROUP_WIDTH // PAIR
    tiles = BALANCE_TOKENS // 8

    def one_task(chunks, side, head, start, skipped):
        lanes = pl.ds(pl.multiple_of(head * HEAD_WIDTH, HEAD_WIDTH), HEAD_WIDTH)
        span = pl.ds(pl.multiple_of(start, BALANCE_TOKENS), chunks * PAIR)
        lower, upper = slice(0, BALANCE_TOKENS), slice(BALANCE_TOKENS, PAIR)
        row = lax.broadcasted_iota(jnp.int32, (BALANCE_TOKENS, PAIR), 0)
        column = lax.broadcasted_iota(jnp.int32, (BALANCE_TOKENS, PAIR), 1)
        allowed = row <= (column & (BALANCE_TOKENS - 1))
        tops = [None] * pairs
        sums = [None] * pairs
        shifts = [None] * pairs

        def rows_of(chunk):
            return pl.ds(pl.multiple_of(start + chunk * PAIR, BALANCE_TOKENS), PAIR)

        def score(pair, chunk):
            parts = [
                q_buf[side, pair * PAIR + member : pair * PAIR + member + HEAD_WIDTH]
                for member in range(0, PAIR, HEAD_WIDTH)
            ]
            product = jnp.dot(
                k_buf[rows_of(chunk), lanes],
                jnp.concatenate(parts, axis=1),
                preferred_element_type=jnp.float32,
            )
            for part in (lower, upper):
                base = chunk * PAIR + part.start
                held = product[part]
                if chunk == 0 and part is lower:
                    held = jnp.where(skipped > 0, -1e30, held)
                if chunk == chunks - 1 and part is upper:
                    held = jnp.where(allowed, held, -1e30)
                s_buf[pair, base : base + BALANCE_TOKENS] = held
                high = jnp.max(held.reshape(tiles, 8, PAIR), axis=0)
                tops[pair] = high if base == 0 else jnp.maximum(tops[pair], high)

        def settle(pair):
            shifts[pair] = jnp.max(tops[pair], axis=0, keepdims=True) * EXP2_SCALE

        def mix(pair, chunk):
            keys = slice(chunk * PAIR, (chunk + 1) * PAIR)
            weight = jnp.exp2(s_buf[pair, keys] * EXP2_SCALE - shifts[pair])
            mixed = jnp.dot(
                vt_buf[:, keys],
                weight.astype(jnp.bfloat16),
                preferred_element_type=jnp.float32,
            )
            sums[pair] = mixed if chunk == 0 else sums[pair] + mixed

        def finish(pair):
            total = sums[pair][HEAD_WIDTH : HEAD_WIDTH + 1]
            scaled = (sums[pair][:HEAD_WIDTH] * (1.0 / total)).astype(o_buf.dtype)
            for member in range(0, PAIR, HEAD_WIDTH):
                piece = scaled[:, member : member + HEAD_WIDTH].T
                o_buf[side, :, pair * PAIR + member : pair * PAIR + member + HEAD_WIDTH] = piece

        for chunk in range(chunks):
            score(0, chunk)
            vt_buf[:HEAD_WIDTH, chunk * PAIR : (chunk + 1) * PAIR] = v_buf[rows_of(chunk), lanes].T
        for pair in range(pairs):
            settle(pair)
            for chunk in range(chunks):
                if pair + 1 < pairs:
                    score(pair + 1, chunk)
                mix(pair, chunk)
            if pair:
                finish(pair - 1)
        finish(pairs - 1)

    def o_copy(task):
        side = task % 2
        lanes = pl.ds(
            pl.multiple_of((low + head_of(task)) * GROUP_WIDTH, GROUP_WIDTH), GROUP_WIDTH
        )
        rows = block_rows(info[piece_of(task), 0])
        return pltpu.make_async_copy(o_buf.at[side], out_ref.at[rows, lanes], o_sem.at[side])

    @pl.loop(0, tasks)
    def _(task):
        @pl.when(task + 1 < tasks)
        def _():
            q_start(task + 1)

        q_copy(task, 0).wait()

        @pl.when(task >= 2)
        def _():
            o_copy(task - 2).wait()

        piece = piece_of(task)
        half, start, skipped = info[piece, 1], info[piece, 2], info[piece, 3]
        for chunks in range(1, MOST_BLK * BALANCE_TOKENS // PAIR + 1):

            @pl.when(half == chunks)
            def _():
                one_task(chunks, task % 2, head_of(task), start, skipped)

        o_copy(task).start()

    for task in range(max(tasks - 2, 0), tasks):
        o_copy(jnp.int32(task)).wait()


def attend(source, docs, pieces, windows, base, shape, blocks, steps, low, heads, rest=0):
    hbm = pl.BlockSpec(memory_space=pltpu.HBM)
    smem = pl.BlockSpec(memory_space=pltpu.SMEM)
    operands = [source, docs, *pieces, *windows] + ([] if base is None else [base])
    reach = MOST_BLK * BALANCE_TOKENS
    held = 3 * blocks * BALANCE_TOKENS
    dtype = pieces[0].dtype
    return pl.pallas_call(
        functools.partial(attend_kernel, blocks, steps, low, heads, rest),
        out_shape=jax.ShapeDtypeStruct(shape, dtype),
        in_specs=[smem, smem] + [hbm] * (len(operands) - 2),
        out_specs=hbm,
        scratch_shapes=[
            pltpu.VMEM((2, GROUP_WIDTH, BALANCE_TOKENS), dtype),
            pltpu.VMEM((held, heads * HEAD_WIDTH), dtype),
            pltpu.VMEM((held, heads * HEAD_WIDTH), dtype),
            pltpu.VMEM((2, BALANCE_TOKENS, GROUP_WIDTH), dtype),
            pltpu.VMEM((GROUP_WIDTH // PAIR, reach, PAIR), jnp.float32),
            pltpu.VMEM((HEAD_WIDTH + SUM_ROWS, reach), dtype),
            pltpu.SMEM((len(steps), 4), jnp.int32),
            pltpu.SemaphoreType.DMA((2,)),
            pltpu.SemaphoreType.DMA((3 * blocks, 2)),
            pltpu.SemaphoreType.DMA((2,)),
        ],
        input_output_aliases={} if base is None else {len(operands) - 1: 0},
        compiler_params=pltpu.CompilerParams(vmem_limit_bytes=VMEM_LIMIT),
        cost_estimate=pl.CostEstimate(flops=0, bytes_accessed=2**10, transcendentals=0),
        name=f"attend_{steps[0]}_{low}",
    )(*operands)


def on_device(query_matrix, key_matrix, value_matrix, block_source, documents):
    dp_count = lax.axis_size("dp")
    sp_count = lax.axis_size("sp")
    sp = lax.axis_index("sp")
    tok_dev = query_matrix.shape[1]
    blocks = tok_dev // BALANCE_TOKENS
    assert blocks == dp_count == 4
    q = query_matrix.reshape(tok_dev, QUERY_HEADS * HEAD_WIDTH)
    k = key_matrix.reshape(tok_dev, KEY_VALUE_HEADS * HEAD_WIDTH)
    v = value_matrix.reshape(tok_dev, KEY_VALUE_HEADS * HEAD_WIDTH)

    def swap_dp(x, step):
        return lax.ppermute(x, "dp", [(i, i ^ step) for i in range(dp_count)])

    def ahead(x):
        return lax.ppermute(x, "sp", [(i, i + 2) for i in range(sp_count - 2)])

    def swap_core(mine, theirs):
        x = jnp.where(sp % 2 == 0, mine, theirs)
        return lax.ppermute(x, "sp", [(i, i ^ 1) for i in range(sp_count)])

    def pack(source, step, low, heads):
        return pack_q(source, q, blocks, step, low, heads)

    tie = lax.optimization_barrier
    all_heads = KEY_VALUE_HEADS
    cut = 5 * KEY_VALUE_HEADS // 8
    own = list(pack_kv(block_source, k, v, blocks))
    own[1:] = [swap_dp(own[step], step) for step in range(1, blocks)]
    two = [None] * blocks
    two[0] = ahead(own[0])
    near = [pack(block_source, step, 0, all_heads) for step in (1, 2)]
    near, source, own[1] = tie((near, block_source, own[1]))
    two[1] = ahead(own[1])
    kept = pack(source, 0, 0, all_heads)
    near, kept, source, own[2], own[3], two[0], two[1] = tie(
        (near, kept, source, own[2], own[3], two[0], two[1])
    )
    near = [swap_dp(x, step) for step, x in enumerate(near, 1)]
    two[2], two[3] = ahead(own[2]), ahead(own[3])
    source, two[3] = tie((source, two[3]))
    far = [pack(source, 3, 0, cut), pack(source, 3, cut, all_heads - cut)]
    far, two[2] = tie((far, two[2]))
    one = [swap_core(mine, theirs) for mine, theirs in zip(own, two)]
    windows = [*two, *one, *own]

    call = functools.partial(attend, block_source, documents, windows=windows, shape=q.shape)
    out = call([kept], base=None, blocks=blocks, steps=(0,), low=0, heads=cut)
    far, near, out = tie((far, near, out))
    far = [swap_dp(x, 3) for x in far]
    out = call(
        [*near, kept],
        base=out,
        blocks=blocks,
        steps=(1, 2, 0),
        low=0,
        heads=all_heads,
        rest=all_heads - cut,
    )
    out = call(far[:1], base=out, blocks=blocks, steps=(3,), low=0, heads=cut)
    out = call(far[1:], base=out, blocks=blocks, steps=(3,), low=cut, heads=all_heads - cut)
    return out.reshape(1, tok_dev, QUERY_HEADS * HEAD_WIDTH)


def solution(mesh):
    placed = (P("dp", "sp", None), P("dp", "sp", None), P("dp", "sp", None), P(), P("dp", None))
    return jax.shard_map(
        on_device, mesh=mesh, in_specs=placed, out_specs=P("dp", "sp", None), check_vma=False
    )
```
